256 devices in a mesh: tile: 64 (over x, z, y_hi), kern: 4 (over y_lo, core).
Axes of the slice: x: 4, y: 4 (y_hi: 2, y_lo: 2; y = y_hi * 2 + y_lo), z: 8, core: 2. Of those that a mesh axis runs over, the one named last changes fastest.
Arguments:
- mask: float32 [4096, 2048], P('tile'), may hold values from -1 to 1
- target: float32 [4096, 2048], P('tile'), may hold values from 0 to 1
- spectra: float32 [24, 16, 128], P('kern'), may hold values from -64 to 64
- weights: float32 [24], P('kern'), may hold values from 0.1 to 1
- counts: int32 [64], P('tile'), may hold values from 32 to 256, as said below
- frag_rows: int32 [16384], P('tile'), may hold values from 0 to 63
- frag_cols: int32 [16384], P('tile'), may hold values from 0 to 2016
- step: float32 [16384], P('tile'), may hold values from -6 to 6
Outputs:
- gradient: float32 [16384], P('tile')
- curvature: float32 [16384], P('tile')
The draws below stay inside these ranges and needn't reach their ends.
Inputs may be any that keep to these rules, and one draw needn't show every extreme that they name: `counts`: the used slots of a slab are its first ones; in every draw some slab uses all 256.
All inputs are finite; a program needn't handle non-finite values.
Results may differ from the reference program's by a relative error of at most 0.0003.
Values sent between devices are 32-bit elements; how exact they have to be, the bound alone decides.
A program may use at most 128 MiB of HBM per device.

```python
import math
import jax
import jax.numpy as jnp
from jax import lax

WIDTH = 2048
COL_FREQS = 64
ROW_FREQS = 16
KERNELS = 24
REACH = 64
FRAG_LEN = 32
SLAB = 64
SLOTS_DEV = 256
GROUPS = 64
ROWS = 4096
SLOTS = 16384


def draw_counts(key, part):
    key = jax.random.fold_in(key, 11)
    first_key, second_key = jax.random.split(key)
    draw_values = jax.random.randint(first_key, (GROUPS,), SLOTS_DEV // 8, SLOTS_DEV + 1)
    full_slab = jax.random.randint(second_key, (), 0, GROUPS)
    return jnp.where(jnp.arange(GROUPS, dtype=jnp.int32) == full_slab, SLOTS_DEV, draw_values).astype(jnp.int32)


def touch_ends(result, own_key, low, largest):
    longest = result.shape.index(max(result.shape))
    spots = []
    for shift in (0, 1):
        where = [jax.random.randint(jax.random.fold_in(own_key, axis), (), 0, length) for axis, length in enumerate(result.shape)]
        where[longest] = (where[longest] + shift) % result.shape[longest]
        spots.append(tuple(where))
    return result.at[spots[0]].set(low).at[spots[1]].set(largest)


def shard_levels(stream_key, dims, cuts, smallest, high):
    def one(axis_at, blocks):
        draws = jax.random.uniform(jax.random.fold_in(jax.random.fold_in(stream_key, 6), axis_at), (blocks,), jnp.float32, smallest / len(cuts), high / len(cuts))
        return jnp.repeat(jnp.exp(draws), dims[axis_at] // blocks).reshape((-1,) + (1,) * (len(dims) - axis_at - 1))

    factor_of = one(*cuts[0])
    for cut in cuts[1:]:
        factor_of = factor_of * one(*cut)
    return factor_of


def noise(key, shape, deviation, reach, shards=(), kind=jnp.bfloat16):
    loudness = shard_levels(key, shape, shards, -0.22, 0.18) if shards else 1.0
    array = jax.random.normal(key, shape, jnp.float32) * deviation * loudness
    return jnp.minimum(jnp.maximum(array, -reach), reach).astype(kind)


def setup_inputs(seed: int = 0) -> dict:
    key_of = jax.random.split(jax.random.key(seed), 9)
    mask = jnp.clip(jax.random.uniform(key_of[0], (ROWS, WIDTH), jnp.float32, -1.0, 1.0) * shard_levels(key_of[0], (ROWS, WIDTH), ((0, 64),), -0.4, 0.0), -1.0, 1.0)
    target = jnp.clip(1.0 * jax.random.uniform(key_of[1], (ROWS, WIDTH), jnp.float32) ** shard_levels(key_of[1], (ROWS, WIDTH), ((0, 64),), -0.2, 0.2), 0.0, 1.0)
    spectra = noise(key_of[2], (KERNELS, ROW_FREQS, 2 * COL_FREQS), ((0.375 * (SLAB + 2 * REACH) * WIDTH / (ROW_FREQS * COL_FREQS)) ** 0.5), 64.0, ((0, 4),), jnp.float32)
    weights = jnp.clip(jnp.exp(math.log(1.0) - 2.3025851 * jax.random.uniform(key_of[3], (KERNELS,), jnp.float32) ** shard_levels(key_of[3], (KERNELS,), ((0, 4),), -0.2, 0.2)), 0.1, 1.0)
    counts = draw_counts(jax.random.fold_in(key_of[8], 71), 0)
    frag_rows = touch_ends(jax.random.randint(key_of[5], (SLOTS,), 0, SLAB), jax.random.fold_in(key_of[5], 1), 0, SLAB - 1).astype(jnp.int32)
    frag_cols = touch_ends(jax.random.randint(key_of[6], (SLOTS,), 0, WIDTH - FRAG_LEN + 1), jax.random.fold_in(key_of[6], 1), 0, WIDTH - FRAG_LEN).astype(jnp.int32)
    step = noise(key_of[7], (SLOTS,), 1.0, 6.0, ((0, 64),), jnp.float32)
    return dict(mask=mask, target=target, spectra=spectra, weights=weights, counts=counts, frag_rows=frag_rows, frag_cols=frag_cols, step=step)


STEEP = 10.0
THRESH = 0.1
HIGH = lax.Precision.HIGHEST

def make_tables(columns, col_freqs, ext_rows, row_freqs):
    col_pos = jnp.arange(columns, dtype=jnp.int32)
    col_wave = jnp.arange(col_freqs, dtype=jnp.int32) - col_freqs // 2
    col_phase = (col_pos[:, None] * col_wave[None, :] % columns).astype(jnp.float32) * (2.0 * math.pi / columns)
    cosine = jnp.cos(col_phase) / math.sqrt(columns)
    sine_part = jnp.sin(col_phase) / math.sqrt(columns)
    forward = jnp.concatenate([cosine, -sine_part], axis=1)
    inverse = jnp.concatenate([jnp.concatenate([cosine.T, sine_part.T], axis=1), jnp.concatenate([-sine_part.T, cosine.T], axis=1)], axis=0)
    row_pos = jnp.arange(ext_rows, dtype=jnp.int32)
    row_wave = jnp.arange(row_freqs, dtype=jnp.int32) - row_freqs // 2
    row_phase = (row_pos[:, None] * row_wave[None, :] % ext_rows).astype(jnp.float32) * (2.0 * math.pi / ext_rows)
    return (forward, inverse, jnp.cos(row_phase) / math.sqrt(ext_rows), jnp.sin(row_phase) / math.sqrt(ext_rows))

def forward_fields(fields, spectra, weights, forward, inverse, table_re, table_im, slab_rows, kernel_total):
    half_spec = spectra.shape[2] // 2
    columns = fields.shape[2]
    spec_re = spectra[:, :, :half_spec]
    spec_im = spectra[:, :, half_spec:]
    packed = jnp.einsum('jyx,xc->jyc', fields, forward, precision=HIGH)
    part_re = packed[..., :half_spec]
    part_im = packed[..., half_spec:]
    mode_re = jnp.einsum('yr,jyc->jrc', table_re, part_re, precision=HIGH) + jnp.einsum('yr,jyc->jrc', table_im, part_im, precision=HIGH)
    mode_im = jnp.einsum('yr,jyc->jrc', table_re, part_im, precision=HIGH) - jnp.einsum('yr,jyc->jrc', table_im, part_re, precision=HIGH)
    prod_re = spec_re[None] * mode_re[:, None] - spec_im[None] * mode_im[:, None]
    prod_im = spec_re[None] * mode_im[:, None] + spec_im[None] * mode_re[:, None]
    out_re = table_re[REACH:REACH + slab_rows]
    out_im = table_im[REACH:REACH + slab_rows]
    slab_re = jnp.einsum('yr,jkrc->jkyc', out_re, prod_re, precision=HIGH) - jnp.einsum('yr,jkrc->jkyc', out_im, prod_im, precision=HIGH)
    slab_im = jnp.einsum('yr,jkrc->jkyc', out_re, prod_im, precision=HIGH) + jnp.einsum('yr,jkrc->jkyc', out_im, prod_re, precision=HIGH)
    images = jnp.einsum('jkyc,cx->jkyx', jnp.concatenate([slab_re, slab_im], axis=-1), inverse, precision=HIGH)
    amp_re = images[..., :columns]
    amp_im = images[..., columns:]
    kernel_scale = weights / kernel_total
    intensity = jnp.einsum('k,kyx->yx', kernel_scale, amp_re[0] * amp_re[0] + amp_im[0] * amp_im[0], precision=HIGH)
    intensity_change = 2.0 * jnp.einsum('k,kyx->yx', kernel_scale, amp_re[0] * amp_re[1] + amp_im[0] * amp_im[1], precision=HIGH)
    return (amp_re[0], amp_im[0], intensity, intensity_change)

def weighting(intensity, intensity_change, target_slab):
    developed = jax.nn.sigmoid(STEEP * (intensity - THRESH))
    steepness = STEEP * developed * (1.0 - developed)
    return jnp.stack([steepness * (developed - target_slab), steepness * steepness * intensity_change])

def adjoint_spectra(weighted, amp_re, amp_im, spectra, weights, inverse, table_re, table_im, slab_rows, kernel_total):
    half_spec = spectra.shape[2] // 2
    spec_re = spectra[:, :, :half_spec]
    spec_im = spectra[:, :, half_spec:]
    load_scale = 2.0 * weights / kernel_total
    load_re = load_scale[None, :, None, None] * weighted[:, None] * amp_re[None]
    load_im = load_scale[None, :, None, None] * weighted[:, None] * amp_im[None]
    returned = jnp.einsum('jkyx,cx->jkyc', jnp.concatenate([load_re, load_im], axis=-1), inverse, precision=HIGH)
    back_re = returned[..., :half_spec]
    back_im = returned[..., half_spec:]
    out_re = table_re[REACH:REACH + slab_rows]
    out_im = table_im[REACH:REACH + slab_rows]
    coef_re = jnp.einsum('yr,jkyc->jkrc', out_re, back_re, precision=HIGH) + jnp.einsum('yr,jkyc->jkrc', out_im, back_im, precision=HIGH)
    coef_im = jnp.einsum('yr,jkyc->jkrc', out_re, back_im, precision=HIGH) - jnp.einsum('yr,jkyc->jkrc', out_im, back_re, precision=HIGH)
    sum_re = lax.optimization_barrier(jnp.sum(spec_re[None] * coef_re + spec_im[None] * coef_im, axis=1))
    sum_im = lax.optimization_barrier(jnp.sum(spec_re[None] * coef_im - spec_im[None] * coef_re, axis=1))
    return jnp.concatenate([sum_re, sum_im], axis=-1)

def rows_from(table_re, table_im, spectrum):
    half_spec = spectrum.shape[2] // 2
    spec_re = spectrum[..., :half_spec]
    spec_im = spectrum[..., half_spec:]
    fold_re = jnp.einsum('yr,jrc->jyc', table_re, spec_re, precision=HIGH) - jnp.einsum('yr,jrc->jyc', table_im, spec_im, precision=HIGH)
    fold_im = jnp.einsum('yr,jrc->jyc', table_re, spec_im, precision=HIGH) + jnp.einsum('yr,jrc->jyc', table_im, spec_re, precision=HIGH)
    return jnp.concatenate([fold_re, fold_im], axis=-1)

def stripe_tables(row_ids, col_ids, slab_rows, columns):
    onehot = (row_ids[:, None] == jnp.arange(slab_rows, dtype=jnp.int32)[None, :]).astype(jnp.float32)
    col_pos = jnp.arange(columns, dtype=jnp.int32)
    covered = ((col_pos[None, :] >= col_ids[:, None]) & (col_pos[None, :] < col_ids[:, None] + FRAG_LEN)).astype(jnp.float32)
    return (onehot, covered)

def reference(mask, target, spectra, weights, counts, frag_rows, frag_cols, step):
    ext_rows = SLAB + 2 * REACH
    forward, inverse, table_re, table_im = make_tables(WIDTH, COL_FREQS, ext_rows, ROW_FREQS)
    slot_pos = jnp.arange(SLOTS_DEV, dtype=jnp.int32)
    active = slot_pos[None, :] < counts[:, None]
    amplitude = jnp.where(active, step.reshape(GROUPS, SLOTS_DEV), 0.0) / math.sqrt(FRAG_LEN)
    row_grid = frag_rows.reshape(GROUPS, SLOTS_DEV)
    col_grid = frag_cols.reshape(GROUPS, SLOTS_DEV)

    def build_slab(operands):
        row_ids, col_ids, amp_slab = operands
        onehot, covered = stripe_tables(row_ids, col_ids, SLAB, WIDTH)
        return jnp.einsum('fy,fx->yx', onehot, amp_slab[:, None] * covered, precision=HIGH)
    shift_field = lax.map(build_slab, (row_grid, col_grid, amplitude)).reshape(ROWS, WIDTH)
    padded = jnp.pad(jnp.stack([mask, shift_field]), ((0, 0), (REACH, REACH), (0, 0)))

    def sweep_slab(running, slab_index):
        row_start = (slab_index * SLAB).astype(jnp.int32)
        zero_start = jnp.int32(0)
        fields = lax.dynamic_slice(padded, (zero_start, row_start, zero_start), (2, ext_rows, WIDTH))
        target_slab = lax.dynamic_slice(target, (row_start, zero_start), (SLAB, WIDTH))
        amp_re, amp_im, intensity, intensity_change = forward_fields(fields, spectra, weights, forward, inverse, table_re, table_im, SLAB, KERNELS)
        weighted = weighting(intensity, intensity_change, target_slab)
        spectrum = adjoint_spectra(weighted, amp_re, amp_im, spectra, weights, inverse, table_re, table_im, SLAB, KERNELS)
        ext_gradient = jnp.einsum('jyc,xc->jyx', rows_from(table_re, table_im, spectrum), forward, precision=HIGH)
        previous = lax.dynamic_slice(running, (zero_start, row_start, zero_start), (2, ext_rows, WIDTH))
        running = lax.dynamic_update_slice(running, previous + ext_gradient, (zero_start, row_start, zero_start))
        return (running, None)
    running = lax.scan(sweep_slab, jnp.zeros((2, ROWS + 2 * REACH, WIDTH), jnp.float32), jnp.arange(GROUPS, dtype=jnp.int32))[0]
    mask_gradient = running[:, REACH:REACH + ROWS].reshape(2, GROUPS, SLAB, WIDTH)

    def project(operands):
        row_ids, col_ids, block = operands
        onehot, covered = stripe_tables(row_ids, col_ids, SLAB, WIDTH)
        picked = jnp.einsum('fy,jyx->jfx', onehot, block, precision=HIGH)
        return lax.optimization_barrier(jnp.sum(picked * covered[None], axis=2)) / math.sqrt(FRAG_LEN)
    projected = lax.map(project, (row_grid, col_grid, jnp.moveaxis(mask_gradient, 1, 0)))
    projected = jnp.where(active[:, None, :], projected, 0.0)
    return (projected[:, 0].reshape(SLOTS), projected[:, 1].reshape(SLOTS))
```

```python
import functools
import math

import jax
import jax.numpy as jnp
import ml_dtypes
import numpy as np
from jax import lax
from jax.experimental import pallas as pl
from jax.experimental.pallas import tpu as pltpu
from jax.sharding import PartitionSpec as P

WIDTH = 2048
COL_FREQS = 64
ROW_FREQS = 16
KERNELS = 24
FRAG_LEN = 32
SLAB = 64
SLOTS = 256
EXT = 192
TILES = 64
KERN = 4
LOCAL = KERNELS // KERN
GRID_ROWS = 32
GRID_COLS = 128
STEEP = 10.0
THRESH = 0.1
F32 = jnp.float32
BF16 = jnp.bfloat16
CHUNKS = 4
MESH = pl.DeviceIdType.MESH


def np_split(x):
    hi = x.astype(np.float32).astype(ml_dtypes.bfloat16)
    lo = (x - hi.astype(np.float64)).astype(np.float32).astype(ml_dtypes.bfloat16)
    return hi, lo


def pad_lanes(x, lanes=256):
    return np.pad(x, ((0, 0), (0, lanes - x.shape[1])))


@functools.lru_cache(maxsize=None)
def make_tables():
    kc = np.arange(COL_FREQS) - COL_FREQS // 2
    kr = np.arange(ROW_FREQS) - ROW_FREQS // 2
    x = np.arange(WIDTH)
    ang = 2 * np.pi * (np.outer(x, kc) % WIDTH) / WIDTH
    f_hi, f_lo = np_split(np.concatenate([np.cos(ang), -np.sin(ang)], 1) / math.sqrt(WIDTH))
    fwd = np.concatenate([f_hi, f_lo], 1)

    n = np.arange(GRID_COLS)
    step = WIDTH // GRID_COLS
    dist = (x[None, :] - step * n[:, None]) % WIDTH
    base = np.ones(WIDTH)
    for kap in range(1, COL_FREQS):
        base += 2 * np.cos(2 * np.pi * ((np.arange(WIDTH) * kap) % WIDTH) / WIDTH)
    g = (base / GRID_COLS)[dist]
    g_hi, g_lo = np_split(g)
    up = np.concatenate([g_hi, g_hi, g_lo], 0)
    gt_hi, gt_lo = np_split(g.T)
    down = np.concatenate([gt_hi, gt_lo], 1)

    ang = 2 * np.pi * (np.outer(kc, n) % GRID_COLS) / GRID_COLS
    c, s = np.cos(ang) / math.sqrt(WIDTH), np.sin(ang) / math.sqrt(WIDTH)
    inv = np.block([[c, s], [-s, c]])
    i_hi, i_lo = np_split(inv)
    inv3 = np.concatenate([i_hi, i_hi, i_lo], 0)
    t_hi, t_lo = np_split(inv.T)
    adj = np.concatenate([t_hi, t_lo], 1)

    e = np.arange(SLAB)
    ang = 2 * np.pi * (np.outer(kr, e) % EXT) / EXT
    a_hi, a_lo = np_split(np.concatenate([np.cos(ang), np.sin(ang)], 0) / math.sqrt(EXT))
    lt3 = np.concatenate([a_hi, a_hi, a_lo], 1)

    m = np.arange(GRID_ROWS)
    ang = 2 * np.pi * (np.outer(m, kr) % GRID_ROWS) / GRID_ROWS
    ag = np.concatenate([np.cos(ang), np.sin(ang)], 1) / math.sqrt(EXT)
    hi, lo = np_split(ag)
    ag3 = np.concatenate([hi, hi, lo], 1)
    hi, lo = np_split(ag.T)
    agt3 = np.concatenate([hi, hi, lo], 1)

    rstep = EXT // GRID_ROWS
    dist = (e[:, None] - rstep * m[None, :]) % EXT
    base = np.ones(EXT)
    for rho in range(1, ROW_FREQS):
        base += 2 * np.cos(2 * np.pi * ((np.arange(EXT) * rho) % EXT) / EXT)
    r = (base / GRID_ROWS)[dist]
    hi, lo = np_split(r)
    r3 = np.concatenate([hi, hi, lo], 1)
    hi, lo = np_split(r.T)
    rt3 = np.concatenate([hi, hi, lo], 1)

    tabs = np.concatenate(
        [inv3, adj, pad_lanes(lt3), pad_lanes(ag3), pad_lanes(agt3), pad_lanes(r3), pad_lanes(rt3)], 0
    )

    ang = 2 * np.pi * (kr % 3) / 3
    cr = np.tile(np.cos(ang), 2)
    ci = np.tile(np.sin(ang), 2)
    with np.errstate(invalid="ignore"):
        d = np.where(kc == 0, FRAG_LEN, np.sin(np.pi * FRAG_LEN * kc / WIDTH) / np.sin(np.pi * kc / WIDTH))
    d = d / math.sqrt(WIDTH)
    col = np.concatenate([cr, ci, d, -d])
    consts = np.repeat(col[:, None], 128, 1).astype(np.float32)
    return fwd, up, down, tabs, consts


def split(x):
    hi = x.astype(BF16)
    return hi, (x - hi.astype(F32)).astype(BF16)


def dot(a, b):
    return lax.dot_general(a, b, (((1,), (0,)), ((), ())), preferred_element_type=F32)


def dot_nt(a, b):
    return lax.dot_general(a, b, (((1,), (1,)), ((), ())), preferred_element_type=F32)


def table_dot(table3, x):
    hi, lo = split(x)
    return dot(table3, jnp.concatenate([hi, lo, hi], 0))


def sin_turns(u):
    y = u * (2.0 * math.pi)
    s = y * y
    p = jnp.full_like(s, -1.0 / 39916800.0)
    for coef in (1.0 / 362880.0, -1.0 / 5040.0, 1.0 / 120.0, -1.0 / 6.0):
        p = p * s + coef
    return y + y * (s * p)


def cos_turns(t):
    t = t - jnp.floor(t + 0.5)
    return sin_turns(0.25 - jnp.abs(t))


def times_i(z, sign):
    return pltpu.roll(z, 64, axis=1) * sign


def lane_sign(shape):
    lane = lax.broadcasted_iota(jnp.int32, shape, 1)
    return jnp.where(lane < 64, -1.0, 1.0).astype(F32)


def fragment_tables(rows, cols, dsc):
    kr = lax.broadcasted_iota(jnp.int32, (32, SLOTS), 0)
    is_sin = kr >= 16
    kr = ((kr & 15) - 8).astype(F32)
    t = kr * rows.astype(F32) * (1.0 / EXT)
    row_tab = cos_turns(t - jnp.where(is_sin, 0.25, 0.0)) * (1.0 / math.sqrt(EXT))
    kc = lax.broadcasted_iota(jnp.int32, (128, SLOTS), 0)
    is_sin = kc >= 64
    kc = ((kc & 63) - 32).astype(F32)
    t = kc * (2 * cols + (FRAG_LEN - 1)).astype(F32) * (1.0 / (2 * WIDTH))
    col_tab = cos_turns(t - jnp.where(is_sin, 0.25, 0.0)) * dsc
    return row_tab, col_tab


def own_modes(packed, row_tab, col_hi, col_lo, amp, lt3, sign):
    u0 = table_dot(lt3, packed)
    hi, lo = split(row_tab * amp)
    u1 = dot_nt(
        jnp.concatenate([hi, lo, hi], 1), jnp.concatenate([col_hi, col_hi, col_lo], 1)
    )
    u_re = jnp.concatenate([u0[:16], u1[:16]], 0)
    u_im = jnp.concatenate([u0[16:], u1[16:]], 0)
    return u_re - times_i(u_im, sign)


def combine(own, left, right, cr, ci, sign):
    return own + cr * (left + right) + ci * times_i(left - right, sign)


def two_forms(h, low):
    turned = pltpu.roll(h, 64, axis=1)
    return jnp.where(low, h, turned), jnp.where(low, turned, h)


def forward_group(hrr, hii, modes, imodes, ag3, inv3):
    blocks = []
    for j in range(2):
        m, im = modes[16 * j : 16 * j + 16], imodes[16 * j : 16 * j + 16]
        for k in range(len(hrr)):
            p = hrr[k] * m + hii[k] * im
            ip = hrr[k] * im - hii[k] * m
            blocks.append(jnp.concatenate([p, ip], 0))
    rows = table_dot(ag3, jnp.concatenate(blocks, 1))
    stacked = jnp.concatenate([rows[:, 128 * b : 128 * b + 128] for b in range(len(blocks))], 0)
    hi, lo = split(stacked)
    amps = dot(jnp.concatenate([hi, lo, hi], 1), inv3)
    half = amps.shape[0] // 2
    return amps[:half], amps[half:]


def intensity_terms(e0, e1, kernels):
    total0 = total1 = None
    for k in range(kernels):
        a, b = e0[32 * k : 32 * k + 32], e1[32 * k : 32 * k + 32]
        s0, s1 = a * a, a * b
        total0 = s0 if total0 is None else total0 + s0
        total1 = s1 if total1 is None else total1 + s1
    return total0[:, :128] + total0[:, 128:], total1[:, :128] + total1[:, 128:]


def weighting(inten, change, target):
    developed = 1.0 / (1.0 + jnp.exp(-STEEP * (inten - THRESH)))
    steep = STEEP * developed * (1.0 - developed)
    return steep * (developed - target), steep * steep * change


def adjoint_group(e0, w0, w1, kernels, hrr, hii, adj, agt3):
    loads = []
    for w in (w0, w1):
        ww = jnp.concatenate([w, w], 1)
        for k in range(kernels):
            loads.append(ww * e0[32 * k : 32 * k + 32])
    hi, lo = split(jnp.concatenate(loads, 0))
    both = dot(hi, adj)
    back = both[:, :128] + both[:, 128:] + dot(lo, adj[:, :128])
    wide = jnp.concatenate([back[32 * b : 32 * b + 32] for b in range(2 * kernels)], 1)
    u = table_dot(agt3, wide)
    first, second = [], []
    for j in range(2):
        f = s = None
        for k in range(kernels):
            at = 128 * (j * kernels + k)
            u1, u2 = u[:16, at : at + 128], u[16:, at : at + 128]
            a = hrr[k] * u1 - hii[k] * u2
            b = hrr[k] * u2 + hii[k] * u1
            f = a if f is None else f + a
            s = b if s is None else s + b
        first.append(f)
        second.append(s)
    return jnp.concatenate(first, 0), jnp.concatenate(second, 0)


def project(total, row_tab, col_hi, col_lo, sign):
    it = times_i(total, sign)
    lhs = jnp.concatenate([total[:16], it[:16], total[16:], it[16:]], 0)
    hi, lo = split(lhs)
    q = dot(jnp.concatenate([hi, lo, hi], 1), jnp.concatenate([col_hi, col_hi, col_lo], 0))
    return [jnp.sum(q[32 * j : 32 * j + 32] * row_tab, axis=0, keepdims=True) for j in range(2)]


def kernel(
    weights_ref,
    counts_ref,
    rows_ref,
    cols_ref,
    step_ref,
    spectra_ref,
    tabs_ref,
    consts_ref,
    mask_hbm,
    target_hbm,
    fwd_hbm,
    up_hbm,
    down_hbm,
    grad_ref,
    curv_ref,
    mask_v,
    target_v,
    fwd_v,
    up_v,
    down_v,
    h_v,
    e0_v,
    m_own,
    m_got,
    y_own,
    y_got,
    load_sem,
    h_send,
    h_recv,
    m_send,
    m_recv,
    y_send,
    y_recv,
):
    tile = lax.axis_index("tile")
    kern = lax.axis_index("kern")
    left = lax.rem(tile + TILES - 1, TILES)
    right = lax.rem(tile + 1, TILES)
    across = lax.rem(kern + 2, KERN)
    sides = ({"tile": left, "kern": across}, {"tile": right, "kern": across})
    peers = [{"tile": tile, "kern": lax.rem(kern + d, KERN)} for d in (1, 2, 3)]

    barrier = pltpu.get_barrier_semaphore()
    for device in (*sides, *peers):
        pl.semaphore_signal(barrier, inc=1, device_id=device, device_id_type=MESH)

    width = WIDTH // CHUNKS
    mask_copies, fwd_copies = [], []
    for c in range(CHUNKS):
        part = pl.ds(c * width, width)
        mask_copies.append(
            pltpu.make_async_copy(mask_hbm.at[:, part], mask_v.at[:, part], load_sem.at[c])
        )
        fwd_copies.append(
            pltpu.make_async_copy(fwd_hbm.at[part, :], fwd_v.at[part, :], load_sem.at[CHUNKS + c])
        )
    later = [
        pltpu.make_async_copy(up_hbm, up_v, load_sem.at[2 * CHUNKS]),
        pltpu.make_async_copy(target_hbm, target_v, load_sem.at[2 * CHUNKS + 1]),
        pltpu.make_async_copy(down_hbm, down_v, load_sem.at[2 * CHUNKS + 2]),
    ]
    for a, b in zip(mask_copies, fwd_copies):
        a.start()
        b.start()
    for copy in later:
        copy.start()

    mine = pl.multiple_of(kern * LOCAL, LOCAL)
    for k in range(LOCAL):
        scale = jnp.sqrt(jnp.full((ROW_FREQS, 128), weights_ref[k] * (2.0 / KERNELS), F32))
        h_v[mine + k] = spectra_ref[k] * scale

    pl.semaphore_wait(barrier, 5)
    h_copies = []
    for d in range(3):
        copy = pltpu.make_async_remote_copy(
            src_ref=h_v.at[pl.ds(mine, LOCAL)],
            dst_ref=h_v.at[pl.ds(mine, LOCAL)],
            send_sem=h_send.at[d],
            recv_sem=h_recv.at[d],
            device_id=peers[d],
            device_id_type=MESH,
        )
        copy.start()
        h_copies.append(copy)

    sign = lane_sign((32, 128))
    cr, ci = consts_ref[0:32], consts_ref[32:64]
    dsc = consts_ref[64:192]
    row_tab, col_tab = fragment_tables(rows_ref[...], cols_ref[...], jnp.concatenate([dsc, dsc], 1))
    col_hi, col_lo = split(col_tab)
    active = lax.broadcasted_iota(jnp.int32, (1, SLOTS), 1) < counts_ref[0]
    amp = jnp.where(active, step_ref[...], 0.0) * (1.0 / math.sqrt(FRAG_LEN))

    total = jnp.zeros((2 * SLAB, 256), F32)
    for c in range(CHUNKS):
        mask_copies[c].wait()
        fwd_copies[c].wait()
        hi, lo = split(mask_v[:, c * width : (c + 1) * width])
        total += dot(jnp.concatenate([hi, lo], 0), fwd_v[c * width : (c + 1) * width, :])
    packed = total[:SLAB, :128] + total[:SLAB, 128:] + total[SLAB:, :128]
    modes_own = own_modes(packed, row_tab, col_hi, col_lo, amp, tabs_ref[640:672, :192], sign)
    m_own[...] = modes_own

    def exchange(own, got, send, recv):
        copies = []
        for d in range(2):
            copy = pltpu.make_async_remote_copy(
                src_ref=own,
                dst_ref=got.at[d],
                send_sem=send.at[d],
                recv_sem=recv.at[d],
                device_id=sides[d],
                device_id_type=MESH,
            )
            copy.start()
            copies.append(copy)
        return copies

    has_left = jnp.where(tile > 0, 1.0, 0.0).astype(F32)
    has_right = jnp.where(tile < TILES - 1, 1.0, 0.0).astype(F32)

    m_copies = exchange(m_own, m_got, m_send, m_recv)
    for copy in m_copies:
        copy.wait()
    modes = combine(modes_own, m_got[1] * has_left, m_got[0] * has_right, cr, ci, sign)
    imodes = times_i(modes, sign)

    for copy in h_copies:
        copy.wait()

    low = lax.broadcasted_iota(jnp.int32, (ROW_FREQS, 128), 1) < 64

    def forms(g):
        pairs = [two_forms(h_v[g * LOCAL + k], low) for k in range(LOCAL)]
        return [a for a, _ in pairs], [b for _, b in pairs]

    inten = change = None
    for g in range(KERN):
        hrr, hii = forms(g)
        e0, e1 = forward_group(hrr, hii, modes, imodes, tabs_ref[672:704, :96], tabs_ref[0:384, :])
        e0_v[g] = e0
        s0, s1 = intensity_terms(e0, e1, LOCAL)
        inten = s0 if inten is None else inten + s0
        change = s1 if change is None else change + s1

    grids = table_dot(tabs_ref[736:800, :96], jnp.concatenate([0.5 * inten, change], 1))
    hi, lo = split(jnp.concatenate([grids[:, :128], grids[:, 128:]], 0))
    rows3 = jnp.concatenate([hi, lo, hi], 1)
    for copy in later:
        copy.wait()
    span = 256
    total = jnp.zeros((4 * SLAB, 256), F32)
    for c in range(WIDTH // span):
        part = slice(c * span, (c + 1) * span)
        full = dot(rows3, up_v[:, part])
        w0, w1 = weighting(full[:SLAB], full[SLAB:], target_v[:, part])
        hi, lo = split(jnp.concatenate([w0, w1], 0))
        total += dot(jnp.concatenate([hi, lo], 0), down_v[part, :])
    n = 2 * SLAB
    cols = total[:n, :128] + total[:n, 128:] + total[n:, :128]
    wgrid = table_dot(tabs_ref[800:832, :192], jnp.concatenate([cols[:SLAB], cols[SLAB:]], 1))
    w0, w1 = wgrid[:, :128], wgrid[:, 128:]

    first = second = None
    for g in range(KERN):
        hrr, hii = forms(g)
        a, b = adjoint_group(
            e0_v[g], w0, w1, LOCAL, hrr, hii, tabs_ref[384:640, :], tabs_ref[704:736, :96]
        )
        first = a if first is None else first + a
        second = b if second is None else second + b
    spectrum = first - times_i(second, sign)
    y_own[...] = spectrum

    y_copies = exchange(y_own, y_got, y_send, y_recv)
    for copy in y_copies:
        copy.wait()
    whole = combine(spectrum, y_got[1] * has_left, y_got[0] * has_right, cr, ci, sign)
    outs = project(whole, row_tab, col_hi, col_lo, sign)
    for ref, out in zip((grad_ref, curv_ref), outs):
        ref[...] = jnp.where(active, out * (1.0 / math.sqrt(FRAG_LEN)), 0.0)


def shards(mask, target, spectra, weights, counts, frag_rows, frag_cols, step):
    fwd, up, down, tabs, consts = make_tables()
    vmem = pl.BlockSpec(memory_space=pltpu.VMEM)
    smem = pl.BlockSpec(memory_space=pltpu.SMEM)
    hbm = pl.BlockSpec(memory_space=pl.ANY)
    dma = pltpu.SemaphoreType.DMA
    grad, curv = pl.pallas_call(
        kernel,
        out_shape=[jax.ShapeDtypeStruct((1, SLOTS), F32)] * 2,
        in_specs=[smem, smem] + [vmem] * 6 + [hbm] * 5,
        out_specs=[vmem, vmem],
        scratch_shapes=[
            pltpu.VMEM((SLAB, WIDTH), F32),
            pltpu.VMEM((SLAB, WIDTH), F32),
            pltpu.VMEM((WIDTH, 256), BF16),
            pltpu.VMEM((384, WIDTH), BF16),
            pltpu.VMEM((WIDTH, 256), BF16),
            pltpu.VMEM((KERNELS, ROW_FREQS, 128), F32),
            pltpu.VMEM((KERN, LOCAL * GRID_ROWS, 256), F32),
            pltpu.VMEM((32, 128), F32),
            pltpu.VMEM((2, 32, 128), F32),
            pltpu.VMEM((32, 128), F32),
            pltpu.VMEM((2, 32, 128), F32),
            dma((2 * CHUNKS + 3,)),
            dma((3,)),
            dma((3,)),
            dma((2,)),
            dma((2,)),
            dma((2,)),
            dma((2,)),
        ],
        compiler_params=pltpu.CompilerParams(
            collective_id=0, has_side_effects=True, vmem_limit_bytes=48 * 1024 * 1024
        ),
    )(
        weights,
        counts,
        frag_rows.reshape(1, SLOTS),
        frag_cols.reshape(1, SLOTS),
        step.reshape(1, SLOTS),
        spectra,
        jnp.asarray(tabs),
        jnp.asarray(consts),
        mask,
        target,
        jnp.asarray(fwd),
        jnp.asarray(up),
        jnp.asarray(down),
    )
    return grad.reshape(SLOTS), curv.reshape(SLOTS)


def solution(mesh):
    return jax.shard_map(
        shards,
        mesh=mesh,
        in_specs=(
            P("tile", None),
            P("tile", None),
            P("kern", None, None),
            P("kern"),
            P("tile"),
            P("tile"),
            P("tile"),
            P("tile"),
        ),
        out_specs=(P("tile"), P("tile")),
        check_vma=False,
    )
```

```python
import functools
import math

import jax
import jax.numpy as jnp
import ml_dtypes
import numpy as np
from jax import lax
from jax.experimental import pallas as pl
from jax.experimental.pallas import tpu as pltpu
from jax.sharding import PartitionSpec as P

WIDTH = 2048
COL_FREQS = 64
ROW_FREQS = 16
KERNELS = 24
FRAG_LEN = 32
SLAB = 64
SLOTS = 256
EXT = 192
TILES = 64
KERN = 4
LOCAL = KERNELS // KERN
GRID_ROWS = 32
GRID_COLS = 128
STEEP = 10.0
THRESH = 0.1
F32 = jnp.float32
BF16 = jnp.bfloat16
CHUNKS = 4
MESH = pl.DeviceIdType.MESH


def np_split(x):
    hi = x.astype(np.float32).astype(ml_dtypes.bfloat16)
    lo = (x - hi.astype(np.float64)).astype(np.float32).astype(ml_dtypes.bfloat16)
    return hi, lo


def pad_lanes(x, lanes=256):
    return np.pad(x, ((0, 0), (0, lanes - x.shape[1])))


@functools.lru_cache(maxsize=None)
def make_tables():
    kc = np.arange(COL_FREQS) - COL_FREQS // 2
    kr = np.arange(ROW_FREQS) - ROW_FREQS // 2
    x = np.arange(WIDTH)
    ang = 2 * np.pi * (np.outer(x, kc) % WIDTH) / WIDTH
    f_hi, f_lo = np_split(np.concatenate([np.cos(ang), -np.sin(ang)], 1) / math.sqrt(WIDTH))
    fwd = np.concatenate([f_hi, f_lo], 1)

    n = np.arange(GRID_COLS)
    step = WIDTH // GRID_COLS
    dist = (x[None, :] - step * n[:, None]) % WIDTH
    base = np.ones(WIDTH)
    for kap in range(1, COL_FREQS):
        base += 2 * np.cos(2 * np.pi * ((np.arange(WIDTH) * kap) % WIDTH) / WIDTH)
    g = (base / GRID_COLS)[dist]
    g_hi, g_lo = np_split(g)
    up = np.concatenate([g_hi, g_hi, g_lo], 0)
    gt_hi, gt_lo = np_split(g.T)
    down = np.concatenate([gt_hi, gt_lo], 1)

    ang = 2 * np.pi * (np.outer(kc, n) % GRID_COLS) / GRID_COLS
    c, s = np.cos(ang) / math.sqrt(WIDTH), np.sin(ang) / math.sqrt(WIDTH)
    inv = np.block([[c, s], [-s, c]])
    i_hi, i_lo = np_split(inv)
    inv3 = np.concatenate([i_hi, i_hi, i_lo], 0)
    t_hi, t_lo = np_split(inv.T)
    adj = np.concatenate([t_hi, t_lo], 1)

    e = np.arange(SLAB)
    ang = 2 * np.pi * (np.outer(kr, e) % EXT) / EXT
    a_hi, a_lo = np_split(np.concatenate([np.cos(ang), np.sin(ang)], 0) / math.sqrt(EXT))
    lt3 = np.concatenate([a_hi, a_hi, a_lo], 1)

    m = np.arange(GRID_ROWS)
    ang = 2 * np.pi * (np.outer(m, kr) % GRID_ROWS) / GRID_ROWS
    ag = np.concatenate([np.cos(ang), np.sin(ang)], 1) / math.sqrt(EXT)
    hi, lo = np_split(ag)
    ag3 = np.concatenate([hi, hi, lo], 1)
    hi, lo = np_split(ag.T)
    agt3 = np.concatenate([hi, hi, lo], 1)

    rstep = EXT // GRID_ROWS
    dist = (e[:, None] - rstep * m[None, :]) % EXT
    base = np.ones(EXT)
    for rho in range(1, ROW_FREQS):
        base += 2 * np.cos(2 * np.pi * ((np.arange(EXT) * rho) % EXT) / EXT)
    r = (base / GRID_ROWS)[dist]
    hi, lo = np_split(r)
    r3 = np.concatenate([hi, hi, lo], 1)
    hi, lo = np_split(r.T)
    rt3 = np.concatenate([hi, hi, lo], 1)

    tabs = np.concatenate(
        [inv3, adj, pad_lanes(lt3), pad_lanes(ag3), pad_lanes(agt3), pad_lanes(r3), pad_lanes(rt3)], 0
    )

    ang = 2 * np.pi * (kr % 3) / 3
    cr = np.tile(np.cos(ang), 2)
    ci = np.tile(np.sin(ang), 2)
    with np.errstate(invalid="ignore"):
        d = np.where(kc == 0, FRAG_LEN, np.sin(np.pi * FRAG_LEN * kc / WIDTH) / np.sin(np.pi * kc / WIDTH))
    d = d / math.sqrt(WIDTH)
    col = np.concatenate([cr, ci, d, -d])
    consts = np.repeat(col[:, None], 128, 1).astype(np.float32)
    return fwd, up, down, tabs, consts


def split(x):
    hi = x.astype(BF16)
    return hi, (x - hi.astype(F32)).astype(BF16)


def dot(a, b):
    return lax.dot_general(a, b, (((1,), (0,)), ((), ())), preferred_element_type=F32)


def dot_nt(a, b):
    return lax.dot_general(a, b, (((1,), (1,)), ((), ())), preferred_element_type=F32)


def table_dot(table3, x):
    hi, lo = split(x)
    return dot(table3, jnp.concatenate([hi, lo, hi], 0))


def sin_turns(u):
    y = u * (2.0 * math.pi)
    s = y * y
    p = jnp.full_like(s, -1.0 / 39916800.0)
    for coef in (1.0 / 362880.0, -1.0 / 5040.0, 1.0 / 120.0, -1.0 / 6.0):
        p = p * s + coef
    return y + y * (s * p)


def cos_turns(t):
    t = t - jnp.floor(t + 0.5)
    return sin_turns(0.25 - jnp.abs(t))


def times_i(z, sign):
    return pltpu.roll(z, 64, axis=1) * sign


def lane_sign(shape):
    lane = lax.broadcasted_iota(jnp.int32, shape, 1)
    return jnp.where(lane < 64, -1.0, 1.0).astype(F32)


def fragment_tables(rows, cols, dsc):
    kr = lax.broadcasted_iota(jnp.int32, (32, SLOTS), 0)
    is_sin = kr >= 16
    kr = ((kr & 15) - 8).astype(F32)
    t = kr * rows.astype(F32) * (1.0 / EXT)
    row_tab = cos_turns(t - jnp.where(is_sin, 0.25, 0.0)) * (1.0 / math.sqrt(EXT))
    kc = lax.broadcasted_iota(jnp.int32, (128, SLOTS), 0)
    is_sin = kc >= 64
    kc = ((kc & 63) - 32).astype(F32)
    t = kc * (2 * cols + (FRAG_LEN - 1)).astype(F32) * (1.0 / (2 * WIDTH))
    col_tab = cos_turns(t - jnp.where(is_sin, 0.25, 0.0)) * dsc
    return row_tab, col_tab


def own_modes(packed, row_tab, col_hi, col_lo, amp, lt3, sign):
    u0 = table_dot(lt3, packed)
    hi, lo = split(row_tab * amp)
    u1 = dot_nt(
        jnp.concatenate([hi, lo, hi], 1), jnp.concatenate([col_hi, col_hi, col_lo], 1)
    )
    u_re = jnp.concatenate([u0[:16], u1[:16]], 0)
    u_im = jnp.concatenate([u0[16:], u1[16:]], 0)
    return u_re - times_i(u_im, sign)


def combine(own, left, right, cr, ci, sign):
    return own + cr * (left + right) + ci * times_i(left - right, sign)


def two_forms(h, low):
    turned = pltpu.roll(h, 64, axis=1)
    return jnp.where(low, h, turned), jnp.where(low, turned, h)


def forward_group(hrr, hii, modes, imodes, ag3, inv3):
    blocks = []
    for j in range(2):
        m, im = modes[16 * j : 16 * j + 16], imodes[16 * j : 16 * j + 16]
        for k in range(len(hrr)):
            p = hrr[k] * m + hii[k] * im
            ip = hrr[k] * im - hii[k] * m
            blocks.append(jnp.concatenate([p, ip], 0))
    rows = table_dot(ag3, jnp.concatenate(blocks, 1))
    stacked = jnp.concatenate([rows[:, 128 * b : 128 * b + 128] for b in range(len(blocks))], 0)
    hi, lo = split(stacked)
    amps = dot(jnp.concatenate([hi, lo, hi], 1), inv3)
    half = amps.shape[0] // 2
    return amps[:half], amps[half:]


def intensity_terms(e0, e1, kernels):
    total0 = total1 = None
    for k in range(kernels):
        a, b = e0[32 * k : 32 * k + 32], e1[32 * k : 32 * k + 32]
        s0, s1 = a * a, a * b
        total0 = s0 if total0 is None else total0 + s0
        total1 = s1 if total1 is None else total1 + s1
    return total0[:, :128] + total0[:, 128:], total1[:, :128] + total1[:, 128:]


def weighting(inten, change, target):
    developed = 1.0 / (1.0 + jnp.exp(-STEEP * (inten - THRESH)))
    steep = STEEP * developed * (1.0 - developed)
    return steep * (developed - target), steep * steep * change


def adjoint_group(e0, w0, w1, kernels, hrr, hii, adj, agt3):
    loads = []
    for w in (w0, w1):
        ww = jnp.concatenate([w, w], 1)
        for k in range(kernels):
            loads.append(ww * e0[32 * k : 32 * k + 32])
    hi, lo = split(jnp.concatenate(loads, 0))
    both = dot(hi, adj)
    back = both[:, :128] + both[:, 128:] + dot(lo, adj[:, :128])
    wide = jnp.concatenate([back[32 * b : 32 * b + 32] for b in range(2 * kernels)], 1)
    u = table_dot(agt3, wide)
    first, second = [], []
    for j in range(2):
        f = s = None
        for k in range(kernels):
            at = 128 * (j * kernels + k)
            u1, u2 = u[:16, at : at + 128], u[16:, at : at + 128]
            a = hrr[k] * u1 - hii[k] * u2
            b = hrr[k] * u2 + hii[k] * u1
            f = a if f is None else f + a
            s = b if s is None else s + b
        first.append(f)
        second.append(s)
    return jnp.concatenate(first, 0), jnp.concatenate(second, 0)


def project(total, row_tab, col_hi, col_lo, sign):
    it = times_i(total, sign)
    lhs = jnp.concatenate([total[:16], it[:16], total[16:], it[16:]], 0)
    hi, lo = split(lhs)
    q = dot(jnp.concatenate([hi, lo, hi], 1), jnp.concatenate([col_hi, col_hi, col_lo], 0))
    return [jnp.sum(q[32 * j : 32 * j + 32] * row_tab, axis=0, keepdims=True) for j in range(2)]


def kernel(
    weights_hbm,
    counts_hbm,
    rows_hbm,
    cols_hbm,
    step_hbm,
    spectra_hbm,
    tabs_hbm,
    consts_hbm,
    mask_hbm,
    target_hbm,
    fwd_hbm,
    up_hbm,
    down_hbm,
    out_ref,
    weights_s,
    counts_s,
    rows_v,
    cols_v,
    step_v,
    spectra_v,
    tabs_v,
    consts_v,
    mask_v,
    target_v,
    fwd_v,
    up_v,
    down_v,
    h_v,
    e0_v,
    m_own,
    m_got,
    y_own,
    y_got,
    load_sem,
    h_send,
    h_recv,
    m_send,
    m_recv,
    y_send,
    y_recv,
):
    tile = lax.axis_index("tile")
    kern = lax.axis_index("kern")
    across = lax.rem(kern + 2, KERN)
    sides = (
        (tile > 0, {"tile": lax.max(tile - 1, 0), "kern": across}),
        (tile < TILES - 1, {"tile": lax.min(tile + 1, TILES - 1), "kern": across}),
    )
    peers = [{"tile": tile, "kern": lax.rem(kern + d, KERN)} for d in (1, 2, 3)]

    for d, (exists, _) in enumerate(sides):

        @pl.when(jnp.logical_not(exists))
        def _():
            m_got[1 - d] = jnp.zeros((32, 128), F32)
            y_got[1 - d] = jnp.zeros((32, 128), F32)

    barrier = pltpu.get_barrier_semaphore()
    for device in peers:
        pl.semaphore_signal(barrier, inc=1, device_id=device, device_id_type=MESH)
    for exists, device in sides:

        @pl.when(exists)
        def _():
            pl.semaphore_signal(barrier, inc=1, device_id=device, device_id_type=MESH)

    used = []

    def load(src, dst):
        copy = pltpu.make_async_copy(src, dst, load_sem.at[len(used)])
        used.append(copy)
        return copy

    width = WIDTH // CHUNKS
    early = [load(weights_hbm, weights_s), load(spectra_hbm, spectra_v)]
    small = [
        load(a, b)
        for a, b in (
            (counts_hbm, counts_s),
            (rows_hbm, rows_v),
            (cols_hbm, cols_v),
            (step_hbm, step_v),
            (consts_hbm, consts_v),
            (tabs_hbm, tabs_v),
        )
    ]
    parts = [pl.ds(c * width, width) for c in range(CHUNKS)]
    mask_copies = [load(mask_hbm.at[:, p], mask_v.at[:, p]) for p in parts]
    fwd_copies = [load(fwd_hbm.at[p, :], fwd_v.at[p, :]) for p in parts]
    later = [load(up_hbm, up_v), load(target_hbm, target_v), load(down_hbm, down_v)]
    for copy in early:
        copy.start()
    for a, b in zip(mask_copies, fwd_copies):
        a.start()
        b.start()
    for copy in small + later:
        copy.start()

    for copy in early:
        copy.wait()
    mine = pl.multiple_of(kern * LOCAL, LOCAL)
    for k in range(LOCAL):
        scale = jnp.sqrt(jnp.full((ROW_FREQS, 128), weights_s[k] * (2.0 / KERNELS), F32))
        h_v[mine + k] = spectra_v[k] * scale

    pl.semaphore_wait(barrier, 3 + lax.min(tile, 1) + lax.min(TILES - 1 - tile, 1))
    h_copies = []
    for d in range(3):
        copy = pltpu.make_async_remote_copy(
            src_ref=h_v.at[pl.ds(mine, LOCAL)],
            dst_ref=h_v.at[pl.ds(mine, LOCAL)],
            send_sem=h_send.at[d],
            recv_sem=h_recv.at[d],
            device_id=peers[d],
            device_id_type=MESH,
        )
        copy.start()
        h_copies.append(copy)

    for copy in small:
        copy.wait()
    sign = lane_sign((32, 128))
    cr, ci = consts_v[0:32], consts_v[32:64]
    dsc = consts_v[64:192]
    row_tab, col_tab = fragment_tables(rows_v[...], cols_v[...], jnp.concatenate([dsc, dsc], 1))
    col_hi, col_lo = split(col_tab)
    active = lax.broadcasted_iota(jnp.int32, (1, SLOTS), 1) < counts_s[0]
    amp = jnp.where(active, step_v[...], 0.0) * (1.0 / math.sqrt(FRAG_LEN))

    total = jnp.zeros((2 * SLAB, 256), F32)
    for c in range(CHUNKS):
        mask_copies[c].wait()
        fwd_copies[c].wait()
        hi, lo = split(mask_v[:, c * width : (c + 1) * width])
        total += dot(jnp.concatenate([hi, lo], 0), fwd_v[c * width : (c + 1) * width, :])
    packed = total[:SLAB, :128] + total[:SLAB, 128:] + total[SLAB:, :128]
    modes_own = own_modes(packed, row_tab, col_hi, col_lo, amp, tabs_v[640:672, :192], sign)
    m_own[...] = modes_own

    def exchange(own, got, send, recv):
        copies = [
            pltpu.make_async_remote_copy(
                src_ref=own,
                dst_ref=got.at[d],
                send_sem=send.at[d],
                recv_sem=recv.at[d],
                device_id=device,
                device_id_type=MESH,
            )
            for d, (_, device) in enumerate(sides)
        ]
        for d, (exists, _) in enumerate(sides):

            @pl.when(exists)
            def _():
                copies[d].start()

        for d, (exists, _) in enumerate(sides):

            @pl.when(exists)
            def _():
                copies[1 - d].wait_recv()

        return copies

    def sent(copies):
        for d, (exists, _) in enumerate(sides):

            @pl.when(exists)
            def _():
                copies[d].wait_send()

    m_copies = exchange(m_own, m_got, m_send, m_recv)
    modes = combine(modes_own, m_got[1], m_got[0], cr, ci, sign)
    imodes = times_i(modes, sign)

    for copy in h_copies:
        copy.wait()

    low = lax.broadcasted_iota(jnp.int32, (ROW_FREQS, 128), 1) < 64

    def forms(g):
        pairs = [two_forms(h_v[g * LOCAL + k], low) for k in range(LOCAL)]
        return [a for a, _ in pairs], [b for _, b in pairs]

    inten = change = None
    for g in range(KERN):
        hrr, hii = forms(g)
        e0, e1 = forward_group(hrr, hii, modes, imodes, tabs_v[672:704, :96], tabs_v[0:384, :])
        e0_v[g] = e0
        s0, s1 = intensity_terms(e0, e1, LOCAL)
        inten = s0 if inten is None else inten + s0
        change = s1 if change is None else change + s1

    grids = table_dot(tabs_v[736:800, :96], jnp.concatenate([0.5 * inten, change], 1))
    hi, lo = split(jnp.concatenate([grids[:, :128], grids[:, 128:]], 0))
    rows3 = jnp.concatenate([hi, lo, hi], 1)
    for copy in later:
        copy.wait()
    span = 256
    total = jnp.zeros((4 * SLAB, 256), F32)
    for c in range(WIDTH // span):
        part = slice(c * span, (c + 1) * span)
        full = dot(rows3, up_v[:, part])
        w0, w1 = weighting(full[:SLAB], full[SLAB:], target_v[:, part])
        hi, lo = split(jnp.concatenate([w0, w1], 0))
        total += dot(jnp.concatenate([hi, lo], 0), down_v[part, :])
    n = 2 * SLAB
    cols = total[:n, :128] + total[:n, 128:] + total[n:, :128]
    wgrid = table_dot(tabs_v[800:832, :192], jnp.concatenate([cols[:SLAB], cols[SLAB:]], 1))
    w0, w1 = wgrid[:, :128], wgrid[:, 128:]

    first = second = None
    for g in range(KERN):
        hrr, hii = forms(g)
        a, b = adjoint_group(
            e0_v[g], w0, w1, LOCAL, hrr, hii, tabs_v[384:640, :], tabs_v[704:736, :96]
        )
        first = a if first is None else first + a
        second = b if second is None else second + b
    spectrum = first - times_i(second, sign)
    y_own[...] = spectrum

    y_copies = exchange(y_own, y_got, y_send, y_recv)
    whole = combine(spectrum, y_got[1], y_got[0], cr, ci, sign)
    outs = project(whole, row_tab, col_hi, col_lo, sign)
    for j in range(2):
        out_ref[j : j + 1, :] = jnp.where(active, outs[j] * (1.0 / math.sqrt(FRAG_LEN)), 0.0)
    sent(m_copies)
    sent(y_copies)


def shards(mask, target, spectra, weights, counts, frag_rows, frag_cols, step):
    fwd, up, down, tabs, consts = make_tables()
    vmem = pl.BlockSpec(memory_space=pltpu.VMEM)
    hbm = pl.BlockSpec(memory_space=pltpu.HBM)
    dma = pltpu.SemaphoreType.DMA
    outs = pl.pallas_call(
        kernel,
        out_shape=jax.ShapeDtypeStruct((2, SLOTS), F32),
        in_specs=[hbm] * 13,
        out_specs=vmem,
        scratch_shapes=[
            pltpu.SMEM((LOCAL,), F32),
            pltpu.SMEM((1,), jnp.int32),
            pltpu.VMEM((1, SLOTS), jnp.int32),
            pltpu.VMEM((1, SLOTS), jnp.int32),
            pltpu.VMEM((1, SLOTS), F32),
            pltpu.VMEM((LOCAL, ROW_FREQS, 128), F32),
            pltpu.VMEM(tabs.shape, BF16),
            pltpu.VMEM(consts.shape, F32),
            pltpu.VMEM((SLAB, WIDTH), F32),
            pltpu.VMEM((SLAB, WIDTH), F32),
            pltpu.VMEM((WIDTH, 256), BF16),
            pltpu.VMEM((384, WIDTH), BF16),
            pltpu.VMEM((WIDTH, 256), BF16),
            pltpu.VMEM((KERNELS, ROW_FREQS, 128), F32),
            pltpu.VMEM((KERN, LOCAL * GRID_ROWS, 256), F32),
            pltpu.VMEM((32, 128), F32),
            pltpu.VMEM((2, 32, 128), F32),
            pltpu.VMEM((32, 128), F32),
            pltpu.VMEM((2, 32, 128), F32),
            dma((2 * CHUNKS + 11,)),
            dma((3,)),
            dma((3,)),
            dma((2,)),
            dma((2,)),
            dma((2,)),
            dma((2,)),
        ],
        compiler_params=pltpu.CompilerParams(
            collective_id=0, has_side_effects=True, vmem_limit_bytes=64 * 1024 * 1024
        ),
    )(
        weights,
        counts,
        frag_rows.reshape(1, SLOTS),
        frag_cols.reshape(1, SLOTS),
        step.reshape(1, SLOTS),
        spectra,
        jnp.asarray(tabs),
        jnp.asarray(consts),
        mask,
        target,
        jnp.asarray(fwd),
        jnp.asarray(up),
        jnp.asarray(down),
    )
    return outs[0], outs[1]


def solution(mesh):
    return jax.shard_map(
        shards,
        mesh=mesh,
        in_specs=(
            P("tile", None),
            P("tile", None),
            P("kern", None, None),
            P("kern"),
            P("tile"),
            P("tile"),
            P("tile"),
            P("tile"),
        ),
        out_specs=(P("tile"), P("tile")),
        check_vma=False,
    )
```

```python
import functools
import math

import jax
import jax.numpy as jnp
import ml_dtypes
import numpy as np
from jax import lax
from jax.experimental import pallas as pl
from jax.experimental.pallas import tpu as pltpu
from jax.sharding import PartitionSpec as P

WIDTH = 2048
COL_FREQS = 64
ROW_FREQS = 16
KERNELS = 24
FRAG_LEN = 32
SLAB = 64
SLOTS = 256
EXT = 192
TILES = 64
KERN = 4
LOCAL = KERNELS // KERN
GRID_ROWS = 32
GRID_COLS = 128
STEEP = 10.0
THRESH = 0.1
F32 = jnp.float32
BF16 = jnp.bfloat16
CHUNKS = 4
MESH = pl.DeviceIdType.MESH


def np_split(x):
    hi = x.astype(np.float32).astype(ml_dtypes.bfloat16)
    lo = (x - hi.astype(np.float64)).astype(np.float32).astype(ml_dtypes.bfloat16)
    return hi, lo


def pad_lanes(x, lanes=256):
    return np.pad(x, ((0, 0), (0, lanes - x.shape[1])))


@functools.lru_cache(maxsize=None)
def make_tables():
    kc = np.arange(COL_FREQS) - COL_FREQS // 2
    kr = np.arange(ROW_FREQS) - ROW_FREQS // 2
    x = np.arange(WIDTH)
    ang = 2 * np.pi * (np.outer(x, kc) % WIDTH) / WIDTH
    f_hi, f_lo = np_split(np.concatenate([np.cos(ang), -np.sin(ang)], 1) / math.sqrt(WIDTH))
    fwd = np.concatenate([f_hi, f_lo], 1)

    n = np.arange(GRID_COLS)
    step = WIDTH // GRID_COLS
    dist = (x[None, :] - step * n[:, None]) % WIDTH
    base = np.ones(WIDTH)
    for kap in range(1, COL_FREQS):
        base += 2 * np.cos(2 * np.pi * ((np.arange(WIDTH) * kap) % WIDTH) / WIDTH)
    g = (base / GRID_COLS)[dist]
    g_hi, g_lo = np_split(g)
    up = np.concatenate([g_hi, g_hi, g_lo], 0)
    gt_hi, gt_lo = np_split(g.T)
    down = np.concatenate([gt_hi, gt_lo], 1)

    ang = 2 * np.pi * (np.outer(kc, n) % GRID_COLS) / GRID_COLS
    c, s = np.cos(ang) / math.sqrt(WIDTH), np.sin(ang) / math.sqrt(WIDTH)
    inv = np.block([[c, s], [-s, c]])
    i_hi, i_lo = np_split(inv)
    inv3 = np.concatenate([i_hi, i_hi, i_lo], 0)
    t_hi, t_lo = np_split(inv.T)
    adj = np.concatenate([t_hi, t_lo], 1)

    e = np.arange(SLAB)
    ang = 2 * np.pi * (np.outer(kr, e) % EXT) / EXT
    a_hi, a_lo = np_split(np.concatenate([np.cos(ang), np.sin(ang)], 0) / math.sqrt(EXT))
    lt3 = np.concatenate([a_hi, a_hi, a_lo], 1)

    m = np.arange(GRID_ROWS)
    ang = 2 * np.pi * (np.outer(m, kr) % GRID_ROWS) / GRID_ROWS
    ag = np.concatenate([np.cos(ang), np.sin(ang)], 1) / math.sqrt(EXT)
    hi, lo = np_split(ag)
    ag3 = np.concatenate([hi, hi, lo], 1)
    hi, lo = np_split(ag.T)
    agt3 = np.concatenate([hi, hi, lo], 1)

    rstep = EXT // GRID_ROWS
    dist = (e[:, None] - rstep * m[None, :]) % EXT
    base = np.ones(EXT)
    for rho in range(1, ROW_FREQS):
        base += 2 * np.cos(2 * np.pi * ((np.arange(EXT) * rho) % EXT) / EXT)
    r = (base / GRID_ROWS)[dist]
    hi, lo = np_split(r)
    r3 = np.concatenate([hi, hi, lo], 1)
    hi, lo = np_split(r.T)
    rt3 = np.concatenate([hi, hi, lo], 1)

    tabs = np.concatenate(
        [inv3, adj, pad_lanes(lt3), pad_lanes(ag3), pad_lanes(agt3), pad_lanes(r3), pad_lanes(rt3)], 0
    )

    ang = 2 * np.pi * (kr % 3) / 3
    cr = np.tile(np.cos(ang), 2)
    ci = np.tile(np.sin(ang), 2)
    with np.errstate(invalid="ignore"):
        d = np.where(kc == 0, FRAG_LEN, np.sin(np.pi * FRAG_LEN * kc / WIDTH) / np.sin(np.pi * kc / WIDTH))
    d = d / math.sqrt(WIDTH)
    col = np.concatenate([cr, ci, d, -d])
    consts = np.repeat(col[:, None], 128, 1).astype(np.float32)
    return fwd, up, down, tabs, consts


def split(x):
    hi = x.astype(BF16)
    return hi, (x - hi.astype(F32)).astype(BF16)


def dot(a, b):
    return lax.dot_general(a, b, (((1,), (0,)), ((), ())), preferred_element_type=F32)


def dot_nt(a, b):
    return lax.dot_general(a, b, (((1,), (1,)), ((), ())), preferred_element_type=F32)


def table_dot(table3, x):
    hi, lo = split(x)
    return dot(table3, jnp.concatenate([hi, lo, hi], 0))


def sin_turns(u):
    y = u * (2.0 * math.pi)
    s = y * y
    p = jnp.full_like(s, -1.0 / 39916800.0)
    for coef in (1.0 / 362880.0, -1.0 / 5040.0, 1.0 / 120.0, -1.0 / 6.0):
        p = p * s + coef
    return y + y * (s * p)


def cos_turns(t):
    t = t - jnp.floor(t + 0.5)
    return sin_turns(0.25 - jnp.abs(t))


def times_i(z, sign):
    return pltpu.roll(z, 64, axis=1) * sign


def lane_sign(shape):
    lane = lax.broadcasted_iota(jnp.int32, shape, 1)
    return jnp.where(lane < 64, -1.0, 1.0).astype(F32)


def fragment_tables(rows, cols, dsc):
    kr = lax.broadcasted_iota(jnp.int32, (32, SLOTS), 0)
    is_sin = kr >= 16
    kr = ((kr & 15) - 8).astype(F32)
    t = kr * rows.astype(F32) * (1.0 / EXT)
    row_tab = cos_turns(t - jnp.where(is_sin, 0.25, 0.0)) * (1.0 / math.sqrt(EXT))
    kc = lax.broadcasted_iota(jnp.int32, (128, SLOTS), 0)
    is_sin = kc >= 64
    kc = ((kc & 63) - 32).astype(F32)
    t = kc * (2 * cols + (FRAG_LEN - 1)).astype(F32) * (1.0 / (2 * WIDTH))
    col_tab = cos_turns(t - jnp.where(is_sin, 0.25, 0.0)) * dsc
    return row_tab, col_tab


def own_modes(packed, row_tab, col_hi, col_lo, amp, lt3, sign):
    u0 = table_dot(lt3, packed)
    hi, lo = split(row_tab * amp)
    u1 = dot_nt(
        jnp.concatenate([hi, lo, hi], 1), jnp.concatenate([col_hi, col_hi, col_lo], 1)
    )
    u_re = jnp.concatenate([u0[:16], u1[:16]], 0)
    u_im = jnp.concatenate([u0[16:], u1[16:]], 0)
    return u_re - times_i(u_im, sign)


def combine(own, left, right, cr, ci, sign):
    return own + cr * (left + right) + ci * times_i(left - right, sign)


def two_forms(h, low):
    turned = pltpu.roll(h, 64, axis=1)
    return jnp.where(low, h, turned), jnp.where(low, turned, h)


def forward_group(hrr, hii, modes, imodes, ag3, inv3):
    blocks = []
    for j in range(2):
        m, im = modes[16 * j : 16 * j + 16], imodes[16 * j : 16 * j + 16]
        for k in range(len(hrr)):
            p = hrr[k] * m + hii[k] * im
            ip = hrr[k] * im - hii[k] * m
            blocks.append(jnp.concatenate([p, ip], 0))
    rows = table_dot(ag3, jnp.concatenate(blocks, 1))
    stacked = jnp.concatenate([rows[:, 128 * b : 128 * b + 128] for b in range(len(blocks))], 0)
    hi, lo = split(stacked)
    amps = dot(jnp.concatenate([hi, lo, hi], 1), inv3)
    half = amps.shape[0] // 2
    return amps[:half], amps[half:]


def intensity_terms(e0, e1, kernels):
    total0 = total1 = None
    for k in range(kernels):
        a, b = e0[32 * k : 32 * k + 32], e1[32 * k : 32 * k + 32]
        s0, s1 = a * a, a * b
        total0 = s0 if total0 is None else total0 + s0
        total1 = s1 if total1 is None else total1 + s1
    return total0[:, :128] + total0[:, 128:], total1[:, :128] + total1[:, 128:]


def weighting(inten, change, target):
    developed = 1.0 / (1.0 + jnp.exp(-STEEP * (inten - THRESH)))
    steep = STEEP * developed * (1.0 - developed)
    return steep * (developed - target), steep * steep * change


def adjoint_group(e0, w0, w1, kernels, hrr, hii, adj, agt3):
    loads = []
    for w in (w0, w1):
        ww = jnp.concatenate([w, w], 1)
        for k in range(kernels):
            loads.append(ww * e0[32 * k : 32 * k + 32])
    hi, lo = split(jnp.concatenate(loads, 0))
    both = dot(hi, adj)
    back = both[:, :128] + both[:, 128:] + dot(lo, adj[:, :128])
    wide = jnp.concatenate([back[32 * b : 32 * b + 32] for b in range(2 * kernels)], 1)
    u = table_dot(agt3, wide)
    first, second = [], []
    for j in range(2):
        f = s = None
        for k in range(kernels):
            at = 128 * (j * kernels + k)
            u1, u2 = u[:16, at : at + 128], u[16:, at : at + 128]
            a = hrr[k] * u1 - hii[k] * u2
            b = hrr[k] * u2 + hii[k] * u1
            f = a if f is None else f + a
            s = b if s is None else s + b
        first.append(f)
        second.append(s)
    return jnp.concatenate(first, 0), jnp.concatenate(second, 0)


def project(total, row_tab, col_hi, col_lo, sign):
    it = times_i(total, sign)
    lhs = jnp.concatenate([total[:16], it[:16], total[16:], it[16:]], 0)
    hi, lo = split(lhs)
    q = dot(jnp.concatenate([hi, lo, hi], 1), jnp.concatenate([col_hi, col_hi, col_lo], 0))
    return [jnp.sum(q[32 * j : 32 * j + 32] * row_tab, axis=0, keepdims=True) for j in range(2)]


def kernel(
    weights_hbm,
    counts_hbm,
    rows_hbm,
    cols_hbm,
    step_hbm,
    spectra_hbm,
    tabs_hbm,
    consts_hbm,
    mask_hbm,
    target_hbm,
    fwd_hbm,
    up_hbm,
    down_hbm,
    out_ref,
    weights_s,
    counts_s,
    rows_v,
    cols_v,
    step_v,
    spectra_v,
    tabs_v,
    consts_v,
    mask_v,
    target_v,
    fwd_v,
    up_v,
    down_v,
    h_v,
    e0_v,
    m_own,
    m_got,
    y_own,
    y_got,
    hrr_v,
    hii_v,
    res_v,
    load_sem,
    h_send,
    h_recv,
    m_send,
    m_recv,
    y_send,
    y_recv,
    res_send,
    res_recv,
):
    tile = lax.axis_index("tile")
    kern = lax.axis_index("kern")
    lead = 3 - 2 * lax.rem(tile, 2)
    is_lead = kern == lead
    others = [{"tile": tile, "kern": lax.rem(lead + d, KERN)} for d in (1, 2, 3)]
    sides = (
        (tile > 0, {"tile": lax.max(tile - 1, 0), "kern": 4 - lead}),
        (tile < TILES - 1, {"tile": lax.min(tile + 1, TILES - 1), "kern": 4 - lead}),
    )
    barrier = pltpu.get_barrier_semaphore()
    used = []

    def load(src, dst):
        copy = pltpu.make_async_copy(src, dst, load_sem.at[len(used)])
        used.append(copy)
        return copy

    early = [load(weights_hbm, weights_s), load(spectra_hbm, spectra_v)]
    mine = pl.multiple_of(kern * LOCAL, LOCAL)

    def scale_own():
        for copy in early:
            copy.wait()
        for k in range(LOCAL):
            scale = jnp.sqrt(jnp.full((ROW_FREQS, 128), weights_s[k] * (2.0 / KERNELS), F32))
            h_v[mine + k] = spectra_v[k] * scale

    @pl.when(jnp.logical_not(is_lead))
    def _():
        lead_device = {"tile": tile, "kern": lead}
        pl.semaphore_signal(barrier, inc=1, device_id=lead_device, device_id_type=MESH)
        for copy in early:
            copy.start()
        scale_own()
        pl.semaphore_wait(barrier, 1)
        place = lax.rem(kern - lead + KERN, KERN) - 1
        copy = pltpu.make_async_remote_copy(
            src_ref=h_v.at[pl.ds(mine, LOCAL)],
            dst_ref=h_v.at[pl.ds(mine, LOCAL)],
            send_sem=h_send.at[0],
            recv_sem=h_recv.at[place],
            device_id=lead_device,
            device_id_type=MESH,
        )
        copy.start()
        copy.wait_send()
        pltpu.make_async_remote_copy(
            src_ref=res_v,
            dst_ref=res_v,
            send_sem=res_send.at[0],
            recv_sem=res_recv.at[0],
            device_id=lead_device,
            device_id_type=MESH,
        ).wait_recv()

    @pl.when(is_lead)
    def _():
        for d, (exists, _) in enumerate(sides):

            @pl.when(jnp.logical_not(exists))
            def _():
                m_got[1 - d] = jnp.zeros((32, 128), F32)
                y_got[1 - d] = jnp.zeros((32, 128), F32)

        for exists, device in sides:

            @pl.when(exists)
            def _():
                pl.semaphore_signal(barrier, inc=1, device_id=device, device_id_type=MESH)

        for device in others:
            pl.semaphore_signal(barrier, inc=1, device_id=device, device_id_type=MESH)

        width = WIDTH // CHUNKS
        small = [
            load(a, b)
            for a, b in (
                (counts_hbm, counts_s),
                (rows_hbm, rows_v),
                (cols_hbm, cols_v),
                (step_hbm, step_v),
                (consts_hbm, consts_v),
                (tabs_hbm, tabs_v),
            )
        ]
        parts = [pl.ds(c * width, width) for c in range(CHUNKS)]
        mask_copies = [load(mask_hbm.at[:, p], mask_v.at[:, p]) for p in parts]
        fwd_copies = [load(fwd_hbm.at[p, :], fwd_v.at[p, :]) for p in parts]
        later = [load(up_hbm, up_v), load(target_hbm, target_v), load(down_hbm, down_v)]
        for a, b in zip(mask_copies, fwd_copies):
            a.start()
            b.start()
        for copy in early + small + later:
            copy.start()

        for copy in small:
            copy.wait()
        sign = lane_sign((32, 128))
        cr, ci = consts_v[0:32], consts_v[32:64]
        dsc = consts_v[64:192]
        row_tab, col_tab = fragment_tables(rows_v[...], cols_v[...], jnp.concatenate([dsc, dsc], 1))
        col_hi, col_lo = split(col_tab)
        active = lax.broadcasted_iota(jnp.int32, (1, SLOTS), 1) < counts_s[0]
        amp = jnp.where(active, step_v[...], 0.0) * (1.0 / math.sqrt(FRAG_LEN))

        total = jnp.zeros((2 * SLAB, 256), F32)
        for c in range(CHUNKS):
            mask_copies[c].wait()
            fwd_copies[c].wait()
            hi, lo = split(mask_v[:, c * width : (c + 1) * width])
            total += dot(jnp.concatenate([hi, lo], 0), fwd_v[c * width : (c + 1) * width, :])
        packed = total[:SLAB, :128] + total[:SLAB, 128:] + total[SLAB:, :128]
        modes_own = own_modes(packed, row_tab, col_hi, col_lo, amp, tabs_v[640:672, :192], sign)
        m_own[...] = modes_own

        def exchange(own, got, send, recv):
            copies = [
                pltpu.make_async_remote_copy(
                    src_ref=own,
                    dst_ref=got.at[d],
                    send_sem=send.at[d],
                    recv_sem=recv.at[d],
                    device_id=device,
                    device_id_type=MESH,
                )
                for d, (_, device) in enumerate(sides)
            ]
            for d, (exists, _) in enumerate(sides):

                @pl.when(exists)
                def _():
                    copies[d].start()

            return copies

        def arrived(copies):
            for d, (exists, _) in enumerate(sides):

                @pl.when(exists)
                def _():
                    copies[1 - d].wait_recv()

        def sent(copies):
            for d, (exists, _) in enumerate(sides):

                @pl.when(exists)
                def _():
                    copies[d].wait_send()

        pl.semaphore_wait(barrier, 3 + lax.min(tile, 1) + lax.min(TILES - 1 - tile, 1))
        m_copies = exchange(m_own, m_got, m_send, m_recv)

        scale_own()
        low = lax.broadcasted_iota(jnp.int32, (ROW_FREQS, 128), 1) < 64
        for d in range(KERN):
            at = pl.multiple_of(lax.rem(lead + d, KERN) * LOCAL, LOCAL)
            if d > 0:
                pltpu.make_async_remote_copy(
                    src_ref=h_v.at[pl.ds(at, LOCAL)],
                    dst_ref=h_v.at[pl.ds(at, LOCAL)],
                    send_sem=h_send.at[0],
                    recv_sem=h_recv.at[d - 1],
                    device_id=others[0],
                    device_id_type=MESH,
                ).wait_recv()
            for k in range(LOCAL):
                a, b = two_forms(h_v[at + k], low)
                hrr_v[d * LOCAL + k] = a
                hii_v[d * LOCAL + k] = b

        def forms(g):
            ks = range(g * LOCAL, (g + 1) * LOCAL)
            return [hrr_v[k] for k in ks], [hii_v[k] for k in ks]

        for copy in later:
            copy.wait()
        arrived(m_copies)
        modes = combine(modes_own, m_got[1], m_got[0], cr, ci, sign)
        imodes = times_i(modes, sign)

        inten = change = None
        for g in range(KERN):
            hrr, hii = forms(g)
            e0, e1 = forward_group(hrr, hii, modes, imodes, tabs_v[672:704, :96], tabs_v[0:384, :])
            e0_v[g] = e0
            s0, s1 = intensity_terms(e0, e1, LOCAL)
            inten = s0 if inten is None else inten + s0
            change = s1 if change is None else change + s1

        grids = table_dot(tabs_v[736:800, :96], jnp.concatenate([0.5 * inten, change], 1))
        hi, lo = split(jnp.concatenate([grids[:, :128], grids[:, 128:]], 0))
        rows3 = jnp.concatenate([hi, lo, hi], 1)
        span = 256
        total = jnp.zeros((4 * SLAB, 256), F32)
        for c in range(WIDTH // span):
            part = slice(c * span, (c + 1) * span)
            full = dot(rows3, up_v[:, part])
            w0, w1 = weighting(full[:SLAB], full[SLAB:], target_v[:, part])
            hi, lo = split(jnp.concatenate([w0, w1], 0))
            total += dot(jnp.concatenate([hi, lo], 0), down_v[part, :])
        n = 2 * SLAB
        cols = total[:n, :128] + total[:n, 128:] + total[n:, :128]
        wgrid = table_dot(tabs_v[800:832, :192], jnp.concatenate([cols[:SLAB], cols[SLAB:]], 1))
        w0, w1 = wgrid[:, :128], wgrid[:, 128:]

        first = second = None
        for g in range(KERN):
            hrr, hii = forms(g)
            a, b = adjoint_group(
                e0_v[g], w0, w1, LOCAL, hrr, hii, tabs_v[384:640, :], tabs_v[704:736, :96]
            )
            first = a if first is None else first + a
            second = b if second is None else second + b
        spectrum = first - times_i(second, sign)
        y_own[...] = spectrum

        y_copies = exchange(y_own, y_got, y_send, y_recv)
        arrived(y_copies)
        whole = combine(spectrum, y_got[1], y_got[0], cr, ci, sign)
        outs = project(whole, row_tab, col_hi, col_lo, sign)
        for j in range(2):
            res_v[j : j + 1, :] = jnp.where(active, outs[j] * (1.0 / math.sqrt(FRAG_LEN)), 0.0)

        res_copies = [
            pltpu.make_async_remote_copy(
                src_ref=res_v,
                dst_ref=res_v,
                send_sem=res_send.at[d],
                recv_sem=res_recv.at[0],
                device_id=device,
                device_id_type=MESH,
            )
            for d, device in enumerate(others)
        ]
        for copy in res_copies:
            copy.start()
        sent(m_copies)
        sent(y_copies)
        for copy in res_copies:
            copy.wait_send()

    out_ref[...] = res_v[...]


def shards(mask, target, spectra, weights, counts, frag_rows, frag_cols, step):
    fwd, up, down, tabs, consts = make_tables()
    vmem = pl.BlockSpec(memory_space=pltpu.VMEM)
    hbm = pl.BlockSpec(memory_space=pltpu.HBM)
    dma = pltpu.SemaphoreType.DMA
    outs = pl.pallas_call(
        kernel,
        out_shape=pltpu.VMEM((2, SLOTS), F32),
        in_specs=[hbm] * 13,
        out_specs=vmem,
        scratch_shapes=[
            pltpu.SMEM((LOCAL,), F32),
            pltpu.SMEM((1,), jnp.int32),
            pltpu.VMEM((1, SLOTS), jnp.int32),
            pltpu.VMEM((1, SLOTS), jnp.int32),
            pltpu.VMEM((1, SLOTS), F32),
            pltpu.VMEM((LOCAL, ROW_FREQS, 128), F32),
            pltpu.VMEM(tabs.shape, BF16),
            pltpu.VMEM(consts.shape, F32),
            pltpu.VMEM((SLAB, WIDTH), F32),
            pltpu.VMEM((SLAB, WIDTH), F32),
            pltpu.VMEM((WIDTH, 256), BF16),
            pltpu.VMEM((384, WIDTH), BF16),
            pltpu.VMEM((WIDTH, 256), BF16),
            pltpu.VMEM((KERNELS, ROW_FREQS, 128), F32),
            pltpu.VMEM((KERN, LOCAL * GRID_ROWS, 256), F32),
            pltpu.VMEM((32, 128), F32),
            pltpu.VMEM((2, 32, 128), F32),
            pltpu.VMEM((32, 128), F32),
            pltpu.VMEM((2, 32, 128), F32),
            pltpu.VMEM((KERNELS, ROW_FREQS, 128), F32),
            pltpu.VMEM((KERNELS, ROW_FREQS, 128), F32),
            pltpu.VMEM((2, SLOTS), F32),
            dma((2 * CHUNKS + 11,)),
            dma((1,)),
            dma((3,)),
            dma((2,)),
            dma((2,)),
            dma((2,)),
            dma((2,)),
            dma((3,)),
            dma((1,)),
        ],
        compiler_params=pltpu.CompilerParams(
            collective_id=0, has_side_effects=True, vmem_limit_bytes=60 * 1024 * 1024
        ),
    )(
        weights,
        counts,
        frag_rows.reshape(1, SLOTS),
        frag_cols.reshape(1, SLOTS),
        step.reshape(1, SLOTS),
        spectra,
        jnp.asarray(tabs),
        jnp.asarray(consts),
        mask,
        target,
        jnp.asarray(fwd),
        jnp.asarray(up),
        jnp.asarray(down),
    )
    return outs[0], outs[1]


def solution(mesh):
    return jax.shard_map(
        shards,
        mesh=mesh,
        in_specs=(
            P("tile", None),
            P("tile", None),
            P("kern", None, None),
            P("kern"),
            P("tile"),
            P("tile"),
            P("tile"),
            P("tile"),
        ),
        out_specs=(P("tile"), P("tile")),
        check_vma=False,
    )
```

```python
import functools
import math

import jax
import jax.numpy as jnp
import ml_dtypes
import numpy as np
from jax import lax
from jax.experimental import pallas as pl
from jax.experimental.pallas import tpu as pltpu
from jax.sharding import PartitionSpec as P

WIDTH = 2048
COL_FREQS = 64
ROW_FREQS = 16
KERNELS = 24
FRAG_LEN = 32
SLAB = 64
SLOTS = 256
EXT = 192
TILES = 64
KERN = 4
LOCAL = KERNELS // KERN
GRID_ROWS = 32
GRID_COLS = 128
STEEP = 10.0
THRESH = 0.1
F32 = jnp.float32
BF16 = jnp.bfloat16
CHUNKS = 4
GROUP = 12
PLANE = 16
MESH = pl.DeviceIdType.MESH


def np_split(x):
    hi = x.astype(np.float32).astype(ml_dtypes.bfloat16)
    lo = (x - hi.astype(np.float64)).astype(np.float32).astype(ml_dtypes.bfloat16)
    return hi, lo


def pad_lanes(x, lanes=256):
    return np.pad(x, ((0, 0), (0, lanes - x.shape[1])))


@functools.lru_cache(maxsize=None)
def make_tables():
    kc = np.arange(COL_FREQS) - COL_FREQS // 2
    kr = np.arange(ROW_FREQS) - ROW_FREQS // 2
    x = np.arange(WIDTH)
    ang = 2 * np.pi * (np.outer(x, kc) % WIDTH) / WIDTH
    f_hi, f_lo = np_split(np.concatenate([np.cos(ang), -np.sin(ang)], 1) / math.sqrt(WIDTH))
    fwd = np.concatenate([f_hi, f_lo], 1)

    n = np.arange(GRID_COLS)
    step = WIDTH // GRID_COLS
    dist = (x[None, :] - step * n[:, None]) % WIDTH
    base = np.ones(WIDTH)
    for kap in range(1, COL_FREQS):
        base += 2 * np.cos(2 * np.pi * ((np.arange(WIDTH) * kap) % WIDTH) / WIDTH)
    g = (base / GRID_COLS)[dist]
    g_hi, g_lo = np_split(g)
    up = np.concatenate([g_hi, g_hi, g_lo], 0)
    gt_hi, gt_lo = np_split(g.T)
    down = np.concatenate([gt_hi, gt_lo], 1)

    ang = 2 * np.pi * (np.outer(kc, n) % GRID_COLS) / GRID_COLS
    c, s = np.cos(ang) / math.sqrt(WIDTH), np.sin(ang) / math.sqrt(WIDTH)
    inv = np.block([[c, s], [-s, c]])
    i_hi, i_lo = np_split(inv)
    inv3 = np.concatenate([i_hi, i_hi, i_lo], 0)
    t_hi, t_lo = np_split(inv.T)
    adj = np.concatenate([t_hi, t_lo], 1)

    e = np.arange(SLAB)
    ang = 2 * np.pi * (np.outer(kr, e) % EXT) / EXT
    a_hi, a_lo = np_split(np.concatenate([np.cos(ang), np.sin(ang)], 0) / math.sqrt(EXT))
    lt3 = np.concatenate([a_hi, a_hi, a_lo], 1)

    m = np.arange(GRID_ROWS)
    ang = 2 * np.pi * (np.outer(m, kr) % GRID_ROWS) / GRID_ROWS
    c, s = np.cos(ang) / math.sqrt(EXT), np.sin(ang) / math.sqrt(EXT)
    ag = np.block([[c, -s], [s, c]])
    hi, lo = np_split(ag)
    ag3 = np.concatenate([hi, hi, lo], 1)
    hi, lo = np_split(ag.T)
    agt3 = np.concatenate([hi, hi, lo], 1)

    rstep = EXT // GRID_ROWS
    dist = (e[:, None] - rstep * m[None, :]) % EXT
    base = np.ones(EXT)
    for rho in range(1, ROW_FREQS):
        base += 2 * np.cos(2 * np.pi * ((np.arange(EXT) * rho) % EXT) / EXT)
    r = (base / GRID_ROWS)[dist]
    hi, lo = np_split(r)
    r3 = np.concatenate([hi, hi, lo], 1)
    hi, lo = np_split(r.T)
    rt3 = np.concatenate([hi, hi, lo], 1)

    tabs = np.concatenate(
        [inv3, adj, pad_lanes(lt3), pad_lanes(ag3), pad_lanes(agt3), pad_lanes(r3), pad_lanes(rt3)], 0
    )

    ang = 2 * np.pi * (kr % 3) / 3
    cr = np.tile(np.cos(ang), 2)
    ci = np.tile(np.sin(ang), 2)
    with np.errstate(invalid="ignore"):
        d = np.where(kc == 0, FRAG_LEN, np.sin(np.pi * FRAG_LEN * kc / WIDTH) / np.sin(np.pi * kc / WIDTH))
    d = d / math.sqrt(WIDTH)
    col = np.concatenate([cr, ci, d, -d])
    consts = np.repeat(col[:, None], 128, 1).astype(np.float32)
    return fwd, up, down, tabs, consts


def split(x):
    hi = x.astype(BF16)
    return hi, (x - hi.astype(F32)).astype(BF16)


def dot(a, b):
    return lax.dot_general(a, b, (((1,), (0,)), ((), ())), preferred_element_type=F32)


def dot_nt(a, b):
    return lax.dot_general(a, b, (((1,), (1,)), ((), ())), preferred_element_type=F32)


def table_dot(table3, x):
    hi, lo = split(x)
    return dot(table3, jnp.concatenate([hi, lo, hi], 0))


def sin_turns(u):
    y = u * (2.0 * math.pi)
    s = y * y
    p = jnp.full_like(s, -1.0 / 39916800.0)
    for coef in (1.0 / 362880.0, -1.0 / 5040.0, 1.0 / 120.0, -1.0 / 6.0):
        p = p * s + coef
    return y + y * (s * p)


def cos_turns(t):
    t = t - jnp.floor(t + 0.5)
    return sin_turns(0.25 - jnp.abs(t))


def times_i(z, sign):
    return pltpu.roll(z, 64, axis=1) * sign


def lane_sign(shape):
    lane = lax.broadcasted_iota(jnp.int32, shape, 1)
    return jnp.where(lane < 64, -1.0, 1.0).astype(F32)


def fragment_tables(rows, cols, dsc):
    kr = lax.broadcasted_iota(jnp.int32, (32, SLOTS), 0)
    is_sin = kr >= 16
    kr = ((kr & 15) - 8).astype(F32)
    t = kr * rows.astype(F32) * (1.0 / EXT)
    row_tab = cos_turns(t - jnp.where(is_sin, 0.25, 0.0)) * (1.0 / math.sqrt(EXT))
    kc = lax.broadcasted_iota(jnp.int32, (128, SLOTS), 0)
    is_sin = kc >= 64
    kc = ((kc & 63) - 32).astype(F32)
    t = kc * (2 * cols + (FRAG_LEN - 1)).astype(F32) * (1.0 / (2 * WIDTH))
    col_tab = cos_turns(t - jnp.where(is_sin, 0.25, 0.0)) * dsc
    return row_tab, col_tab


def own_modes(packed, row_tab, col_hi, col_lo, amp, lt3, sign):
    u0 = table_dot(lt3, packed)
    hi, lo = split(row_tab * amp)
    u1 = dot_nt(
        jnp.concatenate([hi, lo, hi], 1), jnp.concatenate([col_hi, col_hi, col_lo], 1)
    )
    u_re = jnp.concatenate([u0[:16], u1[:16]], 0)
    u_im = jnp.concatenate([u0[16:], u1[16:]], 0)
    return u_re - times_i(u_im, sign)


def combine(own, left, right, cr, ci, sign):
    return own + cr * (left + right) + ci * times_i(left - right, sign)


def two_forms(h, low):
    turned = pltpu.roll(h, 64, axis=1)
    return jnp.where(low, h, turned), jnp.where(low, turned, h)


def side_by_side(x, rows):
    return jnp.concatenate([x[i : i + rows] for i in range(0, x.shape[0], rows)], 1)


def forward_group(hrr, hii, modes, imodes, inv3, ag3):
    blocks = []
    for j in range(2):
        m, im = modes[16 * j : 16 * j + 16], imodes[16 * j : 16 * j + 16]
        blocks += [a * m + b * im for a, b in zip(hrr, hii)]
    hi, lo = split(jnp.concatenate(blocks, 0))
    q = dot(jnp.concatenate([hi, lo, hi], 1), inv3)
    q_re, q_im = side_by_side(q[:, :128], 16), side_by_side(q[:, 128:], 16)
    return table_dot(ag3, jnp.concatenate([q_re, q_im], 0))


def intensity_terms(amps, kernels):
    total0 = total1 = None
    for k in range(kernels):
        a, b = amps[:, 128 * k : 128 * k + 128], amps[:, 128 * (kernels + k) : 128 * (kernels + k) + 128]
        s0, s1 = a * a, a * b
        total0 = s0 if total0 is None else total0 + s0
        total1 = s1 if total1 is None else total1 + s1
    return total0[:32] + total0[32:], total1[:32] + total1[32:]


def weighting(inten, change, target):
    developed = 1.0 / (1.0 + jnp.exp(-STEEP * (inten - THRESH)))
    steep = STEEP * developed * (1.0 - developed)
    return steep * (developed - target), steep * steep * change


def adjoint_group(e0, w0, w1, hrr, hii, adj, agt3):
    kernels = len(hrr)
    loads = []
    for w in (w0, w1):
        ww = jnp.concatenate([w, w], 0)
        loads += [ww * e0[:, 128 * k : 128 * k + 128] for k in range(kernels)]
    u = table_dot(agt3, jnp.concatenate(loads, 1))
    rows = [
        jnp.concatenate([u[:16, 128 * b : 128 * b + 128], u[16:, 128 * b : 128 * b + 128]], 1)
        for b in range(2 * kernels)
    ]
    hi, lo = split(jnp.concatenate(rows, 0))
    both = dot(hi, adj)
    back = both[:, :128] + both[:, 128:] + dot(lo, adj[:, :128])
    first, second = [], []
    for j in range(2):
        f = s = None
        for k in range(kernels):
            at = 16 * (j * kernels + k)
            a, b = hrr[k] * back[at : at + 16], hii[k] * back[at : at + 16]
            f = a if f is None else f + a
            s = b if s is None else s + b
        first.append(f)
        second.append(s)
    return jnp.concatenate(first, 0), jnp.concatenate(second, 0)


def project(total, row_tab, col_hi, col_lo, sign):
    it = times_i(total, sign)
    lhs = jnp.concatenate([total[:16], it[:16], total[16:], it[16:]], 0)
    hi, lo = split(lhs)
    q = dot(jnp.concatenate([hi, lo, hi], 1), jnp.concatenate([col_hi, col_hi, col_lo], 0))
    return [jnp.sum(q[32 * j : 32 * j + 32] * row_tab, axis=0, keepdims=True) for j in range(2)]


def kernel(
    weights_hbm,
    counts_hbm,
    rows_hbm,
    cols_hbm,
    step_hbm,
    spectra_hbm,
    tabs_hbm,
    consts_hbm,
    mask_hbm,
    target_hbm,
    fwd_hbm,
    up_hbm,
    down_hbm,
    out_ref,
    weights_s,
    counts_s,
    rows_v,
    cols_v,
    step_v,
    spectra_v,
    tabs_v,
    consts_v,
    mask_v,
    target_v,
    fwd_v,
    up_v,
    down_v,
    h_v,
    e0_v,
    m_own,
    m_got,
    y_own,
    y_got,
    hrr_v,
    hii_v,
    res_v,
    load_sem,
    h_send,
    h_recv,
    m_send,
    m_recv,
    y_send,
    y_recv,
    res_send,
    res_recv,
):
    tile = lax.axis_index("tile")
    kern = lax.axis_index("kern")
    lead = 3 - 2 * lax.rem(tile, 2)
    is_lead = kern == lead
    others = [{"tile": tile, "kern": lax.rem(lead + d, KERN)} for d in (1, 2, 3)]
    sides = (
        (tile > 0, {"tile": lax.max(tile - 1, 0), "kern": 4 - lead}),
        (tile < TILES - 1, {"tile": lax.min(tile + 1, TILES - 1), "kern": 4 - lead}),
    )
    first = 1 - lax.min(lax.rem(tile, PLANE), 1)
    left_of_modes = {
        "tile": lax.max(tile - 1 - (PLANE - 2) * first, 0),
        "kern": (4 - lead) * (1 - first),
    }
    is_last = jnp.logical_and(lax.rem(tile, PLANE) == PLANE - 1, tile < TILES - 1)
    is_depot = jnp.logical_and(
        kern == 0, jnp.logical_and(lax.rem(tile, PLANE) == 1, tile < TILES - PLANE)
    )
    barrier = pltpu.get_barrier_semaphore()
    used = []

    def load(src, dst):
        copy = pltpu.make_async_copy(src, dst, load_sem.at[len(used)])
        used.append(copy)
        return copy

    early = [load(weights_hbm, weights_s), load(spectra_hbm, spectra_v)]
    mine = pl.multiple_of(kern * LOCAL, LOCAL)

    def scale_own():
        for copy in early:
            copy.wait()
        for k in range(LOCAL):
            scale = jnp.sqrt(jnp.full((ROW_FREQS, 128), weights_s[k] * (2.0 / KERNELS), F32))
            h_v[mine + k] = spectra_v[k] * scale

    @pl.when(jnp.logical_not(is_lead))
    def _():
        lead_device = {"tile": tile, "kern": lead}

        @pl.when(is_depot)
        def _():
            pl.semaphore_signal(
                barrier,
                inc=1,
                device_id={"tile": lax.min(tile + PLANE - 1, TILES - 1), "kern": 3},
                device_id_type=MESH,
            )

        for copy in early:
            copy.start()
        scale_own()
        pl.semaphore_wait(barrier, 1 + is_depot.astype(jnp.int32))

        @pl.when(is_depot)
        def _():
            copy = pltpu.make_async_remote_copy(
                src_ref=m_got.at[0],
                dst_ref=m_got.at[0],
                send_sem=m_send.at[0],
                recv_sem=m_recv.at[0],
                device_id={"tile": lax.min(tile + PLANE - 2, TILES - 1), "kern": 1},
                device_id_type=MESH,
            )
            copy.wait_recv()
            copy.start()
            copy.wait_send()

        place = lax.rem(kern - lead + KERN, KERN) - 1
        copy = pltpu.make_async_remote_copy(
            src_ref=h_v.at[pl.ds(mine, LOCAL)],
            dst_ref=h_v.at[pl.ds(mine, LOCAL)],
            send_sem=h_send.at[0],
            recv_sem=h_recv.at[place],
            device_id=lead_device,
            device_id_type=MESH,
        )
        copy.start()
        copy.wait_send()
        pltpu.make_async_remote_copy(
            src_ref=res_v,
            dst_ref=res_v,
            send_sem=res_send.at[0],
            recv_sem=res_recv.at[0],
            device_id=lead_device,
            device_id_type=MESH,
        ).wait_recv()

    @pl.when(is_lead)
    def _():
        for d, (exists, _) in enumerate(sides):

            @pl.when(jnp.logical_not(exists))
            def _():
                m_got[1 - d] = jnp.zeros((32, 128), F32)
                y_got[1 - d] = jnp.zeros((32, 128), F32)

        @pl.when(is_last)
        def _():
            pl.semaphore_signal(
                barrier,
                inc=1,
                device_id={"tile": lax.max(tile - (PLANE - 2), 0), "kern": 0},
                device_id_type=MESH,
            )

        for exists, device in (sides[0], (jnp.logical_and(sides[1][0], jnp.logical_not(is_last)), sides[1][1])):

            @pl.when(exists)
            def _():
                pl.semaphore_signal(barrier, inc=1, device_id=device, device_id_type=MESH)

        for device in others:
            pl.semaphore_signal(barrier, inc=1, device_id=device, device_id_type=MESH)

        width = WIDTH // CHUNKS
        small = [
            load(a, b)
            for a, b in (
                (counts_hbm, counts_s),
                (rows_hbm, rows_v),
                (cols_hbm, cols_v),
                (step_hbm, step_v),
                (consts_hbm, consts_v),
                (tabs_hbm, tabs_v),
            )
        ]
        parts = [pl.ds(c * width, width) for c in range(CHUNKS)]
        mask_copies = [load(mask_hbm.at[:, p], mask_v.at[:, p]) for p in parts]
        fwd_copies = [load(fwd_hbm.at[p, :], fwd_v.at[p, :]) for p in parts]
        later = [load(up_hbm, up_v), load(target_hbm, target_v), load(down_hbm, down_v)]
        for a, b in zip(mask_copies, fwd_copies):
            a.start()
            b.start()
        for copy in early + small + later:
            copy.start()

        for copy in small:
            copy.wait()
        sign = lane_sign((32, 128))
        cr, ci = consts_v[0:32], consts_v[32:64]
        dsc = consts_v[64:192]
        row_tab, col_tab = fragment_tables(rows_v[...], cols_v[...], jnp.concatenate([dsc, dsc], 1))
        col_hi, col_lo = split(col_tab)
        active = lax.broadcasted_iota(jnp.int32, (1, SLOTS), 1) < counts_s[0]
        amp = jnp.where(active, step_v[...], 0.0) * (1.0 / math.sqrt(FRAG_LEN))

        total = jnp.zeros((2 * SLAB, 256), F32)
        for c in range(CHUNKS):
            mask_copies[c].wait()
            fwd_copies[c].wait()
            hi, lo = split(mask_v[:, c * width : (c + 1) * width])
            total += dot(jnp.concatenate([hi, lo], 0), fwd_v[c * width : (c + 1) * width, :])
        packed = total[:SLAB, :128] + total[:SLAB, 128:] + total[SLAB:, :128]
        modes_own = own_modes(packed, row_tab, col_hi, col_lo, amp, tabs_v[640:672, :192], sign)
        m_own[...] = modes_own

        def exchange(own, got, send, recv, devices):
            copies = [
                pltpu.make_async_remote_copy(
                    src_ref=own,
                    dst_ref=got.at[d],
                    send_sem=send.at[d],
                    recv_sem=recv.at[d],
                    device_id=device,
                    device_id_type=MESH,
                )
                for d, device in enumerate(devices)
            ]
            for d, (exists, _) in enumerate(sides):

                @pl.when(exists)
                def _():
                    copies[d].start()

            return copies

        def arrived(copies):
            for d, (exists, _) in enumerate(sides):

                @pl.when(exists)
                def _():
                    copies[1 - d].wait_recv()

        def sent(copies):
            for d, (exists, _) in enumerate(sides):

                @pl.when(exists)
                def _():
                    copies[d].wait_send()

        pl.semaphore_wait(barrier, lax.min(tile, 1) + lax.min(TILES - 1 - tile, 1))
        m_copies = exchange(m_own, m_got, m_send, m_recv, (left_of_modes, sides[1][1]))

        scale_own()
        low = lax.broadcasted_iota(jnp.int32, (ROW_FREQS, 128), 1) < 64
        for d in range(KERN):
            at = pl.multiple_of(lax.rem(lead + d, KERN) * LOCAL, LOCAL)
            if d > 0:
                pltpu.make_async_remote_copy(
                    src_ref=h_v.at[pl.ds(at, LOCAL)],
                    dst_ref=h_v.at[pl.ds(at, LOCAL)],
                    send_sem=h_send.at[0],
                    recv_sem=h_recv.at[d - 1],
                    device_id=others[0],
                    device_id_type=MESH,
                ).wait_recv()
            for k in range(LOCAL):
                a, b = two_forms(h_v[at + k], low)
                hrr_v[d * LOCAL + k] = a
                hii_v[d * LOCAL + k] = b

        def forms(g):
            ks = range(g * GROUP, (g + 1) * GROUP)
            return [hrr_v[k] for k in ks], [hii_v[k] for k in ks]

        for copy in later:
            copy.wait()
        arrived(m_copies)
        modes = combine(modes_own, m_got[1], m_got[0], cr, ci, sign)
        imodes = times_i(modes, sign)

        inten = change = None
        for g in range(KERNELS // GROUP):
            hrr, hii = forms(g)
            amps = forward_group(hrr, hii, modes, imodes, tabs_v[0:384, :], tabs_v[672:736, :96])
            e0_v[g] = amps[:, : 128 * GROUP]
            s0, s1 = intensity_terms(amps, GROUP)
            inten = s0 if inten is None else inten + s0
            change = s1 if change is None else change + s1

        grids = table_dot(tabs_v[768:832, :96], jnp.concatenate([0.5 * inten, change], 1))
        hi, lo = split(jnp.concatenate([grids[:, :128], grids[:, 128:]], 0))
        rows3 = jnp.concatenate([hi, lo, hi], 1)
        span = 256
        total = jnp.zeros((4 * SLAB, 256), F32)
        for c in range(WIDTH // span):
            part = slice(c * span, (c + 1) * span)
            full = dot(rows3, up_v[:, part])
            w0, w1 = weighting(full[:SLAB], full[SLAB:], target_v[:, part])
            hi, lo = split(jnp.concatenate([w0, w1], 0))
            total += dot(jnp.concatenate([hi, lo], 0), down_v[part, :])
        n = 2 * SLAB
        cols = total[:n, :128] + total[:n, 128:] + total[n:, :128]
        wgrid = table_dot(tabs_v[832:864, :192], jnp.concatenate([cols[:SLAB], cols[SLAB:]], 1))
        w0, w1 = wgrid[:, :128], wgrid[:, 128:]

        first = second = None
        for g in range(KERNELS // GROUP):
            hrr, hii = forms(g)
            a, b = adjoint_group(
                e0_v[g], w0, w1, hrr, hii, tabs_v[384:640, :], tabs_v[736:768, :192]
            )
            first = a if first is None else first + a
            second = b if second is None else second + b
        spectrum = first - times_i(second, sign)
        y_own[...] = spectrum

        y_copies = exchange(y_own, y_got, y_send, y_recv, (sides[0][1], sides[1][1]))
        arrived(y_copies)
        whole = combine(spectrum, y_got[1], y_got[0], cr, ci, sign)
        outs = project(whole, row_tab, col_hi, col_lo, sign)
        for j in range(2):
            res_v[j : j + 1, :] = jnp.where(active, outs[j] * (1.0 / math.sqrt(FRAG_LEN)), 0.0)

        res_copies = [
            pltpu.make_async_remote_copy(
                src_ref=res_v,
                dst_ref=res_v,
                send_sem=res_send.at[d],
                recv_sem=res_recv.at[0],
                device_id=device,
                device_id_type=MESH,
            )
            for d, device in enumerate(others)
        ]
        for d in (1, 0, 2):
            res_copies[d].start()
        sent(m_copies)
        sent(y_copies)
        for copy in res_copies:
            copy.wait_send()

    out_ref[...] = res_v[...]


def shards(mask, target, spectra, weights, counts, frag_rows, frag_cols, step):
    fwd, up, down, tabs, consts = make_tables()
    vmem = pl.BlockSpec(memory_space=pltpu.VMEM)
    hbm = pl.BlockSpec(memory_space=pltpu.HBM)
    dma = pltpu.SemaphoreType.DMA
    outs = pl.pallas_call(
        kernel,
        out_shape=pltpu.VMEM((2, SLOTS), F32),
        in_specs=[hbm] * 13,
        out_specs=vmem,
        scratch_shapes=[
            pltpu.SMEM((LOCAL,), F32),
            pltpu.SMEM((1,), jnp.int32),
            pltpu.VMEM((1, SLOTS), jnp.int32),
            pltpu.VMEM((1, SLOTS), jnp.int32),
            pltpu.VMEM((1, SLOTS), F32),
            pltpu.VMEM((LOCAL, ROW_FREQS, 128), F32),
            pltpu.VMEM(tabs.shape, BF16),
            pltpu.VMEM(consts.shape, F32),
            pltpu.VMEM((SLAB, WIDTH), F32),
            pltpu.VMEM((SLAB, WIDTH), F32),
            pltpu.VMEM((WIDTH, 256), BF16),
            pltpu.VMEM((384, WIDTH), BF16),
            pltpu.VMEM((WIDTH, 256), BF16),
            pltpu.VMEM((KERNELS, ROW_FREQS, 128), F32),
            pltpu.VMEM((KERNELS // GROUP, 2 * GRID_ROWS, 128 * GROUP), F32),
            pltpu.VMEM((32, 128), F32),
            pltpu.VMEM((2, 32, 128), F32),
            pltpu.VMEM((32, 128), F32),
            pltpu.VMEM((2, 32, 128), F32),
            pltpu.VMEM((KERNELS, ROW_FREQS, 128), F32),
            pltpu.VMEM((KERNELS, ROW_FREQS, 128), F32),
            pltpu.VMEM((2, SLOTS), F32),
            dma((2 * CHUNKS + 11,)),
            dma((1,)),
            dma((3,)),
            dma((2,)),
            dma((2,)),
            dma((2,)),
            dma((2,)),
            dma((3,)),
            dma((1,)),
        ],
        compiler_params=pltpu.CompilerParams(
            collective_id=0, has_side_effects=True, vmem_limit_bytes=60 * 1024 * 1024
        ),
    )(
        weights,
        counts,
        frag_rows.reshape(1, SLOTS),
        frag_cols.reshape(1, SLOTS),
        step.reshape(1, SLOTS),
        spectra,
        jnp.asarray(tabs),
        jnp.asarray(consts),
        mask,
        target,
        jnp.asarray(fwd),
        jnp.asarray(up),
        jnp.asarray(down),
    )
    return outs[0], outs[1]


def solution(mesh):
    return jax.shard_map(
        shards,
        mesh=mesh,
        in_specs=(
            P("tile", None),
            P("tile", None),
            P("kern", None, None),
            P("kern"),
            P("tile"),
            P("tile"),
            P("tile"),
            P("tile"),
        ),
        out_specs=(P("tile"), P("tile")),
        check_vma=False,
    )
```

```python
import functools
import math

import jax
import jax.numpy as jnp
import ml_dtypes
import numpy as np
from jax import lax
from jax.experimental import pallas as pl
from jax.experimental.pallas import tpu as pltpu
from jax.sharding import PartitionSpec as P

WIDTH = 2048
COL_FREQS = 64
ROW_FREQS = 16
KERNELS = 24
FRAG_LEN = 32
SLAB = 64
SLOTS = 256
EXT = 192
TILES = 64
KERN = 4
LOCAL = KERNELS // KERN
GRID_ROWS = 32
GRID_COLS = 128
STEEP = 10.0
THRESH = 0.1
F32 = jnp.float32
BF16 = jnp.bfloat16
CHUNKS = 2
GROUP = 6
SPAN = 256
AHEAD = 1
AGROUP = 6
AAHEAD = 1
PLANE = 16
MESH = pl.DeviceIdType.MESH


def np_split(x):
    hi = x.astype(np.float32).astype(ml_dtypes.bfloat16)
    lo = (x - hi.astype(np.float64)).astype(np.float32).astype(ml_dtypes.bfloat16)
    return hi, lo


def pad_lanes(x, lanes=256):
    return np.pad(x, ((0, 0), (0, lanes - x.shape[1])))


@functools.lru_cache(maxsize=None)
def make_tables():
    kc = np.arange(COL_FREQS) - COL_FREQS // 2
    kr = np.arange(ROW_FREQS) - ROW_FREQS // 2
    x = np.arange(WIDTH)
    ang = 2 * np.pi * (np.outer(x, kc) % WIDTH) / WIDTH
    f_hi, f_lo = np_split(np.concatenate([np.cos(ang), -np.sin(ang)], 1) / math.sqrt(WIDTH))
    fwd = np.concatenate([f_hi, f_lo], 1)

    n = np.arange(GRID_COLS)
    step = WIDTH // GRID_COLS
    dist = (x[None, :] - step * n[:, None]) % WIDTH
    base = np.ones(WIDTH)
    for kap in range(1, COL_FREQS):
        base += 2 * np.cos(2 * np.pi * ((np.arange(WIDTH) * kap) % WIDTH) / WIDTH)
    g = (base / GRID_COLS)[dist]
    g = g[:, : WIDTH // 2]
    g_hi, g_lo = np_split(g)
    up = np.concatenate([g_hi.T, g_hi.T, g_lo.T], 1)
    down = np.concatenate([g_hi, g_lo], 0)

    ang = 2 * np.pi * (np.outer(kc, n) % GRID_COLS) / GRID_COLS
    c, s = np.cos(ang) / math.sqrt(WIDTH), np.sin(ang) / math.sqrt(WIDTH)
    inv = np.block([[c, s], [-s, c]])
    i_hi, i_lo = np_split(inv)
    inv3 = np.concatenate([i_hi, i_hi, i_lo], 0)
    t_hi, t_lo = np_split(inv.T)
    adj = np.concatenate([t_hi, t_lo], 1)

    e = np.arange(SLAB)
    ang = 2 * np.pi * (np.outer(kr, e) % EXT) / EXT
    a_hi, a_lo = np_split(np.concatenate([np.cos(ang), np.sin(ang)], 0) / math.sqrt(EXT))
    lt3 = np.concatenate([a_hi, a_hi, a_lo], 1)

    m = np.arange(GRID_ROWS)
    ang = 2 * np.pi * (np.outer(m, kr) % GRID_ROWS) / GRID_ROWS
    c, s = np.cos(ang) / math.sqrt(EXT), np.sin(ang) / math.sqrt(EXT)
    ag = np.block([[c, -s], [s, c]])
    hi, lo = np_split(ag)
    ag3 = np.concatenate([hi, hi, lo], 1)
    hi, lo = np_split(ag.T)
    agt3 = np.concatenate([np.concatenate([hi, hi], 1), np.concatenate([lo, lo], 1)], 0)

    rstep = EXT // GRID_ROWS
    dist = (e[:, None] - rstep * m[None, :]) % EXT
    base = np.ones(EXT)
    for rho in range(1, ROW_FREQS):
        base += 2 * np.cos(2 * np.pi * ((np.arange(EXT) * rho) % EXT) / EXT)
    r = (base / GRID_ROWS)[dist]
    hi, lo = np_split(r)
    r3 = np.concatenate([hi, hi, lo], 1)
    hi, lo = np_split(np.concatenate([r.T, r.T], 1))
    rt2 = np.concatenate([hi, lo], 1)

    tabs = np.concatenate(
        [inv3, adj, pad_lanes(lt3), pad_lanes(ag3), pad_lanes(agt3), pad_lanes(r3), rt2], 0
    )

    ang = 2 * np.pi * (kr % 3) / 3
    cr = np.tile(np.cos(ang), 2)
    ci = np.tile(np.sin(ang), 2)
    with np.errstate(invalid="ignore"):
        d = np.where(kc == 0, FRAG_LEN, np.sin(np.pi * FRAG_LEN * kc / WIDTH) / np.sin(np.pi * kc / WIDTH))
    d = d / math.sqrt(WIDTH)
    col = np.concatenate([cr, ci, d, -d])
    consts = np.repeat(col[:, None], 128, 1).astype(np.float32)
    return fwd, up, down, tabs, consts


def split(x):
    hi = x.astype(BF16)
    return hi, (x - hi.astype(F32)).astype(BF16)


def dot(a, b):
    return lax.dot_general(a, b, (((1,), (0,)), ((), ())), preferred_element_type=F32)


def dot_nt(a, b):
    return lax.dot_general(a, b, (((1,), (1,)), ((), ())), preferred_element_type=F32)


def table_dot(table3, x):
    hi, lo = split(x)
    return dot(table3, jnp.concatenate([hi, lo, hi], 0))


def with_halves_swapped(x):
    return pltpu.roll(x, 64, axis=1)


def column_rows(grids):
    i, d = grids[:, :128], grids[:, 128:]
    hi, lo = split(jnp.concatenate([i, with_halves_swapped(i), d, with_halves_swapped(d)], 0))
    return jnp.concatenate([hi, lo, hi], 1)


def weighted_back(full, target, down):
    w0, w1 = weighting(full[:, :128], full[:, 128:], target)
    hi, lo = split(jnp.concatenate([w0, w1], 1))
    both = dot(down, hi)
    return both[:128] + both[128:] + dot(down[:128], lo)


def weighted_grid(z, rt2):
    swapped = jnp.concatenate([z[64:], z[:64]], 0)
    low = (lax.broadcasted_iota(jnp.int32, z.shape, 1) & 64) == 0
    v = jnp.where(low, z, swapped)
    hi, lo = split(jnp.concatenate([v[:, :128], v[:, 128:]], 0))
    rt_hi, rt_lo = rt2[:, :128], rt2[:, 128:]
    return dot_nt(jnp.concatenate([rt_hi, rt_hi, rt_lo], 1), jnp.concatenate([hi, lo, hi], 1))


def sin_turns(u):
    y = u * (2.0 * math.pi)
    s = y * y
    p = jnp.full_like(s, -1.0 / 39916800.0)
    for coef in (1.0 / 362880.0, -1.0 / 5040.0, 1.0 / 120.0, -1.0 / 6.0):
        p = p * s + coef
    return y + y * (s * p)


def cos_turns(t):
    t = t - jnp.floor(t + 0.5)
    return sin_turns(0.25 - jnp.abs(t))


def times_i(z, sign):
    return pltpu.roll(z, 64, axis=1) * sign


def lane_sign(shape):
    lane = lax.broadcasted_iota(jnp.int32, shape, 1)
    return jnp.where(lane < 64, -1.0, 1.0).astype(F32)


def fragment_tables(rows, cols, dsc):
    kr = lax.broadcasted_iota(jnp.int32, (32, SLOTS), 0)
    is_sin = kr >= 16
    kr = ((kr & 15) - 8).astype(F32)
    t = kr * rows.astype(F32) * (1.0 / EXT)
    row_tab = cos_turns(t - jnp.where(is_sin, 0.25, 0.0)) * (1.0 / math.sqrt(EXT))
    kc = lax.broadcasted_iota(jnp.int32, (128, SLOTS), 0)
    is_sin = kc >= 64
    kc = ((kc & 63) - 32).astype(F32)
    t = kc * (2 * cols + (FRAG_LEN - 1)).astype(F32) * (1.0 / (2 * WIDTH))
    col_tab = cos_turns(t - jnp.where(is_sin, 0.25, 0.0)) * dsc
    return row_tab, col_tab


def own_modes(packed, row_tab, col_hi, col_lo, amp, lt3, sign):
    u0 = table_dot(lt3, packed)
    hi, lo = split(row_tab * amp)
    u1 = dot_nt(
        jnp.concatenate([hi, lo, hi], 1), jnp.concatenate([col_hi, col_hi, col_lo], 1)
    )
    u_re = jnp.concatenate([u0[:16], u1[:16]], 0)
    u_im = jnp.concatenate([u0[16:], u1[16:]], 0)
    return u_re - times_i(u_im, sign)


def combine(own, left, right, cr, ci, sign):
    return own + cr * (left + right) + ci * times_i(left - right, sign)


def two_forms(h, low):
    turned = pltpu.roll(h, 64, axis=1)
    return jnp.where(low, h, turned), jnp.where(low, turned, h)


def side_by_side(x, rows):
    return jnp.concatenate([x[i : i + rows] for i in range(0, x.shape[0], rows)], 1)


def forward_group(hrr, hii, modes, imodes, inv3):
    blocks = []
    for j in range(2):
        m, im = modes[16 * j : 16 * j + 16], imodes[16 * j : 16 * j + 16]
        blocks += [hrr[k] * m + hii[k] * im for k in range(hrr.shape[0])]
    hi, lo = split(jnp.concatenate(blocks, 0))
    return dot(jnp.concatenate([hi, lo, hi], 1), inv3)


def forward_rows(q, ag3):
    q_re, q_im = side_by_side(q[:, :128], 16), side_by_side(q[:, 128:], 16)
    return table_dot(ag3, jnp.concatenate([q_re, q_im], 0))


def intensity_terms(amps, kernels):
    total0 = total1 = None
    for k in range(kernels):
        a, b = amps[:, 128 * k : 128 * k + 128], amps[:, 128 * (kernels + k) : 128 * (kernels + k) + 128]
        s0, s1 = a * a, a * b
        total0 = s0 if total0 is None else total0 + s0
        total1 = s1 if total1 is None else total1 + s1
    return total0[:32] + total0[32:], total1[:32] + total1[32:]


def weighting(inten, change, target):
    developed = 1.0 / (1.0 + jnp.exp(-STEEP * (inten - THRESH)))
    steep = STEEP * developed * (1.0 - developed)
    return steep * (developed - target), steep * steep * change


def adjoint_rows(e0, w0, w1, agt3):
    kernels = e0.shape[1] // 128
    loads = []
    for w in (w0, w1):
        ww = jnp.concatenate([w, w], 0)
        loads += [ww * e0[:, 128 * k : 128 * k + 128] for k in range(kernels)]
    hi, lo = split(jnp.concatenate(loads, 1))
    u = dot(agt3, jnp.concatenate([hi, lo], 0))
    return u[:32] + u[32:]


def adjoint_columns(u, hrr, hii, adj):
    kernels = hrr.shape[0]
    rows = [
        jnp.concatenate([u[:16, 128 * b : 128 * b + 128], u[16:, 128 * b : 128 * b + 128]], 1)
        for b in range(2 * kernels)
    ]
    hi, lo = split(jnp.concatenate(rows, 0))
    both = dot(hi, adj)
    back = both[:, :128] + both[:, 128:] + dot(lo, adj[:, :128])
    first, second = [], []
    for j in range(2):
        f = s = None
        for k in range(kernels):
            at = 16 * (j * kernels + k)
            a, b = hrr[k] * back[at : at + 16], hii[k] * back[at : at + 16]
            f = a if f is None else f + a
            s = b if s is None else s + b
        first.append(f)
        second.append(s)
    return jnp.concatenate(first, 0), jnp.concatenate(second, 0)


def project(total, row_tab, col_hi, col_lo, sign):
    it = times_i(total, sign)
    lhs = jnp.concatenate([total[:16], it[:16], total[16:], it[16:]], 0)
    hi, lo = split(lhs)
    q = dot(jnp.concatenate([hi, lo, hi], 1), jnp.concatenate([col_hi, col_hi, col_lo], 0))
    return [jnp.sum(q[32 * j : 32 * j + 32] * row_tab, axis=0, keepdims=True) for j in range(2)]


def kernel(
    weights_hbm,
    counts_hbm,
    rows_hbm,
    cols_hbm,
    step_hbm,
    spectra_hbm,
    tabs_hbm,
    consts_hbm,
    mask_hbm,
    target_hbm,
    fwd_hbm,
    up_hbm,
    down_hbm,
    out_ref,
    weights_s,
    counts_s,
    rows_v,
    cols_v,
    step_v,
    spectra_v,
    tabs_v,
    consts_v,
    mask_v,
    target_v,
    fwd_v,
    up_v,
    down_v,
    h_v,
    e0_v,
    m_own,
    m_got,
    y_own,
    y_got,
    hrr_v,
    hii_v,
    turned_v,
    res_v,
    load_sem,
    h_send,
    h_recv,
    m_send,
    m_recv,
    y_send,
    y_recv,
    res_send,
    res_recv,
):
    tile = lax.axis_index("tile")
    kern = lax.axis_index("kern")
    lead = 3 - 2 * lax.rem(tile, 2)
    is_lead = kern == lead
    others = [{"tile": tile, "kern": lax.rem(lead + d, KERN)} for d in (1, 2, 3)]
    sides = (
        (tile > 0, {"tile": lax.max(tile - 1, 0), "kern": 4 - lead}),
        (tile < TILES - 1, {"tile": lax.min(tile + 1, TILES - 1), "kern": 4 - lead}),
    )
    first = 1 - lax.min(lax.rem(tile, PLANE), 1)
    left_of_modes = {
        "tile": lax.max(tile - 1 - (PLANE - 2) * first, 0),
        "kern": (4 - lead) * (1 - first),
    }
    is_last = jnp.logical_and(lax.rem(tile, PLANE) == PLANE - 1, tile < TILES - 1)
    is_depot = jnp.logical_and(
        kern == 0, jnp.logical_and(lax.rem(tile, PLANE) == 1, tile < TILES - PLANE)
    )
    barrier = pltpu.get_barrier_semaphore()
    used = []

    def load(src, dst):
        copy = pltpu.make_async_copy(src, dst, load_sem.at[len(used)])
        used.append(copy)
        return copy

    early = [load(weights_hbm, weights_s), load(spectra_hbm, spectra_v)]
    mine = pl.multiple_of(kern * LOCAL, LOCAL)

    def scale_own():
        for copy in early:
            copy.wait()
        for k in range(LOCAL):
            scale = jnp.sqrt(jnp.full((ROW_FREQS, 128), weights_s[k] * (2.0 / KERNELS), F32))
            h_v[mine + k] = spectra_v[k] * scale

    @pl.when(jnp.logical_not(is_lead))
    def _():
        lead_device = {"tile": tile, "kern": lead}

        @pl.when(is_depot)
        def _():
            pl.semaphore_signal(
                barrier,
                inc=1,
                device_id={"tile": lax.min(tile + PLANE - 1, TILES - 1), "kern": 3},
                device_id_type=MESH,
            )

        for copy in early:
            copy.start()
        scale_own()
        pl.semaphore_wait(barrier, 1 + is_depot.astype(jnp.int32))

        @pl.when(is_depot)
        def _():
            copy = pltpu.make_async_remote_copy(
                src_ref=m_got.at[0],
                dst_ref=m_got.at[0],
                send_sem=m_send.at[0],
                recv_sem=m_recv.at[0],
                device_id={"tile": lax.min(tile + PLANE - 2, TILES - 1), "kern": 1},
                device_id_type=MESH,
            )
            copy.wait_recv()
            copy.start()
            copy.wait_send()

        place = lax.rem(kern - lead + KERN, KERN) - 1
        copy = pltpu.make_async_remote_copy(
            src_ref=h_v.at[pl.ds(mine, LOCAL)],
            dst_ref=h_v.at[pl.ds(mine, LOCAL)],
            send_sem=h_send.at[0],
            recv_sem=h_recv.at[place],
            device_id=lead_device,
            device_id_type=MESH,
        )
        copy.start()
        copy.wait_send()
        pltpu.make_async_remote_copy(
            src_ref=res_v,
            dst_ref=res_v,
            send_sem=res_send.at[0],
            recv_sem=res_recv.at[0],
            device_id=lead_device,
            device_id_type=MESH,
        ).wait_recv()

    @pl.when(is_lead)
    def _():
        for d, (exists, _) in enumerate(sides):

            @pl.when(jnp.logical_not(exists))
            def _():
                m_got[1 - d] = jnp.zeros((32, 128), F32)
                y_got[1 - d] = jnp.zeros((32, 128), F32)

        @pl.when(is_last)
        def _():
            pl.semaphore_signal(
                barrier,
                inc=1,
                device_id={"tile": lax.max(tile - (PLANE - 2), 0), "kern": 0},
                device_id_type=MESH,
            )

        for exists, device in (sides[0], (jnp.logical_and(sides[1][0], jnp.logical_not(is_last)), sides[1][1])):

            @pl.when(exists)
            def _():
                pl.semaphore_signal(barrier, inc=1, device_id=device, device_id_type=MESH)

        for device in others:
            pl.semaphore_signal(barrier, inc=1, device_id=device, device_id_type=MESH)

        width = WIDTH // CHUNKS
        small = [
            load(a, b)
            for a, b in (
                (counts_hbm, counts_s),
                (rows_hbm, rows_v),
                (cols_hbm, cols_v),
                (step_hbm, step_v),
                (consts_hbm, consts_v),
                (tabs_hbm, tabs_v),
            )
        ]
        parts = [pl.ds(c * width, width) for c in range(CHUNKS)]
        mask_copies = [load(mask_hbm.at[:, p], mask_v.at[:, p]) for p in parts]
        fwd_copies = [load(fwd_hbm.at[p, :], fwd_v.at[p, :]) for p in parts]
        later = [load(up_hbm, up_v), load(target_hbm, target_v), load(down_hbm, down_v)]
        for copy in small:
            copy.start()
        for a, b in zip(mask_copies, fwd_copies):
            a.start()
            b.start()
        for copy in early + later:
            copy.start()

        for copy in small:
            copy.wait()
        sign = lane_sign((32, 128))
        cr, ci = consts_v[0:32], consts_v[32:64]
        dsc = consts_v[64:192]
        row_tab, col_tab = fragment_tables(rows_v[...], cols_v[...], jnp.concatenate([dsc, dsc], 1))
        col_hi, col_lo = split(col_tab)
        active = lax.broadcasted_iota(jnp.int32, (1, SLOTS), 1) < counts_s[0]
        amp = jnp.where(active, step_v[...], 0.0) * (1.0 / math.sqrt(FRAG_LEN))

        total = jnp.zeros((2 * SLAB, 256), F32)
        for c in range(CHUNKS):
            mask_copies[c].wait()
            fwd_copies[c].wait()
            hi, lo = split(mask_v[:, c * width : (c + 1) * width])
            total += dot(jnp.concatenate([hi, lo], 0), fwd_v[c * width : (c + 1) * width, :])
        packed = total[:SLAB, :128] + total[:SLAB, 128:] + total[SLAB:, :128]
        modes_own = own_modes(packed, row_tab, col_hi, col_lo, amp, tabs_v[640:672, :192], sign)
        m_own[...] = modes_own

        def exchange(own, got, send, recv, devices):
            copies = [
                pltpu.make_async_remote_copy(
                    src_ref=own,
                    dst_ref=got.at[d],
                    send_sem=send.at[d],
                    recv_sem=recv.at[d],
                    device_id=device,
                    device_id_type=MESH,
                )
                for d, device in enumerate(devices)
            ]
            for d, (exists, _) in enumerate(sides):

                @pl.when(exists)
                def _():
                    copies[d].start()

            return copies

        def arrived(copies):
            for d, (exists, _) in enumerate(sides):

                @pl.when(exists)
                def _():
                    copies[1 - d].wait_recv()

        def sent(copies):
            for d, (exists, _) in enumerate(sides):

                @pl.when(exists)
                def _():
                    copies[d].wait_send()

        pl.semaphore_wait(barrier, lax.min(tile, 1) + lax.min(TILES - 1 - tile, 1))
        m_copies = exchange(m_own, m_got, m_send, m_recv, (left_of_modes, sides[1][1]))

        scale_own()
        low = lax.broadcasted_iota(jnp.int32, (ROW_FREQS, 128), 1) < 64

        def take(place, d):
            at = pl.multiple_of(lax.rem(lead + d, KERN) * LOCAL, LOCAL)
            if d > 0:
                pltpu.make_async_remote_copy(
                    src_ref=h_v.at[pl.ds(at, LOCAL)],
                    dst_ref=h_v.at[pl.ds(at, LOCAL)],
                    send_sem=h_send.at[0],
                    recv_sem=h_recv.at[d - 1],
                    device_id=others[0],
                    device_id_type=MESH,
                ).wait_recv()
            for k in range(LOCAL):
                a, b = two_forms(h_v[at + k], low)
                hrr_v[place * LOCAL + k] = a
                hii_v[place * LOCAL + k] = b

        take(0, 0)
        take(1, 3)

        def forms(g):
            ks = pl.ds(g * GROUP, GROUP)
            return hrr_v[ks], hii_v[ks]

        for copy in later:
            copy.wait()
        for c in range(8):
            ends = [target_v[:, h + 128 * c : h + 128 * c + 128] for h in (0, WIDTH // 2)]
            turned_v[128 * c : 128 * c + 128, :] = jnp.transpose(jnp.concatenate(ends, 0))
        arrived(m_copies)
        modes = combine(modes_own, m_got[1], m_got[0], cr, ci, sign)
        imodes = times_i(modes, sign)

        inten = change = jnp.zeros((GRID_ROWS, 128), F32)
        n = KERNELS // GROUP
        ready = []
        for g in range(n + AHEAD):
            if g == n // 2:
                take(2, 2)
            if g == max(3 * n // 4, 1):
                take(3, 1)
            if g < n:
                hrr, hii = forms(g)
                ready.append(forward_group(hrr, hii, modes, imodes, tabs_v[0:384, :]))
            if g >= AHEAD:
                amps = forward_rows(ready[g - AHEAD], tabs_v[672:736, :96])
                e0_v[g - AHEAD] = amps[:, : 128 * GROUP]
                s0, s1 = intensity_terms(amps, GROUP)
                inten, change = inten + s0, change + s1

        grids = table_dot(tabs_v[800:864, :96], jnp.concatenate([0.5 * inten, change], 1))
        rows3 = column_rows(grids)

        n = WIDTH // 2 // SPAN
        parts = [slice(c * SPAN, (c + 1) * SPAN) for c in range(n)]
        total = jnp.zeros((128, 256), F32)
        full = dot_nt(up_v[parts[0], :], rows3)
        for c in range(n):
            ahead = dot_nt(up_v[parts[c + 1], :], rows3) if c + 1 < n else None
            total += weighted_back(full, turned_v[parts[c], :], down_v[:, parts[c]])
            full = ahead
        wgrid = weighted_grid(total, tabs_v[864:896, :])
        w0, w1 = wgrid[:, :128], wgrid[:, 128:]

        first = second = jnp.zeros((32, 128), F32)
        ready = []
        n = KERNELS // AGROUP
        for g in range(n + AAHEAD):
            if g < n:
                e0 = e0_v[g * AGROUP // GROUP, :, pl.ds(g * AGROUP % GROUP * 128, AGROUP * 128)]
                ready.append(adjoint_rows(e0, w0, w1, tabs_v[736:800, :128]))
            if g >= AAHEAD:
                ks = pl.ds((g - AAHEAD) * AGROUP, AGROUP)
                a, b = adjoint_columns(ready[g - AAHEAD], hrr_v[ks], hii_v[ks], tabs_v[384:640, :])
                first, second = first + a, second + b
        spectrum = first - times_i(second, sign)
        y_own[...] = spectrum

        y_copies = exchange(y_own, y_got, y_send, y_recv, (sides[0][1], sides[1][1]))
        arrived(y_copies)
        whole = combine(spectrum, y_got[1], y_got[0], cr, ci, sign)
        outs = project(whole, row_tab, col_hi, col_lo, sign)
        for j in range(2):
            res_v[j : j + 1, :] = jnp.where(active, outs[j] * (1.0 / math.sqrt(FRAG_LEN)), 0.0)

        res_copies = [
            pltpu.make_async_remote_copy(
                src_ref=res_v,
                dst_ref=res_v,
                send_sem=res_send.at[d],
                recv_sem=res_recv.at[0],
                device_id=device,
                device_id_type=MESH,
            )
            for d, device in enumerate(others)
        ]
        for d in (1, 0, 2):
            res_copies[d].start()
        sent(m_copies)
        sent(y_copies)
        for copy in res_copies:
            copy.wait_send()

    out_ref[...] = res_v[...]


def shards(mask, target, spectra, weights, counts, frag_rows, frag_cols, step):
    fwd, up, down, tabs, consts = make_tables()
    vmem = pl.BlockSpec(memory_space=pltpu.VMEM)
    hbm = pl.BlockSpec(memory_space=pltpu.HBM)
    dma = pltpu.SemaphoreType.DMA
    outs = pl.pallas_call(
        kernel,
        out_shape=pltpu.VMEM((2, SLOTS), F32),
        in_specs=[hbm] * 13,
        out_specs=vmem,
        scratch_shapes=[
            pltpu.SMEM((LOCAL,), F32),
            pltpu.SMEM((1,), jnp.int32),
            pltpu.VMEM((1, SLOTS), jnp.int32),
            pltpu.VMEM((1, SLOTS), jnp.int32),
            pltpu.VMEM((1, SLOTS), F32),
            pltpu.VMEM((LOCAL, ROW_FREQS, 128), F32),
            pltpu.VMEM(tabs.shape, BF16),
            pltpu.VMEM(consts.shape, F32),
            pltpu.VMEM((SLAB, WIDTH), F32),
            pltpu.VMEM((SLAB, WIDTH), F32),
            pltpu.VMEM((WIDTH, 256), BF16),
            pltpu.VMEM(up.shape, BF16),
            pltpu.VMEM(down.shape, BF16),
            pltpu.VMEM((KERNELS, ROW_FREQS, 128), F32),
            pltpu.VMEM((KERNELS // GROUP, 2 * GRID_ROWS, 128 * GROUP), F32),
            pltpu.VMEM((32, 128), F32),
            pltpu.VMEM((2, 32, 128), F32),
            pltpu.VMEM((32, 128), F32),
            pltpu.VMEM((2, 32, 128), F32),
            pltpu.VMEM((KERNELS, ROW_FREQS, 128), F32),
            pltpu.VMEM((KERNELS, ROW_FREQS, 128), F32),
            pltpu.VMEM((WIDTH // 2, 128), F32),
            pltpu.VMEM((2, SLOTS), F32),
            dma((2 * CHUNKS + 11,)),
            dma((1,)),
            dma((3,)),
            dma((2,)),
            dma((2,)),
            dma((2,)),
            dma((2,)),
            dma((3,)),
            dma((1,)),
        ],
        compiler_params=pltpu.CompilerParams(
            collective_id=0, has_side_effects=True, vmem_limit_bytes=60 * 1024 * 1024
        ),
    )(
        weights,
        counts,
        frag_rows.reshape(1, SLOTS),
        frag_cols.reshape(1, SLOTS),
        step.reshape(1, SLOTS),
        spectra,
        jnp.asarray(tabs),
        jnp.asarray(consts),
        mask,
        target,
        jnp.asarray(fwd),
        jnp.asarray(up),
        jnp.asarray(down),
    )
    return outs[0], outs[1]


def solution(mesh):
    return jax.shard_map(
        shards,
        mesh=mesh,
        in_specs=(
            P("tile", None),
            P("tile", None),
            P("kern", None, None),
            P("kern"),
            P("tile"),
            P("tile"),
            P("tile"),
            P("tile"),
        ),
        out_specs=(P("tile"), P("tile")),
        check_vma=False,
    )
```

```python
import functools
import math

import jax
import jax.numpy as jnp
import ml_dtypes
import numpy as np
from jax import lax
from jax.experimental import pallas as pl
from jax.experimental.pallas import tpu as pltpu
from jax.sharding import PartitionSpec as P

WIDTH = 2048
COL_FREQS = 64
ROW_FREQS = 16
KERNELS = 24
FRAG_LEN = 32
SLAB = 64
SLOTS = 256
EXT = 192
TILES = 64
KERN = 4
LOCAL = KERNELS // KERN
GRID_ROWS = 32
GRID_COLS = 128
STEEP = 10.0
THRESH = 0.1
F32 = jnp.float32
BF16 = jnp.bfloat16
CHUNKS = 2
GROUP = 8
SPAN = 256
AHEAD = 1
AGROUP = 8
AAHEAD = 1
PLANE = 16
MESH = pl.DeviceIdType.MESH


def np_split(x):
    hi = x.astype(np.float32).astype(ml_dtypes.bfloat16)
    lo = (x - hi.astype(np.float64)).astype(np.float32).astype(ml_dtypes.bfloat16)
    return hi, lo


def pad_lanes(x, lanes=256):
    return np.pad(x, ((0, 0), (0, lanes - x.shape[1])))


@functools.lru_cache(maxsize=None)
def make_tables():
    kc = np.arange(COL_FREQS) - COL_FREQS // 2
    kr = np.arange(ROW_FREQS) - ROW_FREQS // 2
    x = np.arange(WIDTH)
    ang = 2 * np.pi * (np.outer(x, kc) % WIDTH) / WIDTH
    f_hi, f_lo = np_split(np.concatenate([np.cos(ang), -np.sin(ang)], 1) / math.sqrt(WIDTH))
    fwd = np.concatenate([f_hi, f_lo], 1)

    n = np.arange(GRID_COLS)
    step = WIDTH // GRID_COLS
    dist = (x[None, :] - step * n[:, None]) % WIDTH
    base = np.ones(WIDTH)
    for kap in range(1, COL_FREQS):
        base += 2 * np.cos(2 * np.pi * ((np.arange(WIDTH) * kap) % WIDTH) / WIDTH)
    g = (base / GRID_COLS)[dist]
    g = g[:, : WIDTH // 2]
    g_hi, g_lo = np_split(g)
    up = np.concatenate([g_hi.T, g_hi.T, g_lo.T], 1)
    down = np.concatenate([g_hi, g_lo], 0)

    ang = 2 * np.pi * (np.outer(kc, n) % GRID_COLS) / GRID_COLS
    c, s = np.cos(ang) / math.sqrt(WIDTH), np.sin(ang) / math.sqrt(WIDTH)
    inv = np.block([[c, s], [-s, c]])
    i_hi, i_lo = np_split(inv)
    inv3 = np.concatenate([i_hi, i_hi, i_lo], 0)
    t_hi, t_lo = np_split(inv.T)
    adj = np.concatenate([t_hi, t_lo], 1)

    e = np.arange(SLAB)
    ang = 2 * np.pi * (np.outer(kr, e) % EXT) / EXT
    a_hi, a_lo = np_split(np.concatenate([np.cos(ang), np.sin(ang)], 0) / math.sqrt(EXT))
    lt3 = np.concatenate([a_hi, a_hi, a_lo], 1)

    m = np.arange(GRID_ROWS)
    ang = 2 * np.pi * (np.outer(m, kr) % GRID_ROWS) / GRID_ROWS
    c, s = np.cos(ang) / math.sqrt(EXT), np.sin(ang) / math.sqrt(EXT)
    ag = np.block([[c, -s], [s, c]])
    hi, lo = np_split(ag)
    ag3 = np.concatenate([hi, hi, lo], 1)
    hi, lo = np_split(ag.T)
    agt3 = np.concatenate([np.concatenate([hi, hi], 1), np.concatenate([lo, lo], 1)], 0)

    rstep = EXT // GRID_ROWS
    dist = (e[:, None] - rstep * m[None, :]) % EXT
    base = np.ones(EXT)
    for rho in range(1, ROW_FREQS):
        base += 2 * np.cos(2 * np.pi * ((np.arange(EXT) * rho) % EXT) / EXT)
    r = (base / GRID_ROWS)[dist]
    hi, lo = np_split(r)
    r3 = np.concatenate([hi, hi, lo], 1)
    hi, lo = np_split(np.concatenate([r.T, r.T], 1))
    rt2 = np.concatenate([hi, lo], 1)

    tabs = np.concatenate(
        [inv3, adj, pad_lanes(lt3), pad_lanes(ag3), pad_lanes(agt3), pad_lanes(r3), rt2], 0
    )

    ang = 2 * np.pi * (kr % 3) / 3
    cr = np.tile(np.cos(ang), 2)
    ci = np.tile(np.sin(ang), 2)
    with np.errstate(invalid="ignore"):
        d = np.where(kc == 0, FRAG_LEN, np.sin(np.pi * FRAG_LEN * kc / WIDTH) / np.sin(np.pi * kc / WIDTH))
    d = d / math.sqrt(WIDTH)
    col = np.concatenate([cr, ci, d, -d])
    consts = np.repeat(col[:, None], 128, 1).astype(np.float32)
    return fwd, up, down, tabs, consts


def split(x):
    hi = x.astype(BF16)
    return hi, (x - hi.astype(F32)).astype(BF16)


def dot(a, b):
    return lax.dot_general(a, b, (((1,), (0,)), ((), ())), preferred_element_type=F32)


def dot_nt(a, b):
    return lax.dot_general(a, b, (((1,), (1,)), ((), ())), preferred_element_type=F32)


def table_dot(table3, x):
    hi, lo = split(x)
    return dot(table3, jnp.concatenate([hi, lo, hi], 0))


def with_halves_swapped(x):
    return pltpu.roll(x, 64, axis=1)


def column_rows(grids):
    i, d = grids[:, :128], grids[:, 128:]
    hi, lo = split(jnp.concatenate([i, with_halves_swapped(i), d, with_halves_swapped(d)], 0))
    return jnp.concatenate([hi, lo, hi], 1)


def weighted_back(full, target, down):
    w0, w1 = weighting(full[:, :128], full[:, 128:], target)
    hi, lo = split(jnp.concatenate([w0, w1], 1))
    both = dot(down, hi)
    return both[:128] + both[128:] + dot(down[:128], lo)


def weighted_grid(z, rt2):
    swapped = jnp.concatenate([z[64:], z[:64]], 0)
    low = (lax.broadcasted_iota(jnp.int32, z.shape, 1) & 64) == 0
    v = jnp.where(low, z, swapped)
    hi, lo = split(jnp.concatenate([v[:, :128], v[:, 128:]], 0))
    rt_hi, rt_lo = rt2[:, :128], rt2[:, 128:]
    return dot_nt(jnp.concatenate([rt_hi, rt_hi, rt_lo], 1), jnp.concatenate([hi, lo, hi], 1))


def sin_turns(u):
    y = u * (2.0 * math.pi)
    s = y * y
    p = jnp.full_like(s, -1.0 / 39916800.0)
    for coef in (1.0 / 362880.0, -1.0 / 5040.0, 1.0 / 120.0, -1.0 / 6.0):
        p = p * s + coef
    return y + y * (s * p)


def cos_turns(t):
    t = t - jnp.floor(t + 0.5)
    return sin_turns(0.25 - jnp.abs(t))


def times_i(z, sign):
    return pltpu.roll(z, 64, axis=1) * sign


def lane_sign(shape):
    lane = lax.broadcasted_iota(jnp.int32, shape, 1)
    return jnp.where(lane < 64, -1.0, 1.0).astype(F32)


def fragment_tables(rows, cols, dsc):
    kr = lax.broadcasted_iota(jnp.int32, (32, SLOTS), 0)
    is_sin = kr >= 16
    kr = ((kr & 15) - 8).astype(F32)
    t = kr * rows.astype(F32) * (1.0 / EXT)
    row_tab = cos_turns(t - jnp.where(is_sin, 0.25, 0.0)) * (1.0 / math.sqrt(EXT))
    kc = lax.broadcasted_iota(jnp.int32, (128, SLOTS), 0)
    is_sin = kc >= 64
    kc = ((kc & 63) - 32).astype(F32)
    t = kc * (2 * cols + (FRAG_LEN - 1)).astype(F32) * (1.0 / (2 * WIDTH))
    col_tab = cos_turns(t - jnp.where(is_sin, 0.25, 0.0)) * dsc
    return row_tab, col_tab


def own_modes(packed, row_tab, col_hi, col_lo, amp, lt3, sign):
    u0 = table_dot(lt3, packed)
    hi, lo = split(row_tab * amp)
    u1 = dot_nt(
        jnp.concatenate([hi, lo, hi], 1), jnp.concatenate([col_hi, col_hi, col_lo], 1)
    )
    u_re = jnp.concatenate([u0[:16], u1[:16]], 0)
    u_im = jnp.concatenate([u0[16:], u1[16:]], 0)
    return u_re - times_i(u_im, sign)


def combine(own, left, right, cr, ci, sign):
    return own + cr * (left + right) + ci * times_i(left - right, sign)


def two_forms(h, low):
    turned = pltpu.roll(h, 64, axis=1)
    return jnp.where(low, h, turned), jnp.where(low, turned, h)


def side_by_side(x, rows):
    return jnp.concatenate([x[i : i + rows] for i in range(0, x.shape[0], rows)], 1)


def forward_group(hrr, hii, modes, imodes, inv3):
    blocks = []
    for j in range(2):
        m, im = modes[16 * j : 16 * j + 16], imodes[16 * j : 16 * j + 16]
        blocks += [hrr[k] * m + hii[k] * im for k in range(hrr.shape[0])]
    hi, lo = split(jnp.concatenate(blocks, 0))
    return dot(jnp.concatenate([hi, lo, hi], 1), inv3)


def forward_rows(q, ag3):
    q_re, q_im = side_by_side(q[:, :128], 16), side_by_side(q[:, 128:], 16)
    return table_dot(ag3, jnp.concatenate([q_re, q_im], 0))


def intensity_terms(amps, kernels):
    total0 = total1 = None
    for k in range(kernels):
        a, b = amps[:, 128 * k : 128 * k + 128], amps[:, 128 * (kernels + k) : 128 * (kernels + k) + 128]
        s0, s1 = a * a, a * b
        total0 = s0 if total0 is None else total0 + s0
        total1 = s1 if total1 is None else total1 + s1
    return total0[:32] + total0[32:], total1[:32] + total1[32:]


def weighting(inten, change, target):
    developed = 1.0 / (1.0 + jnp.exp(-STEEP * (inten - THRESH)))
    steep = STEEP * developed * (1.0 - developed)
    return steep * (developed - target), steep * steep * change


def adjoint_rows(e0, w0, w1, agt3):
    kernels = e0.shape[1] // 128
    loads = []
    for w in (w0, w1):
        ww = jnp.concatenate([w, w], 0)
        loads += [ww * e0[:, 128 * k : 128 * k + 128] for k in range(kernels)]
    hi, lo = split(jnp.concatenate(loads, 1))
    u = dot(agt3, jnp.concatenate([hi, lo], 0))
    return u[:32] + u[32:]


def adjoint_columns(u, hrr, hii, adj):
    kernels = hrr.shape[0]
    rows = [
        jnp.concatenate([u[:16, 128 * b : 128 * b + 128], u[16:, 128 * b : 128 * b + 128]], 1)
        for b in range(2 * kernels)
    ]
    hi, lo = split(jnp.concatenate(rows, 0))
    both = dot(hi, adj)
    back = both[:, :128] + both[:, 128:] + dot(lo, adj[:, :128])
    first, second = [], []
    for j in range(2):
        f = s = None
        for k in range(kernels):
            at = 16 * (j * kernels + k)
            a, b = hrr[k] * back[at : at + 16], hii[k] * back[at : at + 16]
            f = a if f is None else f + a
            s = b if s is None else s + b
        first.append(f)
        second.append(s)
    return jnp.concatenate(first, 0), jnp.concatenate(second, 0)


def project(total, row_tab, col_hi, col_lo, sign):
    it = times_i(total, sign)
    lhs = jnp.concatenate([total[:16], it[:16], total[16:], it[16:]], 0)
    hi, lo = split(lhs)
    q = dot(jnp.concatenate([hi, lo, hi], 1), jnp.concatenate([col_hi, col_hi, col_lo], 0))
    return [jnp.sum(q[32 * j : 32 * j + 32] * row_tab, axis=0, keepdims=True) for j in range(2)]


def kernel(
    weights_hbm,
    counts_hbm,
    rows_hbm,
    cols_hbm,
    step_hbm,
    spectra_hbm,
    tabs_hbm,
    consts_hbm,
    mask_hbm,
    target_hbm,
    fwd_hbm,
    up_hbm,
    down_hbm,
    out_ref,
    weights_s,
    counts_s,
    rows_v,
    cols_v,
    step_v,
    spectra_v,
    tabs_v,
    consts_v,
    mask_v,
    target_v,
    fwd_v,
    up_v,
    down_v,
    h_v,
    e0_v,
    m_own,
    m_got,
    y_own,
    y_got,
    hrr_v,
    hii_v,
    turned_v,
    res_v,
    load_sem,
    h_send,
    h_recv,
    m_send,
    m_recv,
    y_send,
    y_recv,
    res_send,
    res_recv,
    go_sem,
):
    tile = lax.axis_index("tile")
    kern = lax.axis_index("kern")
    def depot_tile(t):
        return jnp.logical_and(lax.rem(t, PLANE) == 1, t < TILES - PLANE).astype(jnp.int32)

    def lead_of(t):
        return 3 - 2 * lax.rem(t, 2) - depot_tile(t)

    lead = lead_of(tile)
    is_lead = kern == lead
    others = [{"tile": tile, "kern": lax.rem(lead + d, KERN)} for d in (1, 2, 3)]
    before, after = lax.max(tile - 1, 0), lax.min(tile + 1, TILES - 1)
    sides = (
        (tile > 0, {"tile": before, "kern": lead_of(before)}),
        (tile < TILES - 1, {"tile": after, "kern": lead_of(after)}),
    )
    first = 1 - lax.min(lax.rem(tile, PLANE), 1)
    left_of_modes = {
        "tile": lax.max(tile - 1 - (PLANE - 2) * first, 0),
        "kern": lead_of(before) * (1 - first) + first,
    }
    is_last = jnp.logical_and(lax.rem(tile, PLANE) == PLANE - 1, tile < TILES - 1)
    has_depot = depot_tile(tile) == 1
    is_depot = jnp.logical_and(has_depot, kern == 1)
    barrier = pltpu.get_barrier_semaphore()
    used = []

    def load(src, dst):
        copy = pltpu.make_async_copy(src, dst, load_sem.at[len(used)])
        used.append(copy)
        return copy

    early = [load(weights_hbm, weights_s), load(spectra_hbm, spectra_v)]
    mine = pl.multiple_of(kern * LOCAL, LOCAL)

    def scale_own():
        for copy in early:
            copy.wait()
        for k in range(LOCAL):
            scale = jnp.sqrt(jnp.full((ROW_FREQS, 128), weights_s[k] * (2.0 / KERNELS), F32))
            h_v[mine + k] = spectra_v[k] * scale

    @pl.when(jnp.logical_not(is_lead))
    def _():
        lead_device = {"tile": tile, "kern": lead}

        @pl.when(is_depot)
        def _():
            pl.semaphore_signal(
                barrier,
                inc=1,
                device_id={"tile": lax.min(tile + PLANE - 1, TILES - 1), "kern": 3},
                device_id_type=MESH,
            )
            pl.semaphore_signal(barrier, inc=1, device_id=lead_device, device_id_type=MESH)

        for copy in early:
            copy.start()
        scale_own()

        @pl.when(is_depot)
        def _():
            pl.semaphore_wait(go_sem, 1)

        @pl.when(jnp.logical_not(is_depot))
        def _():
            pl.semaphore_wait(barrier, 1)

        place = lax.rem(kern - lead + KERN, KERN) - 1
        copy = pltpu.make_async_remote_copy(
            src_ref=h_v.at[pl.ds(mine, LOCAL)],
            dst_ref=h_v.at[pl.ds(mine, LOCAL)],
            send_sem=h_send.at[0],
            recv_sem=h_recv.at[place],
            device_id=lead_device,
            device_id_type=MESH,
        )
        copy.start()

        @pl.when(is_depot)
        def _():
            pl.semaphore_wait(barrier, 1)
            onward = pltpu.make_async_remote_copy(
                src_ref=m_got.at[0],
                dst_ref=m_got.at[0],
                send_sem=m_send.at[0],
                recv_sem=m_recv.at[0],
                device_id={"tile": lax.min(tile + PLANE - 2, TILES - 1), "kern": 1},
                device_id_type=MESH,
            )
            onward.wait_recv()
            onward.start()
            onward.wait_send()

        copy.wait_send()
        pltpu.make_async_remote_copy(
            src_ref=res_v,
            dst_ref=res_v,
            send_sem=res_send.at[0],
            recv_sem=res_recv.at[0],
            device_id=lead_device,
            device_id_type=MESH,
        ).wait_recv()

    @pl.when(is_lead)
    def _():
        for d, (exists, _) in enumerate(sides):

            @pl.when(jnp.logical_not(exists))
            def _():
                m_got[1 - d] = jnp.zeros((32, 128), F32)
                y_got[1 - d] = jnp.zeros((32, 128), F32)

        @pl.when(is_last)
        def _():
            pl.semaphore_signal(
                barrier,
                inc=1,
                device_id={"tile": lax.max(tile - (PLANE - 2), 0), "kern": 1},
                device_id_type=MESH,
            )

        for exists, device in (sides[0], (jnp.logical_and(sides[1][0], jnp.logical_not(is_last)), sides[1][1])):

            @pl.when(exists)
            def _():
                pl.semaphore_signal(barrier, inc=1, device_id=device, device_id_type=MESH)

        for device in others[1:]:
            pl.semaphore_signal(barrier, inc=1, device_id=device, device_id_type=MESH)

        @pl.when(jnp.logical_not(has_depot))
        def _():
            pl.semaphore_signal(barrier, inc=1, device_id=others[0], device_id_type=MESH)

        width = WIDTH // CHUNKS
        small = [
            load(a, b)
            for a, b in (
                (counts_hbm, counts_s),
                (rows_hbm, rows_v),
                (cols_hbm, cols_v),
                (step_hbm, step_v),
                (consts_hbm, consts_v),
                (tabs_hbm, tabs_v),
            )
        ]
        parts = [pl.ds(c * width, width) for c in range(CHUNKS)]
        mask_copies = [load(mask_hbm.at[:, p], mask_v.at[:, p]) for p in parts]
        fwd_copies = [load(fwd_hbm.at[p, :], fwd_v.at[p, :]) for p in parts]
        later = [load(up_hbm, up_v), load(target_hbm, target_v), load(down_hbm, down_v)]
        for copy in small:
            copy.start()
        for a, b in zip(mask_copies, fwd_copies):
            a.start()
            b.start()
        for copy in early + later:
            copy.start()

        for copy in small:
            copy.wait()
        sign = lane_sign((32, 128))
        cr, ci = consts_v[0:32], consts_v[32:64]
        dsc = consts_v[64:192]
        row_tab, col_tab = fragment_tables(rows_v[...], cols_v[...], jnp.concatenate([dsc, dsc], 1))
        col_hi, col_lo = split(col_tab)
        active = lax.broadcasted_iota(jnp.int32, (1, SLOTS), 1) < counts_s[0]
        amp = jnp.where(active, step_v[...], 0.0) * (1.0 / math.sqrt(FRAG_LEN))

        total = jnp.zeros((2 * SLAB, 256), F32)
        for c in range(CHUNKS):
            mask_copies[c].wait()
            fwd_copies[c].wait()
            hi, lo = split(mask_v[:, c * width : (c + 1) * width])
            total += dot(jnp.concatenate([hi, lo], 0), fwd_v[c * width : (c + 1) * width, :])
        packed = total[:SLAB, :128] + total[:SLAB, 128:] + total[SLAB:, :128]
        modes_own = own_modes(packed, row_tab, col_hi, col_lo, amp, tabs_v[640:672, :192], sign)
        m_own[...] = modes_own

        def exchange(own, got, send, recv, devices):
            copies = [
                pltpu.make_async_remote_copy(
                    src_ref=own,
                    dst_ref=got.at[d],
                    send_sem=send.at[d],
                    recv_sem=recv.at[d],
                    device_id=device,
                    device_id_type=MESH,
                )
                for d, device in enumerate(devices)
            ]
            for d, (exists, _) in enumerate(sides):

                @pl.when(exists)
                def _():
                    copies[d].start()

            return copies

        def arrived(copies):
            for d, (exists, _) in enumerate(sides):

                @pl.when(exists)
                def _():
                    copies[1 - d].wait_recv()

        def sent(copies):
            for d, (exists, _) in enumerate(sides):

                @pl.when(exists)
                def _():
                    copies[d].wait_send()

        pl.semaphore_wait(
            barrier, lax.min(tile, 1) + lax.min(TILES - 1 - tile, 1) + depot_tile(tile)
        )

        @pl.when(has_depot)
        def _():
            pl.semaphore_signal(go_sem, inc=1, device_id=others[0], device_id_type=MESH)

        m_copies = exchange(m_own, m_got, m_send, m_recv, (left_of_modes, sides[1][1]))

        scale_own()
        low = lax.broadcasted_iota(jnp.int32, (ROW_FREQS, 128), 1) < 64

        def take(place, d):
            at = pl.multiple_of(lax.rem(lead + d, KERN) * LOCAL, LOCAL)
            if d > 0:
                pltpu.make_async_remote_copy(
                    src_ref=h_v.at[pl.ds(at, LOCAL)],
                    dst_ref=h_v.at[pl.ds(at, LOCAL)],
                    send_sem=h_send.at[0],
                    recv_sem=h_recv.at[d - 1],
                    device_id=others[0],
                    device_id_type=MESH,
                ).wait_recv()
            for k in range(LOCAL):
                a, b = two_forms(h_v[at + k], low)
                hrr_v[place * LOCAL + k] = a
                hii_v[place * LOCAL + k] = b

        take(0, 0)
        take(1, 3)

        def forms(g):
            ks = pl.ds(g * GROUP, GROUP)
            return hrr_v[ks], hii_v[ks]

        for copy in later:
            copy.wait()
        for c in range(8):
            ends = [target_v[:, h + 128 * c : h + 128 * c + 128] for h in (0, WIDTH // 2)]
            turned_v[128 * c : 128 * c + 128, :] = jnp.transpose(jnp.concatenate(ends, 0))
        arrived(m_copies)
        modes = combine(modes_own, m_got[1], m_got[0], cr, ci, sign)
        imodes = times_i(modes, sign)

        inten = change = jnp.zeros((GRID_ROWS, 128), F32)
        n = KERNELS // GROUP
        ready = []
        for g in range(n + AHEAD):
            if g == n // 2:
                take(2, 2)
            if g == max(3 * n // 4, 1):
                take(3, 1)
            if g < n:
                hrr, hii = forms(g)
                ready.append(forward_group(hrr, hii, modes, imodes, tabs_v[0:384, :]))
            if g >= AHEAD:
                amps = forward_rows(ready[g - AHEAD], tabs_v[672:736, :96])
                e0_v[g - AHEAD] = amps[:, : 128 * GROUP]
                s0, s1 = intensity_terms(amps, GROUP)
                inten, change = inten + s0, change + s1

        grids = table_dot(tabs_v[800:864, :96], jnp.concatenate([0.5 * inten, change], 1))
        rows3 = column_rows(grids)

        n = WIDTH // 2 // SPAN
        parts = [slice(c * SPAN, (c + 1) * SPAN) for c in range(n)]
        total = jnp.zeros((128, 256), F32)
        full = dot_nt(up_v[parts[0], :], rows3)
        for c in range(n):
            ahead = dot_nt(up_v[parts[c + 1], :], rows3) if c + 1 < n else None
            total += weighted_back(full, turned_v[parts[c], :], down_v[:, parts[c]])
            full = ahead
        wgrid = weighted_grid(total, tabs_v[864:896, :])
        w0, w1 = wgrid[:, :128], wgrid[:, 128:]

        first = second = jnp.zeros((32, 128), F32)
        ready = []
        n = KERNELS // AGROUP
        for g in range(n + AAHEAD):
            if g < n:
                e0 = e0_v[g * AGROUP // GROUP, :, pl.ds(g * AGROUP % GROUP * 128, AGROUP * 128)]
                ready.append(adjoint_rows(e0, w0, w1, tabs_v[736:800, :128]))
            if g >= AAHEAD:
                ks = pl.ds((g - AAHEAD) * AGROUP, AGROUP)
                a, b = adjoint_columns(ready[g - AAHEAD], hrr_v[ks], hii_v[ks], tabs_v[384:640, :])
                first, second = first + a, second + b
        spectrum = first - times_i(second, sign)
        y_own[...] = spectrum

        y_copies = exchange(y_own, y_got, y_send, y_recv, (sides[0][1], sides[1][1]))
        arrived(y_copies)
        whole = combine(spectrum, y_got[1], y_got[0], cr, ci, sign)
        outs = project(whole, row_tab, col_hi, col_lo, sign)
        for j in range(2):
            res_v[j : j + 1, :] = jnp.where(active, outs[j] * (1.0 / math.sqrt(FRAG_LEN)), 0.0)

        res_copies = [
            pltpu.make_async_remote_copy(
                src_ref=res_v,
                dst_ref=res_v,
                send_sem=res_send.at[d],
                recv_sem=res_recv.at[0],
                device_id=device,
                device_id_type=MESH,
            )
            for d, device in enumerate(others)
        ]
        for d in (1, 0, 2):
            res_copies[d].start()
        sent(m_copies)
        sent(y_copies)
        for copy in res_copies:
            copy.wait_send()

    out_ref[...] = res_v[...]


def shards(mask, target, spectra, weights, counts, frag_rows, frag_cols, step):
    fwd, up, down, tabs, consts = make_tables()
    vmem = pl.BlockSpec(memory_space=pltpu.VMEM)
    hbm = pl.BlockSpec(memory_space=pltpu.HBM)
    dma = pltpu.SemaphoreType.DMA
    outs = pl.pallas_call(
        kernel,
        out_shape=pltpu.VMEM((2, SLOTS), F32),
        in_specs=[hbm] * 13,
        out_specs=vmem,
        scratch_shapes=[
            pltpu.SMEM((LOCAL,), F32),
            pltpu.SMEM((1,), jnp.int32),
            pltpu.VMEM((1, SLOTS), jnp.int32),
            pltpu.VMEM((1, SLOTS), jnp.int32),
            pltpu.VMEM((1, SLOTS), F32),
            pltpu.VMEM((LOCAL, ROW_FREQS, 128), F32),
            pltpu.VMEM(tabs.shape, BF16),
            pltpu.VMEM(consts.shape, F32),
            pltpu.VMEM((SLAB, WIDTH), F32),
            pltpu.VMEM((SLAB, WIDTH), F32),
            pltpu.VMEM((WIDTH, 256), BF16),
            pltpu.VMEM(up.shape, BF16),
            pltpu.VMEM(down.shape, BF16),
            pltpu.VMEM((KERNELS, ROW_FREQS, 128), F32),
            pltpu.VMEM((KERNELS // GROUP, 2 * GRID_ROWS, 128 * GROUP), F32),
            pltpu.VMEM((32, 128), F32),
            pltpu.VMEM((2, 32, 128), F32),
            pltpu.VMEM((32, 128), F32),
            pltpu.VMEM((2, 32, 128), F32),
            pltpu.VMEM((KERNELS, ROW_FREQS, 128), F32),
            pltpu.VMEM((KERNELS, ROW_FREQS, 128), F32),
            pltpu.VMEM((WIDTH // 2, 128), F32),
            pltpu.VMEM((2, SLOTS), F32),
            dma((2 * CHUNKS + 11,)),
            dma((1,)),
            dma((3,)),
            dma((2,)),
            dma((2,)),
            dma((2,)),
            dma((2,)),
            dma((3,)),
            dma((1,)),
            pltpu.SemaphoreType.REGULAR,
        ],
        compiler_params=pltpu.CompilerParams(
            collective_id=0, has_side_effects=True, vmem_limit_bytes=60 * 1024 * 1024
        ),
    )(
        weights,
        counts,
        frag_rows.reshape(1, SLOTS),
        frag_cols.reshape(1, SLOTS),
        step.reshape(1, SLOTS),
        spectra,
        jnp.asarray(tabs),
        jnp.asarray(consts),
        mask,
        target,
        jnp.asarray(fwd),
        jnp.asarray(up),
        jnp.asarray(down),
    )
    return outs[0], outs[1]


def solution(mesh):
    return jax.shard_map(
        shards,
        mesh=mesh,
        in_specs=(
            P("tile", None),
            P("tile", None),
            P("kern", None, None),
            P("kern"),
            P("tile"),
            P("tile"),
            P("tile"),
            P("tile"),
        ),
        out_specs=(P("tile"), P("tile")),
        check_vma=False,
    )
```

```python
import functools
import math

import jax
import jax.numpy as jnp
import ml_dtypes
import numpy as np
from jax import lax
from jax.experimental import pallas as pl
from jax.experimental.pallas import tpu as pltpu
from jax.sharding import PartitionSpec as P

WIDTH = 2048
COL_FREQS = 64
ROW_FREQS = 16
KERNELS = 24
FRAG_LEN = 32
SLAB = 64
SLOTS = 256
EXT = 192
TILES = 64
KERN = 4
LOCAL = KERNELS // KERN
GRID_ROWS = 32
GRID_COLS = 128
STEEP = 10.0
THRESH = 0.1
F32 = jnp.float32
BF16 = jnp.bfloat16
CHUNKS = 2
GROUP = 8
SPAN = 256
AHEAD = 1
AGROUP = 8
AAHEAD = 1
PLANE = 16
MESH = pl.DeviceIdType.MESH


def np_split(x):
    hi = x.astype(np.float32).astype(ml_dtypes.bfloat16)
    lo = (x - hi.astype(np.float64)).astype(np.float32).astype(ml_dtypes.bfloat16)
    return hi, lo


def pad_lanes(x, lanes=256):
    return np.pad(x, ((0, 0), (0, lanes - x.shape[1])))


@functools.lru_cache(maxsize=None)
def make_tables():
    kc = np.arange(COL_FREQS) - COL_FREQS // 2
    kr = np.arange(ROW_FREQS) - ROW_FREQS // 2
    x = np.arange(WIDTH)
    ang = 2 * np.pi * (np.outer(x, kc) % WIDTH) / WIDTH
    f_hi, f_lo = np_split(np.concatenate([np.cos(ang), -np.sin(ang)], 1) / math.sqrt(WIDTH))
    fwd = np.concatenate([f_hi, f_lo], 1)

    n = np.arange(GRID_COLS)
    step = WIDTH // GRID_COLS
    dist = (x[None, :] - step * n[:, None]) % WIDTH
    base = np.ones(WIDTH)
    for kap in range(1, COL_FREQS):
        base += 2 * np.cos(2 * np.pi * ((np.arange(WIDTH) * kap) % WIDTH) / WIDTH)
    g = (base / GRID_COLS)[dist]
    g = g[:, : WIDTH // 2]
    g_hi, g_lo = np_split(g)
    up = np.concatenate([g_hi.T, g_hi.T, g_lo.T], 1)
    down = np.concatenate([g_hi, g_lo], 0)

    ang = 2 * np.pi * (np.outer(kc, n) % GRID_COLS) / GRID_COLS
    c, s = np.cos(ang) / math.sqrt(WIDTH), np.sin(ang) / math.sqrt(WIDTH)
    inv = np.block([[c, s], [-s, c]])
    i_hi, i_lo = np_split(inv)
    inv3 = np.concatenate([i_hi, i_hi, i_lo], 0)
    t_hi, t_lo = np_split(inv.T)
    adj = np.concatenate([t_hi, t_lo], 1)

    e = np.arange(SLAB)
    ang = 2 * np.pi * (np.outer(kr, e) % EXT) / EXT
    a_hi, a_lo = np_split(np.concatenate([np.cos(ang), np.sin(ang)], 0) / math.sqrt(EXT))
    lt3 = np.concatenate([a_hi, a_hi, a_lo], 1)

    m = np.arange(GRID_ROWS)
    ang = 2 * np.pi * (np.outer(m, kr) % GRID_ROWS) / GRID_ROWS
    c, s = np.cos(ang) / math.sqrt(EXT), np.sin(ang) / math.sqrt(EXT)
    ag = np.block([[c, -s], [s, c]])
    hi, lo = np_split(ag)
    ag3 = np.concatenate([hi, hi, lo], 1)
    hi, lo = np_split(ag.T)
    agt3 = np.concatenate([np.concatenate([hi, hi], 1), np.concatenate([lo, lo], 1)], 0)

    rstep = EXT // GRID_ROWS
    dist = (e[:, None] - rstep * m[None, :]) % EXT
    base = np.ones(EXT)
    for rho in range(1, ROW_FREQS):
        base += 2 * np.cos(2 * np.pi * ((np.arange(EXT) * rho) % EXT) / EXT)
    r = (base / GRID_ROWS)[dist]
    hi, lo = np_split(r)
    r3 = np.concatenate([hi, hi, lo], 1)
    hi, lo = np_split(np.concatenate([r.T, r.T], 1))
    rt2 = np.concatenate([hi, lo], 1)

    tabs = np.concatenate(
        [inv3, adj, pad_lanes(lt3), pad_lanes(ag3), pad_lanes(agt3), pad_lanes(r3), rt2], 0
    )

    ang = 2 * np.pi * (kr % 3) / 3
    cr = np.tile(np.cos(ang), 2)
    ci = np.tile(np.sin(ang), 2)
    with np.errstate(invalid="ignore"):
        d = np.where(kc == 0, FRAG_LEN, np.sin(np.pi * FRAG_LEN * kc / WIDTH) / np.sin(np.pi * kc / WIDTH))
    d = d / math.sqrt(WIDTH)
    col = np.concatenate([cr, ci, d, -d])
    consts = np.repeat(col[:, None], 128, 1).astype(np.float32)
    return fwd, up, down, tabs, consts


def split(x):
    hi = x.astype(BF16)
    return hi, (x - hi.astype(F32)).astype(BF16)


def dot(a, b):
    return lax.dot_general(a, b, (((1,), (0,)), ((), ())), preferred_element_type=F32)


def dot_nt(a, b):
    return lax.dot_general(a, b, (((1,), (1,)), ((), ())), preferred_element_type=F32)


def table_dot(table3, x):
    hi, lo = split(x)
    return dot(table3, jnp.concatenate([hi, lo, hi], 0))


def with_halves_swapped(x):
    return pltpu.roll(x, 64, axis=1)


def column_rows(grids):
    i, d = grids[:, :128], grids[:, 128:]
    hi, lo = split(jnp.concatenate([i, with_halves_swapped(i), d, with_halves_swapped(d)], 0))
    return jnp.concatenate([hi, lo, hi], 1)


def weighted_back(full, target, down):
    w0, w1 = weighting(full[:, :128], full[:, 128:], target)
    hi, lo = split(jnp.concatenate([w0, w1], 1))
    both = dot(down, hi)
    return both[:128] + both[128:] + dot(down[:128], lo)


def weighted_grid(z, rt2):
    swapped = jnp.concatenate([z[64:], z[:64]], 0)
    low = (lax.broadcasted_iota(jnp.int32, z.shape, 1) & 64) == 0
    v = jnp.where(low, z, swapped)
    hi, lo = split(jnp.concatenate([v[:, :128], v[:, 128:]], 0))
    rt_hi, rt_lo = rt2[:, :128], rt2[:, 128:]
    return dot_nt(jnp.concatenate([rt_hi, rt_hi, rt_lo], 1), jnp.concatenate([hi, lo, hi], 1))


def sin_turns(u):
    y = u * (2.0 * math.pi)
    s = y * y
    p = jnp.full_like(s, -1.0 / 39916800.0)
    for coef in (1.0 / 362880.0, -1.0 / 5040.0, 1.0 / 120.0, -1.0 / 6.0):
        p = p * s + coef
    return y + y * (s * p)


def cos_turns(t):
    t = t - jnp.floor(t + 0.5)
    return sin_turns(0.25 - jnp.abs(t))


def times_i(z, sign):
    return pltpu.roll(z, 64, axis=1) * sign


def lane_sign(shape):
    lane = lax.broadcasted_iota(jnp.int32, shape, 1)
    return jnp.where(lane < 64, -1.0, 1.0).astype(F32)


def fragment_tables(rows, cols, dsc):
    kr = lax.broadcasted_iota(jnp.int32, (32, SLOTS), 0)
    is_sin = kr >= 16
    kr = ((kr & 15) - 8).astype(F32)
    t = kr * rows.astype(F32) * (1.0 / EXT)
    row_tab = cos_turns(t - jnp.where(is_sin, 0.25, 0.0)) * (1.0 / math.sqrt(EXT))
    kc = lax.broadcasted_iota(jnp.int32, (128, SLOTS), 0)
    is_sin = kc >= 64
    kc = ((kc & 63) - 32).astype(F32)
    t = kc * (2 * cols + (FRAG_LEN - 1)).astype(F32) * (1.0 / (2 * WIDTH))
    col_tab = cos_turns(t - jnp.where(is_sin, 0.25, 0.0)) * dsc
    return row_tab, col_tab


def own_modes(packed, row_tab, col_hi, col_lo, amp, lt3, sign):
    u0 = table_dot(lt3, packed)
    hi, lo = split(row_tab * amp)
    u1 = dot_nt(
        jnp.concatenate([hi, lo, hi], 1), jnp.concatenate([col_hi, col_hi, col_lo], 1)
    )
    u_re = jnp.concatenate([u0[:16], u1[:16]], 0)
    u_im = jnp.concatenate([u0[16:], u1[16:]], 0)
    return u_re - times_i(u_im, sign)


def combine(own, left, right, cr, ci, sign):
    return own + cr * (left + right) + ci * times_i(left - right, sign)


def two_forms(h, low):
    turned = pltpu.roll(h, 64, axis=1)
    return jnp.where(low, h, turned), jnp.where(low, turned, h)


def side_by_side(x, rows):
    return jnp.concatenate([x[i : i + rows] for i in range(0, x.shape[0], rows)], 1)


def forward_group(hrr, hii, modes, imodes, inv3):
    blocks = []
    for j in range(2):
        m, im = modes[16 * j : 16 * j + 16], imodes[16 * j : 16 * j + 16]
        blocks += [hrr[k] * m + hii[k] * im for k in range(hrr.shape[0])]
    hi, lo = split(jnp.concatenate(blocks, 0))
    return dot(jnp.concatenate([hi, lo, hi], 1), inv3)


def forward_rows(q, ag3):
    q_re, q_im = side_by_side(q[:, :128], 16), side_by_side(q[:, 128:], 16)
    return table_dot(ag3, jnp.concatenate([q_re, q_im], 0))


def intensity_terms(amps, kernels):
    total0 = total1 = None
    for k in range(kernels):
        a, b = amps[:, 128 * k : 128 * k + 128], amps[:, 128 * (kernels + k) : 128 * (kernels + k) + 128]
        s0, s1 = a * a, a * b
        total0 = s0 if total0 is None else total0 + s0
        total1 = s1 if total1 is None else total1 + s1
    return total0[:32] + total0[32:], total1[:32] + total1[32:]


def weighting(inten, change, target):
    developed = 1.0 / (1.0 + jnp.exp(-STEEP * (inten - THRESH)))
    steep = STEEP * developed * (1.0 - developed)
    return steep * (developed - target), steep * steep * change


def adjoint_rows(e0, w0, w1, agt3):
    kernels = e0.shape[1] // 128
    loads = []
    for w in (w0, w1):
        ww = jnp.concatenate([w, w], 0)
        loads += [ww * e0[:, 128 * k : 128 * k + 128] for k in range(kernels)]
    hi, lo = split(jnp.concatenate(loads, 1))
    u = dot(agt3, jnp.concatenate([hi, lo], 0))
    return u[:32] + u[32:]


def adjoint_columns(u, hrr, hii, adj):
    kernels = hrr.shape[0]
    rows = [
        jnp.concatenate([u[:16, 128 * b : 128 * b + 128], u[16:, 128 * b : 128 * b + 128]], 1)
        for b in range(2 * kernels)
    ]
    hi, lo = split(jnp.concatenate(rows, 0))
    both = dot(hi, adj)
    back = both[:, :128] + both[:, 128:] + dot(lo, adj[:, :128])
    first, second = [], []
    for j in range(2):
        f = s = None
        for k in range(kernels):
            at = 16 * (j * kernels + k)
            a, b = hrr[k] * back[at : at + 16], hii[k] * back[at : at + 16]
            f = a if f is None else f + a
            s = b if s is None else s + b
        first.append(f)
        second.append(s)
    return jnp.concatenate(first, 0), jnp.concatenate(second, 0)


def project(total, row_tab, col_hi, col_lo, sign):
    it = times_i(total, sign)
    lhs = jnp.concatenate([total[:16], it[:16], total[16:], it[16:]], 0)
    hi, lo = split(lhs)
    q = dot(jnp.concatenate([hi, lo, hi], 1), jnp.concatenate([col_hi, col_hi, col_lo], 0))
    return [jnp.sum(q[32 * j : 32 * j + 32] * row_tab, axis=0, keepdims=True) for j in range(2)]


def kernel(
    weights_hbm,
    counts_hbm,
    rows_hbm,
    cols_hbm,
    step_hbm,
    spectra_hbm,
    tabs_hbm,
    consts_hbm,
    mask_hbm,
    target_hbm,
    fwd_hbm,
    up_hbm,
    down_hbm,
    out_ref,
    weights_s,
    counts_s,
    rows_v,
    cols_v,
    step_v,
    spectra_v,
    tabs_v,
    consts_v,
    mask_v,
    target_v,
    fwd_v,
    up_v,
    down_v,
    h_v,
    e0_v,
    m_own,
    m_got,
    y_own,
    y_got,
    hrr_v,
    hii_v,
    turned_v,
    res_v,
    load_sem,
    h_send,
    h_recv,
    m_send,
    m_recv,
    y_send,
    y_recv,
    res_send,
    res_recv,
    go_sem,
    own_recv,
    far_sem,
):
    tile = lax.axis_index("tile")
    kern = lax.axis_index("kern")
    def depot_tile(t):
        return jnp.logical_and(lax.rem(t, PLANE) == 1, t < TILES - PLANE).astype(jnp.int32)

    def lead_of(t):
        return 3 - 2 * lax.rem(t, 2) - depot_tile(t)

    lead = lead_of(tile)
    is_lead = kern == lead
    others = [{"tile": tile, "kern": lax.rem(lead + d, KERN)} for d in (1, 2, 3)]
    before, after = lax.max(tile - 1, 0), lax.min(tile + 1, TILES - 1)
    sides = (
        (tile > 0, {"tile": before, "kern": lead_of(before)}),
        (tile < TILES - 1, {"tile": after, "kern": lead_of(after)}),
    )
    first = 1 - lax.min(lax.rem(tile, PLANE), 1)
    left_of_modes = {
        "tile": lax.max(tile - 1 - (PLANE - 2) * first, 0),
        "kern": lead_of(before) * (1 - first) + first,
    }
    is_last = jnp.logical_and(lax.rem(tile, PLANE) == PLANE - 1, tile < TILES - 1)
    is_first = jnp.logical_and(first == 1, tile > 0)
    has_depot = depot_tile(tile) == 1

    def far_of(t):
        base = 2 - 2 * (lead_of(t) // 2)
        return [{"tile": t, "kern": base + c} for c in range(2)]

    is_far = kern // 2 != lead // 2
    mate = {"tile": tile, "kern": lead + 1 - 2 * lax.rem(lead, 2)}
    is_depot = jnp.logical_and(has_depot, kern == 1)
    barrier = pltpu.get_barrier_semaphore()
    used = []

    def load(src, dst):
        copy = pltpu.make_async_copy(src, dst, load_sem.at[len(used)])
        used.append(copy)
        return copy

    early = [load(weights_hbm, weights_s), load(spectra_hbm, spectra_v)]
    mine = pl.multiple_of(kern * LOCAL, LOCAL)

    def scale_own():
        for copy in early:
            copy.wait()
        for k in range(LOCAL):
            scale = jnp.sqrt(jnp.full((ROW_FREQS, 128), weights_s[k] * (2.0 / KERNELS), F32))
            h_v[mine + k] = spectra_v[k] * scale

    def fragments():
        sign = lane_sign((32, 128))
        cr, ci = consts_v[0:32], consts_v[32:64]
        dsc = consts_v[64:192]
        row_tab, col_tab = fragment_tables(rows_v[...], cols_v[...], jnp.concatenate([dsc, dsc], 1))
        col_hi, col_lo = split(col_tab)
        active = lax.broadcasted_iota(jnp.int32, (1, SLOTS), 1) < counts_s[0]
        return sign, cr, ci, row_tab, col_hi, col_lo, active

    def finish(spectrum, sign, cr, ci, row_tab, col_hi, col_lo, active):
        whole = combine(spectrum, y_got[1], y_got[0], cr, ci, sign)
        outs = project(whole, row_tab, col_hi, col_lo, sign)
        for j in range(2):
            res_v[j : j + 1, :] = jnp.where(active, outs[j] * (1.0 / math.sqrt(FRAG_LEN)), 0.0)

    @pl.when(jnp.logical_not(is_lead))
    def _():
        lead_device = {"tile": tile, "kern": lead}
        small = [
            load(a, b)
            for a, b in (
                (counts_hbm, counts_s),
                (rows_hbm, rows_v),
                (cols_hbm, cols_v),
                (consts_hbm, consts_v),
            )
        ]

        @pl.when(is_far)
        def _():
            for d, (exists, _) in enumerate(sides):

                @pl.when(jnp.logical_not(exists))
                def _():
                    y_got[1 - d] = jnp.zeros((32, 128), F32)


        @pl.when(is_depot)
        def _():
            pl.semaphore_signal(
                barrier,
                inc=1,
                device_id={"tile": lax.min(tile + PLANE - 1, TILES - 1), "kern": 3},
                device_id_type=MESH,
            )
            pl.semaphore_signal(barrier, inc=1, device_id=lead_device, device_id_type=MESH)

        for copy in early:
            copy.start()
        scale_own()

        @pl.when(is_depot)
        def _():
            pl.semaphore_wait(go_sem, 1)

        @pl.when(jnp.logical_not(is_depot))
        def _():
            pl.semaphore_wait(barrier, 1)

        place = lax.rem(kern - lead + KERN, KERN) - 1
        copy = pltpu.make_async_remote_copy(
            src_ref=h_v.at[pl.ds(mine, LOCAL)],
            dst_ref=h_v.at[pl.ds(mine, LOCAL)],
            send_sem=h_send.at[0],
            recv_sem=h_recv.at[place],
            device_id=lead_device,
            device_id_type=MESH,
        )
        copy.start()

        @pl.when(is_depot)
        def _():
            pl.semaphore_wait(barrier, 1)
            onward = pltpu.make_async_remote_copy(
                src_ref=m_got.at[0],
                dst_ref=m_got.at[0],
                send_sem=m_send.at[0],
                recv_sem=m_recv.at[0],
                device_id={"tile": lax.min(tile + PLANE - 2, TILES - 1), "kern": 1},
                device_id_type=MESH,
            )
            onward.wait_recv()
            onward.start()
            pl.semaphore_wait(far_sem.at[0], 1)
            pl.semaphore_signal(
                far_sem.at[0],
                inc=1,
                device_id={"tile": lax.min(tile + PLANE - 2, TILES - 1), "kern": 1},
                device_id_type=MESH,
            )
            onward.wait_send()

        @pl.when(jnp.logical_not(is_far))
        def _():
            pltpu.make_async_remote_copy(
                src_ref=res_v,
                dst_ref=res_v,
                send_sem=res_send.at[0],
                recv_sem=res_recv.at[0],
                device_id=lead_device,
                device_id_type=MESH,
            ).wait_recv()

        @pl.when(is_far)
        def _():
            for load_copy in small:
                load_copy.start()
            for load_copy in small:
                load_copy.wait()
            sign, cr, ci, row_tab, col_hi, col_lo, active = fragments()
            for d, (exists, _) in enumerate(sides):

                @pl.when(exists)
                def _():
                    pltpu.make_async_remote_copy(
                        src_ref=y_own,
                        dst_ref=y_got.at[1 - d],
                        send_sem=y_send.at[0],
                        recv_sem=y_recv.at[1 - d],
                        device_id=lead_device,
                        device_id_type=MESH,
                    ).wait_recv()

            pltpu.make_async_remote_copy(
                src_ref=y_own,
                dst_ref=y_own,
                send_sem=y_send.at[0],
                recv_sem=own_recv.at[0],
                device_id=lead_device,
                device_id_type=MESH,
            ).wait_recv()
            finish(y_own[...], sign, cr, ci, row_tab, col_hi, col_lo, active)

        copy.wait_send()

    @pl.when(is_lead)
    def _():
        for d, (exists, _) in enumerate(sides):

            @pl.when(jnp.logical_not(exists))
            def _():
                m_got[1 - d] = jnp.zeros((32, 128), F32)
                y_got[1 - d] = jnp.zeros((32, 128), F32)

        @pl.when(is_last)
        def _():
            pl.semaphore_signal(
                barrier,
                inc=1,
                device_id={"tile": lax.max(tile - (PLANE - 2), 0), "kern": 1},
                device_id_type=MESH,
            )

        @pl.when(jnp.logical_not(has_depot))
        def _():
            pl.semaphore_signal(barrier, inc=1, device_id=others[0], device_id_type=MESH)

        for device in others[1:]:
            pl.semaphore_signal(barrier, inc=1, device_id=device, device_id_type=MESH)

        for exists, device in (sides[0], (jnp.logical_and(sides[1][0], jnp.logical_not(is_last)), sides[1][1])):

            @pl.when(exists)
            def _():
                pl.semaphore_signal(barrier, inc=1, device_id=device, device_id_type=MESH)

        width = WIDTH // CHUNKS
        small = [
            load(a, b)
            for a, b in (
                (counts_hbm, counts_s),
                (rows_hbm, rows_v),
                (cols_hbm, cols_v),
                (step_hbm, step_v),
                (consts_hbm, consts_v),
                (tabs_hbm, tabs_v),
            )
        ]
        parts = [pl.ds(c * width, width) for c in range(CHUNKS)]
        mask_copies = [load(mask_hbm.at[:, p], mask_v.at[:, p]) for p in parts]
        fwd_copies = [load(fwd_hbm.at[p, :], fwd_v.at[p, :]) for p in parts]
        later = [load(up_hbm, up_v), load(target_hbm, target_v), load(down_hbm, down_v)]
        for copy in small:
            copy.start()
        for a, b in zip(mask_copies, fwd_copies):
            a.start()
            b.start()
        for copy in early + later:
            copy.start()

        for copy in small:
            copy.wait()
        sign, cr, ci, row_tab, col_hi, col_lo, active = fragments()
        amp = jnp.where(active, step_v[...], 0.0) * (1.0 / math.sqrt(FRAG_LEN))

        total = jnp.zeros((2 * SLAB, 256), F32)
        for c in range(CHUNKS):
            mask_copies[c].wait()
            fwd_copies[c].wait()
            hi, lo = split(mask_v[:, c * width : (c + 1) * width])
            total += dot(jnp.concatenate([hi, lo], 0), fwd_v[c * width : (c + 1) * width, :])
        packed = total[:SLAB, :128] + total[:SLAB, 128:] + total[SLAB:, :128]
        modes_own = own_modes(packed, row_tab, col_hi, col_lo, amp, tabs_v[640:672, :192], sign)
        m_own[...] = modes_own

        def exchange(own, got, send, recv, devices):
            copies = [
                pltpu.make_async_remote_copy(
                    src_ref=own,
                    dst_ref=got.at[d],
                    send_sem=send.at[d],
                    recv_sem=recv.at[d],
                    device_id=device,
                    device_id_type=MESH,
                )
                for d, device in enumerate(devices)
            ]
            for d, (exists, _) in enumerate(sides):

                @pl.when(exists)
                def _():
                    copies[d].start()

            return copies

        def arrived(copies):
            for d, (exists, _) in enumerate(sides):

                @pl.when(exists)
                def _():
                    copies[1 - d].wait_recv()

        def sent(copies):
            for d, (exists, _) in enumerate(sides):

                @pl.when(exists)
                def _():
                    copies[d].wait_send()

        pl.semaphore_wait(
            barrier, lax.min(tile, 1) + lax.min(TILES - 1 - tile, 1) + depot_tile(tile)
        )

        @pl.when(has_depot)
        def _():
            pl.semaphore_signal(go_sem, inc=1, device_id=others[0], device_id_type=MESH)

        m_copies = exchange(m_own, m_got, m_send, m_recv, (left_of_modes, sides[1][1]))

        scale_own()
        low = lax.broadcasted_iota(jnp.int32, (ROW_FREQS, 128), 1) < 64

        def spectra_from(d):
            at = pl.multiple_of(lax.rem(lead + d, KERN) * LOCAL, LOCAL)
            return pltpu.make_async_remote_copy(
                src_ref=h_v.at[pl.ds(at, LOCAL)],
                dst_ref=h_v.at[pl.ds(at, LOCAL)],
                send_sem=h_send.at[0],
                recv_sem=h_recv.at[d - 1],
                device_id=others[0],
                device_id_type=MESH,
            )

        def far_is_here(d):
            pl.semaphore_signal(
                far_sem.at[d],
                inc=1,
                device_id=(left_of_modes, sides[1][1])[d],
                device_id_type=MESH,
            )

        @pl.when(is_first)
        def _():
            for d in (1, 2, 3):
                spectra_from(d).wait_recv()
            far_is_here(0)

        def take(place, d):
            at = pl.multiple_of(lax.rem(lead + d, KERN) * LOCAL, LOCAL)
            if d > 0:

                @pl.when(jnp.logical_not(is_first))
                def _():
                    spectra_from(d).wait_recv()

            for k in range(LOCAL):
                a, b = two_forms(h_v[at + k], low)
                hrr_v[place * LOCAL + k] = a
                hii_v[place * LOCAL + k] = b

        take(0, 0)
        take(1, 3)

        def forms(g):
            ks = pl.ds(g * GROUP, GROUP)
            return hrr_v[ks], hii_v[ks]

        for copy in later:
            copy.wait()
        for c in range(8):
            ends = [target_v[:, h + 128 * c : h + 128 * c + 128] for h in (0, WIDTH // 2)]
            turned_v[128 * c : 128 * c + 128, :] = jnp.transpose(jnp.concatenate(ends, 0))
        arrived(m_copies)
        modes = combine(modes_own, m_got[1], m_got[0], cr, ci, sign)
        imodes = times_i(modes, sign)

        inten = change = jnp.zeros((GRID_ROWS, 128), F32)
        n = KERNELS // GROUP
        ready = []
        for g in range(n + AHEAD):
            if g == n // 2:
                take(2, 2)
            if g == max(3 * n // 4, 1):
                take(3, 1)

                @pl.when(jnp.logical_and(sides[0][0], jnp.logical_not(is_first)))
                def _():
                    far_is_here(0)

                @pl.when(sides[1][0])
                def _():
                    far_is_here(1)

            if g < n:
                hrr, hii = forms(g)
                ready.append(forward_group(hrr, hii, modes, imodes, tabs_v[0:384, :]))
            if g >= AHEAD:
                amps = forward_rows(ready[g - AHEAD], tabs_v[672:736, :96])
                e0_v[g - AHEAD] = amps[:, : 128 * GROUP]
                s0, s1 = intensity_terms(amps, GROUP)
                inten, change = inten + s0, change + s1

        grids = table_dot(tabs_v[800:864, :96], jnp.concatenate([0.5 * inten, change], 1))
        rows3 = column_rows(grids)

        n = WIDTH // 2 // SPAN
        parts = [slice(c * SPAN, (c + 1) * SPAN) for c in range(n)]
        total = jnp.zeros((128, 256), F32)
        full = dot_nt(up_v[parts[0], :], rows3)
        for c in range(n):
            ahead = dot_nt(up_v[parts[c + 1], :], rows3) if c + 1 < n else None
            total += weighted_back(full, turned_v[parts[c], :], down_v[:, parts[c]])
            full = ahead
        wgrid = weighted_grid(total, tabs_v[864:896, :])
        w0, w1 = wgrid[:, :128], wgrid[:, 128:]

        first = second = jnp.zeros((32, 128), F32)
        ready = []
        n = KERNELS // AGROUP
        for g in range(n + AAHEAD):
            if g < n:
                e0 = e0_v[g * AGROUP // GROUP, :, pl.ds(g * AGROUP % GROUP * 128, AGROUP * 128)]
                ready.append(adjoint_rows(e0, w0, w1, tabs_v[736:800, :128]))
            if g >= AAHEAD:
                ks = pl.ds((g - AAHEAD) * AGROUP, AGROUP)
                a, b = adjoint_columns(ready[g - AAHEAD], hrr_v[ks], hii_v[ks], tabs_v[384:640, :])
                first, second = first + a, second + b
        spectrum = first - times_i(second, sign)
        y_own[...] = spectrum

        def send_own(i, device, d=None):
            return pltpu.make_async_remote_copy(
                src_ref=y_own,
                dst_ref=y_own if d is None else y_got.at[d],
                send_sem=y_send.at[i],
                recv_sem=own_recv.at[0] if d is None else y_recv.at[d],
                device_id=device,
                device_id_type=MESH,
            )

        y_copies = [send_own(d, sides[d][1], d) for d in range(2)]
        own_copies = [send_own(2 + c, device) for c, device in enumerate(far_of(tile))]
        far_copies = [
            [send_own(4 + 2 * d + c, device, d) for c, device in enumerate(far_of(t))]
            for d, t in enumerate((before, after))
        ]
        for d in (1, 0):

            @pl.when(sides[d][0])
            def _():
                pl.semaphore_wait(far_sem.at[1 - d], 1)
                for copy in reversed(far_copies[d]):
                    copy.start()
                y_copies[d].start()

            if d == 1:
                for copy in own_copies:
                    copy.start()

        arrived(y_copies)
        finish(spectrum, sign, cr, ci, row_tab, col_hi, col_lo, active)
        res_copy = pltpu.make_async_remote_copy(
            src_ref=res_v,
            dst_ref=res_v,
            send_sem=res_send.at[0],
            recv_sem=res_recv.at[0],
            device_id=mate,
            device_id_type=MESH,
        )
        res_copy.start()
        sent(m_copies)
        sent(y_copies)
        for copy in own_copies:
            copy.wait_send()
        for d in range(2):

            @pl.when(sides[d][0])
            def _():
                for copy in far_copies[d]:
                    copy.wait_send()

        res_copy.wait_send()

    out_ref[...] = res_v[...]


def shards(mask, target, spectra, weights, counts, frag_rows, frag_cols, step):
    fwd, up, down, tabs, consts = make_tables()
    vmem = pl.BlockSpec(memory_space=pltpu.VMEM)
    hbm = pl.BlockSpec(memory_space=pltpu.HBM)
    dma = pltpu.SemaphoreType.DMA
    outs = pl.pallas_call(
        kernel,
        out_shape=pltpu.VMEM((2, SLOTS), F32),
        in_specs=[hbm] * 13,
        out_specs=vmem,
        scratch_shapes=[
            pltpu.SMEM((LOCAL,), F32),
            pltpu.SMEM((1,), jnp.int32),
            pltpu.VMEM((1, SLOTS), jnp.int32),
            pltpu.VMEM((1, SLOTS), jnp.int32),
            pltpu.VMEM((1, SLOTS), F32),
            pltpu.VMEM((LOCAL, ROW_FREQS, 128), F32),
            pltpu.VMEM(tabs.shape, BF16),
            pltpu.VMEM(consts.shape, F32),
            pltpu.VMEM((SLAB, WIDTH), F32),
            pltpu.VMEM((SLAB, WIDTH), F32),
            pltpu.VMEM((WIDTH, 256), BF16),
            pltpu.VMEM(up.shape, BF16),
            pltpu.VMEM(down.shape, BF16),
            pltpu.VMEM((KERNELS, ROW_FREQS, 128), F32),
            pltpu.VMEM((KERNELS // GROUP, 2 * GRID_ROWS, 128 * GROUP), F32),
            pltpu.VMEM((32, 128), F32),
            pltpu.VMEM((2, 32, 128), F32),
            pltpu.VMEM((32, 128), F32),
            pltpu.VMEM((2, 32, 128), F32),
            pltpu.VMEM((KERNELS, ROW_FREQS, 128), F32),
            pltpu.VMEM((KERNELS, ROW_FREQS, 128), F32),
            pltpu.VMEM((WIDTH // 2, 128), F32),
            pltpu.VMEM((2, SLOTS), F32),
            dma((2 * CHUNKS + 15,)),
            dma((1,)),
            dma((3,)),
            dma((2,)),
            dma((2,)),
            dma((8,)),
            dma((2,)),
            dma((1,)),
            dma((1,)),
            pltpu.SemaphoreType.REGULAR,
            dma((1,)),
            pltpu.SemaphoreType.REGULAR((2,)),
        ],
        compiler_params=pltpu.CompilerParams(
            collective_id=0, has_side_effects=True, vmem_limit_bytes=60 * 1024 * 1024
        ),
    )(
        weights,
        counts,
        frag_rows.reshape(1, SLOTS),
        frag_cols.reshape(1, SLOTS),
        step.reshape(1, SLOTS),
        spectra,
        jnp.asarray(tabs),
        jnp.asarray(consts),
        mask,
        target,
        jnp.asarray(fwd),
        jnp.asarray(up),
        jnp.asarray(down),
    )
    return outs[0], outs[1]


def solution(mesh):
    return jax.shard_map(
        shards,
        mesh=mesh,
        in_specs=(
            P("tile", None),
            P("tile", None),
            P("kern", None, None),
            P("kern"),
            P("tile"),
            P("tile"),
            P("tile"),
            P("tile"),
        ),
        out_specs=(P("tile"), P("tile")),
        check_vma=False,
    )
```

```python
import functools
import math

import jax
import jax.numpy as jnp
import ml_dtypes
import numpy as np
from jax import lax
from jax.experimental import pallas as pl
from jax.experimental.pallas import tpu as pltpu
from jax.sharding import PartitionSpec as P

WIDTH = 2048
COL_FREQS = 64
ROW_FREQS = 16
KERNELS = 24
FRAG_LEN = 32
SLAB = 64
SLOTS = 256
EXT = 192
TILES = 64
KERN = 4
LOCAL = KERNELS // KERN
GRID_ROWS = 32
GRID_COLS = 128
STEEP = 10.0
THRESH = 0.1
F32 = jnp.float32
BF16 = jnp.bfloat16
CHUNKS = 2
GROUP = 8
SPAN = 256
AHEAD = 1
AGROUP = 8
AAHEAD = 1
PLANE = 16
MESH = pl.DeviceIdType.MESH


def np_split(x):
    hi = x.astype(np.float32).astype(ml_dtypes.bfloat16)
    lo = (x - hi.astype(np.float64)).astype(np.float32).astype(ml_dtypes.bfloat16)
    return hi, lo


def pad_lanes(x, lanes=256):
    return np.pad(x, ((0, 0), (0, lanes - x.shape[1])))


@functools.lru_cache(maxsize=None)
def make_tables():
    kc = np.arange(COL_FREQS) - COL_FREQS // 2
    kr = np.arange(ROW_FREQS) - ROW_FREQS // 2
    x = np.arange(WIDTH)
    ang = 2 * np.pi * (np.outer(x, kc) % WIDTH) / WIDTH
    f_hi, f_lo = np_split(np.concatenate([np.cos(ang), -np.sin(ang)], 1) / math.sqrt(WIDTH))
    fwd = np.concatenate([f_hi, f_lo], 1)

    n = np.arange(GRID_COLS)
    step = WIDTH // GRID_COLS
    dist = (x[None, :] - step * n[:, None]) % WIDTH
    base = np.ones(WIDTH)
    for kap in range(1, COL_FREQS):
        base += 2 * np.cos(2 * np.pi * ((np.arange(WIDTH) * kap) % WIDTH) / WIDTH)
    g = (base / GRID_COLS)[dist]
    g = g[:, : WIDTH // 2]
    g_hi, g_lo = np_split(g)
    up = np.concatenate([g_hi.T, g_hi.T, g_lo.T], 1)
    down = np.concatenate([g_hi, g_lo], 0)

    ang = 2 * np.pi * (np.outer(kc, n) % GRID_COLS) / GRID_COLS
    c, s = np.cos(ang) / math.sqrt(WIDTH), np.sin(ang) / math.sqrt(WIDTH)
    inv = np.block([[c, s], [-s, c]])
    i_hi, i_lo = np_split(inv)
    inv3 = np.concatenate([i_hi, i_hi, i_lo], 0)
    t_hi, t_lo = np_split(inv.T)
    adj = np.concatenate([t_hi, t_lo], 1)

    e = np.arange(SLAB)
    ang = 2 * np.pi * (np.outer(kr, e) % EXT) / EXT
    a_hi, a_lo = np_split(np.concatenate([np.cos(ang), np.sin(ang)], 0) / math.sqrt(EXT))
    lt3 = np.concatenate([a_hi, a_hi, a_lo], 1)

    m = np.arange(GRID_ROWS)
    ang = 2 * np.pi * (np.outer(m, kr) % GRID_ROWS) / GRID_ROWS
    c, s = np.cos(ang) / math.sqrt(EXT), np.sin(ang) / math.sqrt(EXT)
    ag = np.block([[c, -s], [s, c]])
    hi, lo = np_split(ag)
    ag3 = np.concatenate([hi, hi, lo], 1)
    hi, lo = np_split(ag.T)
    agt3 = np.concatenate([np.concatenate([hi, hi], 1), np.concatenate([lo, lo], 1)], 0)

    rstep = EXT // GRID_ROWS
    dist = (e[:, None] - rstep * m[None, :]) % EXT
    base = np.ones(EXT)
    for rho in range(1, ROW_FREQS):
        base += 2 * np.cos(2 * np.pi * ((np.arange(EXT) * rho) % EXT) / EXT)
    r = (base / GRID_ROWS)[dist]
    hi, lo = np_split(r)
    r3 = np.concatenate([hi, hi, lo], 1)
    hi, lo = np_split(np.concatenate([r.T, r.T], 1))
    rt2 = np.concatenate([hi, lo], 1)

    tabs = np.concatenate(
        [inv3, adj, pad_lanes(lt3), pad_lanes(ag3), pad_lanes(agt3), pad_lanes(r3), rt2], 0
    )

    ang = 2 * np.pi * (kr % 3) / 3
    cr = np.tile(np.cos(ang), 2)
    ci = np.tile(np.sin(ang), 2)
    with np.errstate(invalid="ignore"):
        d = np.where(kc == 0, FRAG_LEN, np.sin(np.pi * FRAG_LEN * kc / WIDTH) / np.sin(np.pi * kc / WIDTH))
    d = d / math.sqrt(WIDTH)
    col = np.concatenate([cr, ci, d, -d])
    consts = np.repeat(col[:, None], 128, 1).astype(np.float32)
    return fwd, up, down, tabs, consts


def split(x):
    hi = x.astype(BF16)
    return hi, (x - hi.astype(F32)).astype(BF16)


def dot(a, b):
    return lax.dot_general(a, b, (((1,), (0,)), ((), ())), preferred_element_type=F32)


def dot_nt(a, b):
    return lax.dot_general(a, b, (((1,), (1,)), ((), ())), preferred_element_type=F32)


def table_dot(table3, x):
    hi, lo = split(x)
    return dot(table3, jnp.concatenate([hi, lo, hi], 0))


def with_halves_swapped(x):
    return pltpu.roll(x, 64, axis=1)


def column_rows(grids):
    i, d = grids[:, :128], grids[:, 128:]
    hi, lo = split(jnp.concatenate([i, with_halves_swapped(i), d, with_halves_swapped(d)], 0))
    return jnp.concatenate([hi, lo, hi], 1)


def weighted_back(full, target, down):
    w0, w1 = weighting(full[:, :128], full[:, 128:], target)
    hi, lo = split(jnp.concatenate([w0, w1], 1))
    both = dot(down, hi)
    return both[:128] + both[128:] + dot(down[:128], lo)


def weighted_grid(z, rt2):
    swapped = jnp.concatenate([z[64:], z[:64]], 0)
    low = (lax.broadcasted_iota(jnp.int32, z.shape, 1) & 64) == 0
    v = jnp.where(low, z, swapped)
    hi, lo = split(jnp.concatenate([v[:, :128], v[:, 128:]], 0))
    rt_hi, rt_lo = rt2[:, :128], rt2[:, 128:]
    return dot_nt(jnp.concatenate([rt_hi, rt_hi, rt_lo], 1), jnp.concatenate([hi, lo, hi], 1))


def sin_turns(u):
    y = u * (2.0 * math.pi)
    s = y * y
    p = jnp.full_like(s, -1.0 / 39916800.0)
    for coef in (1.0 / 362880.0, -1.0 / 5040.0, 1.0 / 120.0, -1.0 / 6.0):
        p = p * s + coef
    return y + y * (s * p)


def cos_turns(t):
    t = t - jnp.floor(t + 0.5)
    return sin_turns(0.25 - jnp.abs(t))


def times_i(z, sign):
    return pltpu.roll(z, 64, axis=1) * sign


def lane_sign(shape):
    lane = lax.broadcasted_iota(jnp.int32, shape, 1)
    return jnp.where(lane < 64, -1.0, 1.0).astype(F32)


def fragment_tables(rows, cols, dsc):
    kr = lax.broadcasted_iota(jnp.int32, (32, SLOTS), 0)
    is_sin = kr >= 16
    kr = ((kr & 15) - 8).astype(F32)
    t = kr * rows.astype(F32) * (1.0 / EXT)
    row_tab = cos_turns(t - jnp.where(is_sin, 0.25, 0.0)) * (1.0 / math.sqrt(EXT))
    kc = lax.broadcasted_iota(jnp.int32, (128, SLOTS), 0)
    is_sin = kc >= 64
    kc = ((kc & 63) - 32).astype(F32)
    t = kc * (2 * cols + (FRAG_LEN - 1)).astype(F32) * (1.0 / (2 * WIDTH))
    col_tab = cos_turns(t - jnp.where(is_sin, 0.25, 0.0)) * dsc
    return row_tab, col_tab


def own_modes(packed, row_tab, col_hi, col_lo, amp, lt3, sign):
    u0 = table_dot(lt3, packed)
    hi, lo = split(row_tab * amp)
    u1 = dot_nt(
        jnp.concatenate([hi, lo, hi], 1), jnp.concatenate([col_hi, col_hi, col_lo], 1)
    )
    u_re = jnp.concatenate([u0[:16], u1[:16]], 0)
    u_im = jnp.concatenate([u0[16:], u1[16:]], 0)
    return u_re - times_i(u_im, sign)


def combine(own, left, right, cr, ci, sign):
    return own + cr * (left + right) + ci * times_i(left - right, sign)


def two_forms(h, low):
    turned = pltpu.roll(h, 64, axis=1)
    return jnp.where(low, h, turned), jnp.where(low, turned, h)


def side_by_side(x, rows):
    return jnp.concatenate([x[i : i + rows] for i in range(0, x.shape[0], rows)], 1)


def forward_group(hrr, hii, modes, imodes, inv3):
    blocks = []
    for j in range(2):
        m, im = modes[16 * j : 16 * j + 16], imodes[16 * j : 16 * j + 16]
        blocks += [hrr[k] * m + hii[k] * im for k in range(hrr.shape[0])]
    hi, lo = split(jnp.concatenate(blocks, 0))
    return dot(jnp.concatenate([hi, lo, hi], 1), inv3)


def forward_rows(q, ag3):
    q_re, q_im = side_by_side(q[:, :128], 16), side_by_side(q[:, 128:], 16)
    return table_dot(ag3, jnp.concatenate([q_re, q_im], 0))


def intensity_terms(amps, kernels):
    total0 = total1 = None
    for k in range(kernels):
        a, b = amps[:, 128 * k : 128 * k + 128], amps[:, 128 * (kernels + k) : 128 * (kernels + k) + 128]
        s0, s1 = a * a, a * b
        total0 = s0 if total0 is None else total0 + s0
        total1 = s1 if total1 is None else total1 + s1
    return total0[:32] + total0[32:], total1[:32] + total1[32:]


def weighting(inten, change, target):
    developed = 1.0 / (1.0 + jnp.exp(-STEEP * (inten - THRESH)))
    steep = STEEP * developed * (1.0 - developed)
    return steep * (developed - target), steep * steep * change


def adjoint_rows(e0, w0, w1, agt3):
    kernels = e0.shape[1] // 128
    loads = []
    for w in (w0, w1):
        ww = jnp.concatenate([w, w], 0)
        loads += [ww * e0[:, 128 * k : 128 * k + 128] for k in range(kernels)]
    hi, lo = split(jnp.concatenate(loads, 1))
    u = dot(agt3, jnp.concatenate([hi, lo], 0))
    return u[:32] + u[32:]


def adjoint_columns(u, hrr, hii, adj):
    kernels = hrr.shape[0]
    rows = [
        jnp.concatenate([u[:16, 128 * b : 128 * b + 128], u[16:, 128 * b : 128 * b + 128]], 1)
        for b in range(2 * kernels)
    ]
    hi, lo = split(jnp.concatenate(rows, 0))
    both = dot(hi, adj)
    back = both[:, :128] + both[:, 128:] + dot(lo, adj[:, :128])
    first, second = [], []
    for j in range(2):
        f = s = None
        for k in range(kernels):
            at = 16 * (j * kernels + k)
            a, b = hrr[k] * back[at : at + 16], hii[k] * back[at : at + 16]
            f = a if f is None else f + a
            s = b if s is None else s + b
        first.append(f)
        second.append(s)
    return jnp.concatenate(first, 0), jnp.concatenate(second, 0)


def project(total, row_tab, col_hi, col_lo, sign):
    it = times_i(total, sign)
    lhs = jnp.concatenate([total[:16], it[:16], total[16:], it[16:]], 0)
    hi, lo = split(lhs)
    q = dot(jnp.concatenate([hi, lo, hi], 1), jnp.concatenate([col_hi, col_hi, col_lo], 0))
    return [jnp.sum(q[32 * j : 32 * j + 32] * row_tab, axis=0, keepdims=True) for j in range(2)]


def kernel(
    weights_hbm,
    counts_hbm,
    rows_hbm,
    cols_hbm,
    step_hbm,
    spectra_hbm,
    tabs_hbm,
    consts_hbm,
    mask_hbm,
    target_hbm,
    fwd_hbm,
    up_hbm,
    down_hbm,
    out_ref,
    weights_s,
    counts_s,
    rows_v,
    cols_v,
    step_v,
    spectra_v,
    tabs_v,
    consts_v,
    mask_v,
    target_v,
    fwd_v,
    up_v,
    down_v,
    h_v,
    e0_v,
    m_own,
    m_got,
    y_own,
    y_got,
    hrr_v,
    hii_v,
    turned_v,
    res_v,
    load_sem,
    h_send,
    h_recv,
    m_send,
    m_recv,
    y_send,
    y_recv,
    res_send,
    res_recv,
    go_sem,
    own_recv,
    far_sem,
):
    tile = lax.axis_index("tile")
    kern = lax.axis_index("kern")
    barrier = pltpu.get_barrier_semaphore()
    is_last = jnp.logical_and(lax.rem(tile, PLANE) == PLANE - 1, tile < TILES - 1)

    @pl.when(jnp.logical_and(is_last, kern == 1))
    def _():
        pl.semaphore_signal(
            barrier,
            inc=1,
            device_id={"tile": lax.max(tile - (PLANE - 2), 0), "kern": 1},
            device_id_type=MESH,
        )

    def depot_tile(t):
        return jnp.logical_and(lax.rem(t, PLANE) == 1, t < TILES - PLANE).astype(jnp.int32)

    def lead_of(t):
        return 3 - 2 * lax.rem(t, 2) - depot_tile(t)

    lead = lead_of(tile)
    is_lead = kern == lead
    others = [{"tile": tile, "kern": lax.rem(lead + d, KERN)} for d in (1, 2, 3)]
    before, after = lax.max(tile - 1, 0), lax.min(tile + 1, TILES - 1)
    sides = (
        (tile > 0, {"tile": before, "kern": lead_of(before)}),
        (tile < TILES - 1, {"tile": after, "kern": lead_of(after)}),
    )
    first = 1 - lax.min(lax.rem(tile, PLANE), 1)
    left_of_modes = {
        "tile": lax.max(tile - 1 - (PLANE - 2) * first, 0),
        "kern": lead_of(before) * (1 - first) + first,
    }
    is_first = jnp.logical_and(first == 1, tile > 0)
    has_depot = depot_tile(tile) == 1

    def far_of(t):
        base = 2 - 2 * (lead_of(t) // 2)
        return [{"tile": t, "kern": base + c} for c in range(2)]

    is_far = kern // 2 != lead // 2
    mate = {"tile": tile, "kern": lead + 1 - 2 * lax.rem(lead, 2)}
    is_depot = jnp.logical_and(has_depot, kern == 1)
    used = []

    def load(src, dst):
        copy = pltpu.make_async_copy(src, dst, load_sem.at[len(used)])
        used.append(copy)
        return copy

    early = [load(weights_hbm, weights_s), load(spectra_hbm, spectra_v)]
    mine = pl.multiple_of(kern * LOCAL, LOCAL)

    def scale_own():
        for copy in early:
            copy.wait()
        for k in range(LOCAL):
            scale = jnp.sqrt(jnp.full((ROW_FREQS, 128), weights_s[k] * (2.0 / KERNELS), F32))
            h_v[mine + k] = spectra_v[k] * scale

    def fragments():
        sign = lane_sign((32, 128))
        cr, ci = consts_v[0:32], consts_v[32:64]
        dsc = consts_v[64:192]
        row_tab, col_tab = fragment_tables(rows_v[...], cols_v[...], jnp.concatenate([dsc, dsc], 1))
        col_hi, col_lo = split(col_tab)
        active = lax.broadcasted_iota(jnp.int32, (1, SLOTS), 1) < counts_s[0]
        return sign, cr, ci, row_tab, col_hi, col_lo, active

    def finish(spectrum, sign, cr, ci, row_tab, col_hi, col_lo, active):
        whole = combine(spectrum, y_got[1], y_got[0], cr, ci, sign)
        outs = project(whole, row_tab, col_hi, col_lo, sign)
        for j in range(2):
            res_v[j : j + 1, :] = jnp.where(active, outs[j] * (1.0 / math.sqrt(FRAG_LEN)), 0.0)

    @pl.when(jnp.logical_not(is_lead))
    def _():
        lead_device = {"tile": tile, "kern": lead}
        small = [
            load(a, b)
            for a, b in (
                (counts_hbm, counts_s),
                (rows_hbm, rows_v),
                (cols_hbm, cols_v),
                (consts_hbm, consts_v),
            )
        ]

        @pl.when(is_far)
        def _():
            for d, (exists, _) in enumerate(sides):

                @pl.when(jnp.logical_not(exists))
                def _():
                    y_got[1 - d] = jnp.zeros((32, 128), F32)


        @pl.when(is_depot)
        def _():
            pl.semaphore_signal(
                barrier,
                inc=1,
                device_id={"tile": lax.min(tile + PLANE - 1, TILES - 1), "kern": 3},
                device_id_type=MESH,
            )
            pl.semaphore_signal(barrier, inc=1, device_id=lead_device, device_id_type=MESH)

        for copy in early:
            copy.start()
        scale_own()

        @pl.when(is_depot)
        def _():
            pl.semaphore_wait(go_sem, 1)

        @pl.when(jnp.logical_not(is_depot))
        def _():
            pl.semaphore_wait(barrier, 1)

        place = lax.rem(kern - lead + KERN, KERN) - 1
        copy = pltpu.make_async_remote_copy(
            src_ref=h_v.at[pl.ds(mine, LOCAL)],
            dst_ref=h_v.at[pl.ds(mine, LOCAL)],
            send_sem=h_send.at[0],
            recv_sem=h_recv.at[place],
            device_id=lead_device,
            device_id_type=MESH,
        )
        copy.start()

        @pl.when(is_depot)
        def _():
            pl.semaphore_wait(barrier, 1)
            onward = pltpu.make_async_remote_copy(
                src_ref=m_got.at[0],
                dst_ref=m_got.at[0],
                send_sem=m_send.at[0],
                recv_sem=m_recv.at[0],
                device_id={"tile": lax.min(tile + PLANE - 2, TILES - 1), "kern": 1},
                device_id_type=MESH,
            )
            onward.wait_recv()
            onward.start()
            pl.semaphore_wait(far_sem.at[0], 1)
            pl.semaphore_signal(
                far_sem.at[0],
                inc=1,
                device_id={"tile": lax.min(tile + PLANE - 2, TILES - 1), "kern": 1},
                device_id_type=MESH,
            )
            onward.wait_send()

        @pl.when(jnp.logical_not(is_far))
        def _():
            pltpu.make_async_remote_copy(
                src_ref=res_v,
                dst_ref=res_v,
                send_sem=res_send.at[0],
                recv_sem=res_recv.at[0],
                device_id=lead_device,
                device_id_type=MESH,
            ).wait_recv()

        @pl.when(is_far)
        def _():
            for load_copy in small:
                load_copy.start()
            for load_copy in small:
                load_copy.wait()
            sign, cr, ci, row_tab, col_hi, col_lo, active = fragments()
            for d, (exists, _) in enumerate(sides):

                @pl.when(exists)
                def _():
                    pltpu.make_async_remote_copy(
                        src_ref=y_own,
                        dst_ref=y_got.at[1 - d],
                        send_sem=y_send.at[0],
                        recv_sem=y_recv.at[1 - d],
                        device_id=lead_device,
                        device_id_type=MESH,
                    ).wait_recv()

            pltpu.make_async_remote_copy(
                src_ref=y_own,
                dst_ref=y_own,
                send_sem=y_send.at[0],
                recv_sem=own_recv.at[0],
                device_id=lead_device,
                device_id_type=MESH,
            ).wait_recv()
            finish(y_own[...], sign, cr, ci, row_tab, col_hi, col_lo, active)

        copy.wait_send()

    @pl.when(is_lead)
    def _():
        for d, (exists, _) in enumerate(sides):

            @pl.when(jnp.logical_not(exists))
            def _():
                m_got[1 - d] = jnp.zeros((32, 128), F32)
                y_got[1 - d] = jnp.zeros((32, 128), F32)

        @pl.when(jnp.logical_not(has_depot))
        def _():
            pl.semaphore_signal(barrier, inc=1, device_id=others[0], device_id_type=MESH)

        for device in others[1:]:
            pl.semaphore_signal(barrier, inc=1, device_id=device, device_id_type=MESH)

        for exists, device in (sides[0], (jnp.logical_and(sides[1][0], jnp.logical_not(is_last)), sides[1][1])):

            @pl.when(exists)
            def _():
                pl.semaphore_signal(barrier, inc=1, device_id=device, device_id_type=MESH)

        width = WIDTH // CHUNKS
        small = [
            load(a, b)
            for a, b in (
                (counts_hbm, counts_s),
                (rows_hbm, rows_v),
                (cols_hbm, cols_v),
                (step_hbm, step_v),
                (consts_hbm, consts_v),
                (tabs_hbm, tabs_v),
            )
        ]
        parts = [pl.ds(c * width, width) for c in range(CHUNKS)]
        mask_copies = [load(mask_hbm.at[:, p], mask_v.at[:, p]) for p in parts]
        fwd_copies = [load(fwd_hbm.at[p, :], fwd_v.at[p, :]) for p in parts]
        later = [load(up_hbm, up_v), load(target_hbm, target_v), load(down_hbm, down_v)]
        for copy in small:
            copy.start()
        for a, b in zip(mask_copies, fwd_copies):
            a.start()
            b.start()
        for copy in early + later:
            copy.start()

        for copy in small:
            copy.wait()
        sign, cr, ci, row_tab, col_hi, col_lo, active = fragments()
        amp = jnp.where(active, step_v[...], 0.0) * (1.0 / math.sqrt(FRAG_LEN))

        total = jnp.zeros((2 * SLAB, 256), F32)
        for c in range(CHUNKS):
            mask_copies[c].wait()
            fwd_copies[c].wait()
            hi, lo = split(mask_v[:, c * width : (c + 1) * width])
            total += dot(jnp.concatenate([hi, lo], 0), fwd_v[c * width : (c + 1) * width, :])
        packed = total[:SLAB, :128] + total[:SLAB, 128:] + total[SLAB:, :128]
        modes_own = own_modes(packed, row_tab, col_hi, col_lo, amp, tabs_v[640:672, :192], sign)
        m_own[...] = modes_own

        def exchange(own, got, send, recv, devices):
            copies = [
                pltpu.make_async_remote_copy(
                    src_ref=own,
                    dst_ref=got.at[d],
                    send_sem=send.at[d],
                    recv_sem=recv.at[d],
                    device_id=device,
                    device_id_type=MESH,
                )
                for d, device in enumerate(devices)
            ]
            for d, (exists, _) in enumerate(sides):

                @pl.when(exists)
                def _():
                    copies[d].start()

            return copies

        def arrived(copies):
            for d, (exists, _) in enumerate(sides):

                @pl.when(exists)
                def _():
                    copies[1 - d].wait_recv()

        def sent(copies):
            for d, (exists, _) in enumerate(sides):

                @pl.when(exists)
                def _():
                    copies[d].wait_send()

        pl.semaphore_wait(
            barrier, lax.min(tile, 1) + lax.min(TILES - 1 - tile, 1) + depot_tile(tile)
        )

        @pl.when(has_depot)
        def _():
            pl.semaphore_signal(go_sem, inc=1, device_id=others[0], device_id_type=MESH)

        m_copies = exchange(m_own, m_got, m_send, m_recv, (left_of_modes, sides[1][1]))

        scale_own()
        low = lax.broadcasted_iota(jnp.int32, (ROW_FREQS, 128), 1) < 64

        def spectra_from(d):
            at = pl.multiple_of(lax.rem(lead + d, KERN) * LOCAL, LOCAL)
            return pltpu.make_async_remote_copy(
                src_ref=h_v.at[pl.ds(at, LOCAL)],
                dst_ref=h_v.at[pl.ds(at, LOCAL)],
                send_sem=h_send.at[0],
                recv_sem=h_recv.at[d - 1],
                device_id=others[0],
                device_id_type=MESH,
            )

        def far_is_here(d):
            pl.semaphore_signal(
                far_sem.at[d],
                inc=1,
                device_id=(left_of_modes, sides[1][1])[d],
                device_id_type=MESH,
            )

        @pl.when(is_first)
        def _():
            for d in (1, 2, 3):
                spectra_from(d).wait_recv()
            far_is_here(0)

        def take(place, d):
            at = pl.multiple_of(lax.rem(lead + d, KERN) * LOCAL, LOCAL)
            if d > 0:

                @pl.when(jnp.logical_not(is_first))
                def _():
                    spectra_from(d).wait_recv()

            for k in range(LOCAL):
                a, b = two_forms(h_v[at + k], low)
                hrr_v[place * LOCAL + k] = a
                hii_v[place * LOCAL + k] = b

        take(0, 0)
        take(1, 3)

        def forms(g):
            ks = pl.ds(g * GROUP, GROUP)
            return hrr_v[ks], hii_v[ks]

        for copy in later:
            copy.wait()
        for c in range(8):
            ends = [target_v[:, h + 128 * c : h + 128 * c + 128] for h in (0, WIDTH // 2)]
            turned_v[128 * c : 128 * c + 128, :] = jnp.transpose(jnp.concatenate(ends, 0))
        take(2, 2)
        arrived(m_copies)
        modes = combine(modes_own, m_got[1], m_got[0], cr, ci, sign)
        imodes = times_i(modes, sign)

        inten = change = jnp.zeros((GRID_ROWS, 128), F32)
        n = KERNELS // GROUP
        ready = []
        for g in range(n + AHEAD):
            if g == max(3 * n // 4, 1):
                take(3, 1)

                @pl.when(jnp.logical_and(sides[0][0], jnp.logical_not(is_first)))
                def _():
                    far_is_here(0)

                @pl.when(sides[1][0])
                def _():
                    far_is_here(1)

            if g < n:
                hrr, hii = forms(g)
                ready.append(forward_group(hrr, hii, modes, imodes, tabs_v[0:384, :]))
            if g >= AHEAD:
                amps = forward_rows(ready[g - AHEAD], tabs_v[672:736, :96])
                e0_v[g - AHEAD] = amps[:, : 128 * GROUP]
                s0, s1 = intensity_terms(amps, GROUP)
                inten, change = inten + s0, change + s1

        grids = table_dot(tabs_v[800:864, :96], jnp.concatenate([0.5 * inten, change], 1))
        rows3 = column_rows(grids)

        n = WIDTH // 2 // SPAN
        parts = [slice(c * SPAN, (c + 1) * SPAN) for c in range(n)]
        total = jnp.zeros((128, 256), F32)
        full = dot_nt(up_v[parts[0], :], rows3)
        for c in range(n):
            ahead = dot_nt(up_v[parts[c + 1], :], rows3) if c + 1 < n else None
            total += weighted_back(full, turned_v[parts[c], :], down_v[:, parts[c]])
            full = ahead
        wgrid = weighted_grid(total, tabs_v[864:896, :])
        w0, w1 = wgrid[:, :128], wgrid[:, 128:]

        first = second = jnp.zeros((32, 128), F32)
        ready = []
        n = KERNELS // AGROUP
        for g in range(n + AAHEAD):
            if g < n:
                e0 = e0_v[g * AGROUP // GROUP, :, pl.ds(g * AGROUP % GROUP * 128, AGROUP * 128)]
                ready.append(adjoint_rows(e0, w0, w1, tabs_v[736:800, :128]))
            if g >= AAHEAD:
                ks = pl.ds((g - AAHEAD) * AGROUP, AGROUP)
                a, b = adjoint_columns(ready[g - AAHEAD], hrr_v[ks], hii_v[ks], tabs_v[384:640, :])
                first, second = first + a, second + b
        spectrum = first - times_i(second, sign)
        y_own[...] = spectrum

        def send_own(i, device, d=None):
            return pltpu.make_async_remote_copy(
                src_ref=y_own,
                dst_ref=y_own if d is None else y_got.at[d],
                send_sem=y_send.at[i],
                recv_sem=own_recv.at[0] if d is None else y_recv.at[d],
                device_id=device,
                device_id_type=MESH,
            )

        y_copies = [send_own(d, sides[d][1], d) for d in range(2)]
        own_copies = [send_own(2 + c, device) for c, device in enumerate(far_of(tile))]
        far_copies = [
            [send_own(4 + 2 * d + c, device, d) for c, device in enumerate(far_of(t))]
            for d, t in enumerate((before, after))
        ]
        for d in (1, 0):

            @pl.when(sides[d][0])
            def _():
                pl.semaphore_wait(far_sem.at[1 - d], 1)
                for copy in reversed(far_copies[d]):
                    copy.start()
                y_copies[d].start()

            if d == 1:
                for copy in own_copies:
                    copy.start()

        arrived(y_copies)
        finish(spectrum, sign, cr, ci, row_tab, col_hi, col_lo, active)
        res_copy = pltpu.make_async_remote_copy(
            src_ref=res_v,
            dst_ref=res_v,
            send_sem=res_send.at[0],
            recv_sem=res_recv.at[0],
            device_id=mate,
            device_id_type=MESH,
        )
        res_copy.start()
        sent(m_copies)
        sent(y_copies)
        for copy in own_copies:
            copy.wait_send()
        for d in range(2):

            @pl.when(sides[d][0])
            def _():
                for copy in far_copies[d]:
                    copy.wait_send()

        res_copy.wait_send()

    out_ref[...] = res_v[...]


def shards(mask, target, spectra, weights, counts, frag_rows, frag_cols, step):
    fwd, up, down, tabs, consts = make_tables()
    vmem = pl.BlockSpec(memory_space=pltpu.VMEM)
    hbm = pl.BlockSpec(memory_space=pltpu.HBM)
    dma = pltpu.SemaphoreType.DMA
    outs = pl.pallas_call(
        kernel,
        out_shape=pltpu.VMEM((2, SLOTS), F32),
        in_specs=[hbm] * 13,
        out_specs=vmem,
        scratch_shapes=[
            pltpu.SMEM((LOCAL,), F32),
            pltpu.SMEM((1,), jnp.int32),
            pltpu.VMEM((1, SLOTS), jnp.int32),
            pltpu.VMEM((1, SLOTS), jnp.int32),
            pltpu.VMEM((1, SLOTS), F32),
            pltpu.VMEM((LOCAL, ROW_FREQS, 128), F32),
            pltpu.VMEM(tabs.shape, BF16),
            pltpu.VMEM(consts.shape, F32),
            pltpu.VMEM((SLAB, WIDTH), F32),
            pltpu.VMEM((SLAB, WIDTH), F32),
            pltpu.VMEM((WIDTH, 256), BF16),
            pltpu.VMEM(up.shape, BF16),
            pltpu.VMEM(down.shape, BF16),
            pltpu.VMEM((KERNELS, ROW_FREQS, 128), F32),
            pltpu.VMEM((KERNELS // GROUP, 2 * GRID_ROWS, 128 * GROUP), F32),
            pltpu.VMEM((32, 128), F32),
            pltpu.VMEM((2, 32, 128), F32),
            pltpu.VMEM((32, 128), F32),
            pltpu.VMEM((2, 32, 128), F32),
            pltpu.VMEM((KERNELS, ROW_FREQS, 128), F32),
            pltpu.VMEM((KERNELS, ROW_FREQS, 128), F32),
            pltpu.VMEM((WIDTH // 2, 128), F32),
            pltpu.VMEM((2, SLOTS), F32),
            dma((2 * CHUNKS + 15,)),
            dma((1,)),
            dma((3,)),
            dma((2,)),
            dma((2,)),
            dma((8,)),
            dma((2,)),
            dma((1,)),
            dma((1,)),
            pltpu.SemaphoreType.REGULAR,
            dma((1,)),
            pltpu.SemaphoreType.REGULAR((2,)),
        ],
        compiler_params=pltpu.CompilerParams(
            collective_id=0, has_side_effects=True, vmem_limit_bytes=60 * 1024 * 1024
        ),
    )(
        weights,
        counts,
        frag_rows.reshape(1, SLOTS),
        frag_cols.reshape(1, SLOTS),
        step.reshape(1, SLOTS),
        spectra,
        jnp.asarray(tabs),
        jnp.asarray(consts),
        mask,
        target,
        jnp.asarray(fwd),
        jnp.asarray(up),
        jnp.asarray(down),
    )
    return outs[0], outs[1]


def solution(mesh):
    return jax.shard_map(
        shards,
        mesh=mesh,
        in_specs=(
            P("tile", None),
            P("tile", None),
            P("kern", None, None),
            P("kern"),
            P("tile"),
            P("tile"),
            P("tile"),
            P("tile"),
        ),
        out_specs=(P("tile"), P("tile")),
        check_vma=False,
    )
```

```python
import functools
import math

import jax
import jax.numpy as jnp
import ml_dtypes
import numpy as np
from jax import lax
from jax.experimental import pallas as pl
from jax.experimental.pallas import tpu as pltpu
from jax.sharding import PartitionSpec as P

WIDTH = 2048
COL_FREQS = 64
ROW_FREQS = 16
KERNELS = 24
FRAG_LEN = 32
SLAB = 64
SLOTS = 256
EXT = 192
TILES = 64
KERN = 4
LOCAL = KERNELS // KERN
GRID_ROWS = 32
GRID_COLS = 128
STEEP = 10.0
THRESH = 0.1
F32 = jnp.float32
BF16 = jnp.bfloat16
CHUNKS = 1
GROUP = 8
SPAN = 256
AHEAD = 1
AGROUP = 8
AAHEAD = 1
PLANE = 16
MESH = pl.DeviceIdType.MESH


def np_split(x):
    hi = x.astype(np.float32).astype(ml_dtypes.bfloat16)
    lo = (x - hi.astype(np.float64)).astype(np.float32).astype(ml_dtypes.bfloat16)
    return hi, lo


def pad_lanes(x, lanes=256):
    return np.pad(x, ((0, 0), (0, lanes - x.shape[1])))


@functools.lru_cache(maxsize=None)
def make_tables():
    kc = np.arange(COL_FREQS) - COL_FREQS // 2
    kr = np.arange(ROW_FREQS) - ROW_FREQS // 2
    x = np.arange(WIDTH)
    ang = 2 * np.pi * (np.outer(x, kc) % WIDTH) / WIDTH
    f_hi, f_lo = np_split(np.concatenate([np.cos(ang), -np.sin(ang)], 1) / math.sqrt(WIDTH))
    fwd = np.concatenate([f_hi, f_lo], 1)

    n = np.arange(GRID_COLS)
    step = WIDTH // GRID_COLS
    dist = (x[None, :] - step * n[:, None]) % WIDTH
    base = np.ones(WIDTH)
    for kap in range(1, COL_FREQS):
        base += 2 * np.cos(2 * np.pi * ((np.arange(WIDTH) * kap) % WIDTH) / WIDTH)
    g = (base / GRID_COLS)[dist]
    g = g[:, : WIDTH // 2]
    g_hi, g_lo = np_split(g)
    up = np.concatenate([g_hi.T, g_hi.T, g_lo.T], 1)
    down = np.concatenate([g_hi, g_lo], 0)

    ang = 2 * np.pi * (np.outer(kc, n) % GRID_COLS) / GRID_COLS
    c, s = np.cos(ang) / math.sqrt(WIDTH), np.sin(ang) / math.sqrt(WIDTH)
    inv = np.block([[c, s], [-s, c]])
    i_hi, i_lo = np_split(inv)
    inv3 = np.concatenate([i_hi, i_hi, i_lo], 0)
    t_hi, t_lo = np_split(inv.T)
    adj = np.concatenate([t_hi, t_lo], 1)

    e = np.arange(SLAB)
    ang = 2 * np.pi * (np.outer(kr, e) % EXT) / EXT
    a_hi, a_lo = np_split(np.concatenate([np.cos(ang), np.sin(ang)], 0) / math.sqrt(EXT))
    lt3 = np.concatenate([a_hi, a_hi, a_lo], 1)

    m = np.arange(GRID_ROWS)
    ang = 2 * np.pi * (np.outer(m, kr) % GRID_ROWS) / GRID_ROWS
    c, s = np.cos(ang) / math.sqrt(EXT), np.sin(ang) / math.sqrt(EXT)
    ag = np.block([[c, -s], [s, c]])
    hi, lo = np_split(ag)
    ag3 = np.concatenate([hi, hi, lo], 1)
    hi, lo = np_split(ag.T)
    agt3 = np.concatenate([np.concatenate([hi, hi], 1), np.concatenate([lo, lo], 1)], 0)

    rstep = EXT // GRID_ROWS
    dist = (e[:, None] - rstep * m[None, :]) % EXT
    base = np.ones(EXT)
    for rho in range(1, ROW_FREQS):
        base += 2 * np.cos(2 * np.pi * ((np.arange(EXT) * rho) % EXT) / EXT)
    r = (base / GRID_ROWS)[dist]
    hi, lo = np_split(r)
    r3 = np.concatenate([hi, hi, lo], 1)
    hi, lo = np_split(np.concatenate([r.T, r.T], 1))
    rt2 = np.concatenate([hi, lo], 1)

    tabs = np.concatenate(
        [inv3, adj, pad_lanes(lt3), pad_lanes(ag3), pad_lanes(agt3), pad_lanes(r3), rt2], 0
    )

    ang = 2 * np.pi * (kr % 3) / 3
    cr = np.tile(np.cos(ang), 2)
    ci = np.tile(np.sin(ang), 2)
    with np.errstate(invalid="ignore"):
        d = np.where(kc == 0, FRAG_LEN, np.sin(np.pi * FRAG_LEN * kc / WIDTH) / np.sin(np.pi * kc / WIDTH))
    d = d / math.sqrt(WIDTH)
    col = np.concatenate([cr, ci, d, -d])
    consts = np.repeat(col[:, None], 128, 1).astype(np.float32)
    return fwd, up, down, tabs, consts


def split(x):
    hi = x.astype(BF16)
    return hi, (x - hi.astype(F32)).astype(BF16)


def dot(a, b):
    return lax.dot_general(a, b, (((1,), (0,)), ((), ())), preferred_element_type=F32)


def dot_nt(a, b):
    return lax.dot_general(a, b, (((1,), (1,)), ((), ())), preferred_element_type=F32)


def table_dot(table3, x):
    hi, lo = split(x)
    return dot(table3, jnp.concatenate([hi, lo, hi], 0))


def with_halves_swapped(x):
    return pltpu.roll(x, 64, axis=1)


def column_rows(grids):
    i, d = grids[:, :128], grids[:, 128:]
    hi, lo = split(jnp.concatenate([i, with_halves_swapped(i), d, with_halves_swapped(d)], 0))
    return jnp.concatenate([hi, lo, hi], 1)


def weighted_back(full, target, down):
    w0, w1 = weighting(full[:, :128], full[:, 128:], target)
    hi, lo = split(jnp.concatenate([w0, w1], 1))
    both = dot(down, hi)
    return both[:128] + both[128:] + dot(down[:128], lo)


def weighted_grid(z, rt2):
    swapped = jnp.concatenate([z[64:], z[:64]], 0)
    low = (lax.broadcasted_iota(jnp.int32, z.shape, 1) & 64) == 0
    v = jnp.where(low, z, swapped)
    hi, lo = split(jnp.concatenate([v[:, :128], v[:, 128:]], 0))
    rt_hi, rt_lo = rt2[:, :128], rt2[:, 128:]
    return dot_nt(jnp.concatenate([rt_hi, rt_hi, rt_lo], 1), jnp.concatenate([hi, lo, hi], 1))


def sin_turns(u):
    y = u * (2.0 * math.pi)
    s = y * y
    p = jnp.full_like(s, -1.0 / 39916800.0)
    for coef in (1.0 / 362880.0, -1.0 / 5040.0, 1.0 / 120.0, -1.0 / 6.0):
        p = p * s + coef
    return y + y * (s * p)


def cos_turns(t):
    t = t - jnp.floor(t + 0.5)
    return sin_turns(0.25 - jnp.abs(t))


def times_i(z, sign):
    return pltpu.roll(z, 64, axis=1) * sign


def lane_sign(shape):
    lane = lax.broadcasted_iota(jnp.int32, shape, 1)
    return jnp.where(lane < 64, -1.0, 1.0).astype(F32)


def fragment_tables(rows, cols, dsc):
    kr = lax.broadcasted_iota(jnp.int32, (32, SLOTS), 0)
    is_sin = kr >= 16
    kr = ((kr & 15) - 8).astype(F32)
    t = kr * rows.astype(F32) * (1.0 / EXT)
    row_tab = cos_turns(t - jnp.where(is_sin, 0.25, 0.0)) * (1.0 / math.sqrt(EXT))
    kc = lax.broadcasted_iota(jnp.int32, (128, SLOTS), 0)
    is_sin = kc >= 64
    kc = ((kc & 63) - 32).astype(F32)
    t = kc * (2 * cols + (FRAG_LEN - 1)).astype(F32) * (1.0 / (2 * WIDTH))
    col_tab = cos_turns(t - jnp.where(is_sin, 0.25, 0.0)) * dsc
    return row_tab, col_tab


def own_modes(packed, row_tab, col_hi, col_lo, amp, lt3, sign):
    u0 = table_dot(lt3, packed)
    hi, lo = split(row_tab * amp)
    u1 = dot_nt(
        jnp.concatenate([hi, lo, hi], 1), jnp.concatenate([col_hi, col_hi, col_lo], 1)
    )
    u_re = jnp.concatenate([u0[:16], u1[:16]], 0)
    u_im = jnp.concatenate([u0[16:], u1[16:]], 0)
    return u_re - times_i(u_im, sign)


def combine(own, left, right, cr, ci, sign):
    both, odd = left + right, left - right
    return (
        own + cr * both + ci * times_i(odd, sign),
        times_i(own, sign) + cr * times_i(both, sign) - ci * odd,
    )


def two_forms(h, low):
    turned = pltpu.roll(h, 64, axis=1)
    return jnp.where(low, h, turned), jnp.where(low, turned, h)


def side_by_side(x, rows):
    return jnp.concatenate([x[i : i + rows] for i in range(0, x.shape[0], rows)], 1)


def forward_group(hrr, hii, modes, imodes, inv3):
    blocks = []
    for j in range(2):
        m, im = modes[16 * j : 16 * j + 16], imodes[16 * j : 16 * j + 16]
        blocks += [hrr[k] * m + hii[k] * im for k in range(hrr.shape[0])]
    hi, lo = split(jnp.concatenate(blocks, 0))
    return dot(jnp.concatenate([hi, lo, hi], 1), inv3)


def forward_rows(q, ag3):
    q_re, q_im = side_by_side(q[:, :128], 16), side_by_side(q[:, 128:], 16)
    return table_dot(ag3, jnp.concatenate([q_re, q_im], 0))


def intensity_terms(amps, kernels):
    total0 = total1 = None
    for k in range(kernels):
        a, b = amps[:, 128 * k : 128 * k + 128], amps[:, 128 * (kernels + k) : 128 * (kernels + k) + 128]
        s0, s1 = a * a, a * b
        total0 = s0 if total0 is None else total0 + s0
        total1 = s1 if total1 is None else total1 + s1
    return total0[:32] + total0[32:], total1[:32] + total1[32:]


def weighting(inten, change, target):
    developed = 1.0 / (1.0 + jnp.exp(-STEEP * (inten - THRESH)))
    steep = STEEP * developed * (1.0 - developed)
    return steep * (developed - target), steep * steep * change


def adjoint_rows(e0, w0, w1, agt3):
    kernels = e0.shape[1] // 128
    loads = []
    for w in (w0, w1):
        ww = jnp.concatenate([w, w], 0)
        loads += [ww * e0[:, 128 * k : 128 * k + 128] for k in range(kernels)]
    hi, lo = split(jnp.concatenate(loads, 1))
    u = dot(agt3, jnp.concatenate([hi, lo], 0))
    return u[:32] + u[32:]


def adjoint_columns(u, hrr, hii, adj):
    kernels = hrr.shape[0]
    rows = [
        jnp.concatenate([u[:16, 128 * b : 128 * b + 128], u[16:, 128 * b : 128 * b + 128]], 1)
        for b in range(2 * kernels)
    ]
    hi, lo = split(jnp.concatenate(rows, 0))
    both = dot(hi, adj)
    back = both[:, :128] + both[:, 128:] + dot(lo, adj[:, :128])
    first, second = [], []
    for j in range(2):
        f = s = None
        for k in range(kernels):
            at = 16 * (j * kernels + k)
            a, b = hrr[k] * back[at : at + 16], hii[k] * back[at : at + 16]
            f = a if f is None else f + a
            s = b if s is None else s + b
        first.append(f)
        second.append(s)
    return jnp.concatenate(first, 0), jnp.concatenate(second, 0)


def project(total, it, row_tab, col_hi, col_lo):
    lhs = jnp.concatenate([total[:16], it[:16], total[16:], it[16:]], 0)
    hi, lo = split(lhs)
    q = dot(jnp.concatenate([hi, lo, hi], 1), jnp.concatenate([col_hi, col_hi, col_lo], 0))
    return [jnp.sum(q[32 * j : 32 * j + 32] * row_tab, axis=0, keepdims=True) for j in range(2)]


def kernel(
    weights_hbm,
    counts_s,
    rows_hbm,
    cols_hbm,
    step_hbm,
    spectra_hbm,
    tabs_hbm,
    consts_hbm,
    mask_hbm,
    target_hbm,
    fwd_hbm,
    up_hbm,
    down_hbm,
    out_ref,
    weights_s,
    rows_v,
    cols_v,
    step_v,
    spectra_v,
    tabs_v,
    consts_v,
    mask_v,
    target_v,
    fwd_v,
    up_v,
    down_v,
    h_v,
    e0_v,
    m_own,
    m_got,
    y_own,
    y_got,
    hrr_v,
    hii_v,
    turned_v,
    res_v,
    load_sem,
    h_recv,
    m_recv,
    y_recv,
    far_sem,
):
    tile = lax.axis_index("tile")
    kern = lax.axis_index("kern")
    barrier = pltpu.get_barrier_semaphore()
    is_last = jnp.logical_and(lax.rem(tile, PLANE) == PLANE - 1, tile < TILES - 1)

    @pl.when(jnp.logical_and(is_last, kern == 1))
    def _():
        pl.semaphore_signal(
            barrier,
            inc=1,
            device_id={"tile": lax.max(tile - (PLANE - 2), 0), "kern": 1},
            device_id_type=MESH,
        )

    def depot_tile(t):
        return jnp.logical_and(lax.rem(t, PLANE) == 1, t < TILES - PLANE).astype(jnp.int32)

    def lead_of(t):
        return 3 - 2 * lax.rem(t, 2) - depot_tile(t)

    lead = lead_of(tile)
    is_lead = kern == lead
    others = [{"tile": tile, "kern": lax.rem(lead + d, KERN)} for d in (1, 2, 3)]
    before, after = lax.max(tile - 1, 0), lax.min(tile + 1, TILES - 1)
    sides = (
        (tile > 0, {"tile": before, "kern": lead_of(before)}),
        (tile < TILES - 1, {"tile": after, "kern": lead_of(after)}),
    )
    first = 1 - lax.min(lax.rem(tile, PLANE), 1)
    left_of_modes = {
        "tile": lax.max(tile - 1 - (PLANE - 2) * first, 0),
        "kern": lead_of(before) * (1 - first) + first,
    }
    is_first = jnp.logical_and(first == 1, tile > 0)
    has_depot = depot_tile(tile) == 1

    def far_of(t):
        base = 2 - 2 * (lead_of(t) // 2)
        return [{"tile": t, "kern": base + c} for c in range(2)]

    is_far = kern // 2 != lead // 2
    mate = {"tile": tile, "kern": lead + 1 - 2 * lax.rem(lead, 2)}
    is_depot = jnp.logical_and(has_depot, kern == 1)
    used = []

    def load(src, dst):
        copy = pltpu.make_async_copy(src, dst, load_sem.at[len(used)])
        used.append(copy)
        return copy

    early = [load(weights_hbm, weights_s), load(spectra_hbm, spectra_v)]
    mine = pl.multiple_of(kern * LOCAL, LOCAL)

    def scale_own():
        for copy in early:
            copy.wait()
        for k in range(LOCAL):
            scale = jnp.sqrt(jnp.full((ROW_FREQS, 128), weights_s[k] * (2.0 / KERNELS), F32))
            h_v[mine + k] = spectra_v[k] * scale

    def fragments():
        sign = lane_sign((32, 128))
        cr, ci = consts_v[0:32], consts_v[32:64]
        dsc = consts_v[64:192]
        row_tab, col_tab = fragment_tables(rows_v[...], cols_v[...], jnp.concatenate([dsc, dsc], 1))
        col_hi, col_lo = split(col_tab)
        active = lax.broadcasted_iota(jnp.int32, (1, SLOTS), 1) < counts_s[0]
        return sign, cr, ci, row_tab, col_hi, col_lo, active

    def finish(spectrum, sign, cr, ci, row_tab, col_hi, col_lo, active):
        whole = combine(spectrum, y_got[1], y_got[0], cr, ci, sign)
        outs = project(*whole, row_tab, col_hi, col_lo)
        for j in range(2):
            res_v[j : j + 1, :] = jnp.where(active, outs[j] * (1.0 / math.sqrt(FRAG_LEN)), 0.0)

    @pl.when(jnp.logical_not(is_lead))
    def _():
        lead_device = {"tile": tile, "kern": lead}
        small = [
            load(a, b)
            for a, b in (
                (rows_hbm, rows_v),
                (cols_hbm, cols_v),
                (consts_hbm, consts_v),
            )
        ]

        @pl.when(is_far)
        def _():
            for d, (exists, _) in enumerate(sides):

                @pl.when(jnp.logical_not(exists))
                def _():
                    y_got[1 - d] = jnp.zeros((32, 128), F32)


        @pl.when(is_depot)
        def _():
            pl.semaphore_signal(
                barrier,
                inc=1,
                device_id={"tile": lax.min(tile + PLANE - 1, TILES - 1), "kern": 3},
                device_id_type=MESH,
            )
            pl.semaphore_signal(barrier, inc=1, device_id=lead_device, device_id_type=MESH)

        for copy in early:
            copy.start()
        scale_own()

        @pl.when(is_depot)
        def _():
            pl.semaphore_wait(far_sem.at[1], 1)

        @pl.when(jnp.logical_not(is_depot))
        def _():
            pl.semaphore_wait(barrier, 1)

        place = lax.rem(kern - lead + KERN, KERN) - 1
        copy = pltpu.make_async_remote_copy(
            src_ref=h_v.at[pl.ds(mine, LOCAL)],
            dst_ref=h_v.at[pl.ds(mine, LOCAL)],
            send_sem=load_sem.at[5],
            recv_sem=h_recv.at[place],
            device_id=lead_device,
            device_id_type=MESH,
        )
        copy.start()

        @pl.when(is_depot)
        def _():
            pl.semaphore_wait(barrier, 1)
            onward = pltpu.make_async_remote_copy(
                src_ref=m_got.at[0],
                dst_ref=m_got.at[0],
                send_sem=load_sem.at[6],
                recv_sem=m_recv.at[0],
                device_id={"tile": lax.min(tile + PLANE - 2, TILES - 1), "kern": 1},
                device_id_type=MESH,
            )
            onward.wait_recv()
            onward.start()
            pl.semaphore_wait(far_sem.at[0], 1)
            pl.semaphore_signal(
                far_sem.at[0],
                inc=1,
                device_id={"tile": lax.min(tile + PLANE - 2, TILES - 1), "kern": 1},
                device_id_type=MESH,
            )
            onward.wait_send()

        @pl.when(jnp.logical_not(is_far))
        def _():
            pltpu.make_async_remote_copy(
                src_ref=res_v,
                dst_ref=res_v,
                send_sem=load_sem.at[0],
                recv_sem=h_recv.at[0],
                device_id=lead_device,
                device_id_type=MESH,
            ).wait_recv()

        @pl.when(is_far)
        def _():
            for load_copy in small:
                load_copy.start()
            for load_copy in small:
                load_copy.wait()
            sign, cr, ci, row_tab, col_hi, col_lo, active = fragments()
            for d, (exists, _) in enumerate(sides):

                @pl.when(exists)
                def _():
                    pltpu.make_async_remote_copy(
                        src_ref=y_own,
                        dst_ref=y_got.at[1 - d],
                        send_sem=load_sem.at[0],
                        recv_sem=y_recv.at[1 - d],
                        device_id=lead_device,
                        device_id_type=MESH,
                    ).wait_recv()

            pltpu.make_async_remote_copy(
                src_ref=y_own,
                dst_ref=y_own,
                send_sem=load_sem.at[0],
                recv_sem=h_recv.at[1],
                device_id=lead_device,
                device_id_type=MESH,
            ).wait_recv()
            finish(y_own[...], sign, cr, ci, row_tab, col_hi, col_lo, active)

        copy.wait_send()

    @pl.when(is_lead)
    def _():
        for d, (exists, _) in enumerate(sides):

            @pl.when(jnp.logical_not(exists))
            def _():
                m_got[1 - d] = jnp.zeros((32, 128), F32)
                y_got[1 - d] = jnp.zeros((32, 128), F32)

        @pl.when(jnp.logical_not(has_depot))
        def _():
            pl.semaphore_signal(barrier, inc=1, device_id=others[0], device_id_type=MESH)

        for device in others[1:]:
            pl.semaphore_signal(barrier, inc=1, device_id=device, device_id_type=MESH)

        for exists, device in (sides[0], (jnp.logical_and(sides[1][0], jnp.logical_not(is_last)), sides[1][1])):

            @pl.when(exists)
            def _():
                pl.semaphore_signal(barrier, inc=1, device_id=device, device_id_type=MESH)

        del used[2:]
        width = WIDTH // CHUNKS
        small = [
            load(a, b)
            for a, b in (
                (rows_hbm, rows_v),
                (cols_hbm, cols_v),
                (step_hbm, step_v),
                (consts_hbm, consts_v),
                (tabs_hbm, tabs_v),
            )
        ]
        parts = [pl.ds(c * width, width) for c in range(CHUNKS)]
        mask_copies = [load(mask_hbm.at[:, p], mask_v.at[:, p]) for p in parts]
        fwd_copies = [load(fwd_hbm.at[p, :], fwd_v.at[p, :]) for p in parts]
        later = [load(up_hbm, up_v), load(target_hbm, target_v), load(down_hbm, down_v)]
        for copy in small:
            copy.start()
        for a, b in zip(mask_copies, fwd_copies):
            a.start()
            b.start()
        for copy in early + later:
            copy.start()

        for copy in small:
            copy.wait()
        sign, cr, ci, row_tab, col_hi, col_lo, active = fragments()
        amp = jnp.where(active, step_v[...], 0.0) * (1.0 / math.sqrt(FRAG_LEN))

        total = jnp.zeros((2 * SLAB, 256), F32)
        for c in range(CHUNKS):
            mask_copies[c].wait()
            fwd_copies[c].wait()
            hi, lo = split(mask_v[:, c * width : (c + 1) * width])
            total += dot(jnp.concatenate([hi, lo], 0), fwd_v[c * width : (c + 1) * width, :])
        packed = total[:SLAB, :128] + total[:SLAB, 128:] + total[SLAB:, :128]
        modes_own = own_modes(packed, row_tab, col_hi, col_lo, amp, tabs_v[640:672, :192], sign)
        m_own[...] = modes_own

        def exchange(own, got, recv, devices):
            copies = [
                pltpu.make_async_remote_copy(
                    src_ref=own,
                    dst_ref=got.at[d],
                    send_sem=load_sem.at[2 + d],
                    recv_sem=recv.at[d],
                    device_id=device,
                    device_id_type=MESH,
                )
                for d, device in enumerate(devices)
            ]
            for d, (exists, _) in enumerate(sides):

                @pl.when(exists)
                def _():
                    copies[d].start()

            return copies

        def arrived(copies):
            for d, (exists, _) in enumerate(sides):

                @pl.when(exists)
                def _():
                    copies[1 - d].wait_recv()

        def sent(copies):
            for d, (exists, _) in enumerate(sides):

                @pl.when(exists)
                def _():
                    copies[d].wait_send()

        pl.semaphore_wait(
            barrier, lax.min(tile, 1) + lax.min(TILES - 1 - tile, 1) + depot_tile(tile)
        )

        @pl.when(has_depot)
        def _():
            pl.semaphore_signal(far_sem.at[1], inc=1, device_id=others[0], device_id_type=MESH)

        m_copies = exchange(m_own, m_got, m_recv, (left_of_modes, sides[1][1]))

        scale_own()
        low = lax.broadcasted_iota(jnp.int32, (ROW_FREQS, 128), 1) < 64

        def spectra_from(d):
            at = pl.multiple_of(lax.rem(lead + d, KERN) * LOCAL, LOCAL)
            return pltpu.make_async_remote_copy(
                src_ref=h_v.at[pl.ds(at, LOCAL)],
                dst_ref=h_v.at[pl.ds(at, LOCAL)],
                send_sem=load_sem.at[0],
                recv_sem=h_recv.at[d - 1],
                device_id=others[0],
                device_id_type=MESH,
            )

        def far_is_here(d):
            pl.semaphore_signal(
                far_sem.at[d],
                inc=1,
                device_id=(left_of_modes, sides[1][1])[d],
                device_id_type=MESH,
            )

        @pl.when(is_first)
        def _():
            for d in (1, 2, 3):
                spectra_from(d).wait_recv()
            far_is_here(0)

        def take(place, d):
            at = pl.multiple_of(lax.rem(lead + d, KERN) * LOCAL, LOCAL)
            if d > 0:

                @pl.when(jnp.logical_not(is_first))
                def _():
                    spectra_from(d).wait_recv()

            for k in range(LOCAL):
                a, b = two_forms(h_v[at + k], low)
                hrr_v[place * LOCAL + k] = a
                hii_v[place * LOCAL + k] = b

        take(0, 0)
        take(1, 3)

        def forms(g):
            ks = pl.ds(g * GROUP, GROUP)
            return hrr_v[ks], hii_v[ks]

        for copy in later:
            copy.wait()
        for c in range(8):
            ends = [target_v[:, h + 128 * c : h + 128 * c + 128] for h in (0, WIDTH // 2)]
            turned_v[128 * c : 128 * c + 128, :] = jnp.transpose(jnp.concatenate(ends, 0))
        take(2, 2)
        arrived(m_copies)
        modes, imodes = combine(modes_own, m_got[1], m_got[0], cr, ci, sign)

        inten = change = jnp.zeros((GRID_ROWS, 128), F32)
        n = KERNELS // GROUP
        ready = []
        for g in range(n + AHEAD):
            if g == max(3 * n // 4, 1):
                take(3, 1)

                @pl.when(jnp.logical_and(sides[0][0], jnp.logical_not(is_first)))
                def _():
                    far_is_here(0)

                @pl.when(sides[1][0])
                def _():
                    far_is_here(1)

            if g < n:
                hrr, hii = forms(g)
                ready.append(forward_group(hrr, hii, modes, imodes, tabs_v[0:384, :]))
            if g >= AHEAD:
                amps = forward_rows(ready[g - AHEAD], tabs_v[672:736, :96])
                e0_v[g - AHEAD] = amps[:, : 128 * GROUP]
                s0, s1 = intensity_terms(amps, GROUP)
                inten, change = inten + s0, change + s1

        grids = table_dot(tabs_v[800:864, :96], jnp.concatenate([0.5 * inten, change], 1))
        rows3 = column_rows(grids)

        n = WIDTH // 2 // SPAN
        parts = [slice(c * SPAN, (c + 1) * SPAN) for c in range(n)]
        total = jnp.zeros((128, 256), F32)
        full = dot_nt(up_v[parts[0], :], rows3)
        for c in range(n):
            ahead = dot_nt(up_v[parts[c + 1], :], rows3) if c + 1 < n else None
            total += weighted_back(full, turned_v[parts[c], :], down_v[:, parts[c]])
            full = ahead
        wgrid = weighted_grid(total, tabs_v[864:896, :])
        w0, w1 = wgrid[:, :128], wgrid[:, 128:]

        first = second = jnp.zeros((32, 128), F32)
        ready = []
        n = KERNELS // AGROUP
        for g in range(n + AAHEAD):
            if g < n:
                e0 = e0_v[g * AGROUP // GROUP, :, pl.ds(g * AGROUP % GROUP * 128, AGROUP * 128)]
                ready.append(adjoint_rows(e0, w0, w1, tabs_v[736:800, :128]))
            if g >= AAHEAD:
                ks = pl.ds((g - AAHEAD) * AGROUP, AGROUP)
                a, b = adjoint_columns(ready[g - AAHEAD], hrr_v[ks], hii_v[ks], tabs_v[384:640, :])
                first, second = first + a, second + b
        spectrum = first - times_i(second, sign)
        y_own[...] = spectrum

        def send_own(i, device, d=None):
            return pltpu.make_async_remote_copy(
                src_ref=y_own,
                dst_ref=y_own if d is None else y_got.at[d],
                send_sem=load_sem.at[4 + i],
                recv_sem=h_recv.at[1] if d is None else y_recv.at[d],
                device_id=device,
                device_id_type=MESH,
            )

        y_copies = [send_own(d, sides[d][1], d) for d in range(2)]
        own_copies = [send_own(2 + c, device) for c, device in enumerate(far_of(tile))]
        far_copies = [
            [send_own(4 + 2 * d + c, device, d) for c, device in enumerate(far_of(t))]
            for d, t in enumerate((before, after))
        ]
        for d in (1, 0):

            @pl.when(sides[d][0])
            def _():
                pl.semaphore_wait(far_sem.at[1 - d], 1)
                for copy in reversed(far_copies[d]):
                    copy.start()
                y_copies[d].start()

            if d == 1:
                for copy in own_copies:
                    copy.start()

        arrived(y_copies)
        finish(spectrum, sign, cr, ci, row_tab, col_hi, col_lo, active)
        res_copy = pltpu.make_async_remote_copy(
            src_ref=res_v,
            dst_ref=res_v,
            send_sem=load_sem.at[0],
            recv_sem=h_recv.at[0],
            device_id=mate,
            device_id_type=MESH,
        )
        res_copy.start()
        sent(m_copies)
        sent(y_copies)
        for copy in own_copies:
            copy.wait_send()
        for d in range(2):

            @pl.when(sides[d][0])
            def _():
                for copy in far_copies[d]:
                    copy.wait_send()

        res_copy.wait_send()

    out_ref[...] = res_v[...]


def shards(mask, target, spectra, weights, counts, frag_rows, frag_cols, step):
    fwd, up, down, tabs, consts = make_tables()
    vmem = pl.BlockSpec(memory_space=pltpu.VMEM)
    hbm = pl.BlockSpec(memory_space=pltpu.HBM)
    dma = pltpu.SemaphoreType.DMA
    outs = pl.pallas_call(
        kernel,
        out_shape=pltpu.VMEM((2, SLOTS), F32),
        in_specs=[hbm, pl.BlockSpec(memory_space=pltpu.SMEM)] + [hbm] * 11,
        out_specs=vmem,
        scratch_shapes=[
            pltpu.SMEM((LOCAL,), F32),
            pltpu.VMEM((1, SLOTS), jnp.int32),
            pltpu.VMEM((1, SLOTS), jnp.int32),
            pltpu.VMEM((1, SLOTS), F32),
            pltpu.VMEM((LOCAL, ROW_FREQS, 128), F32),
            pltpu.VMEM(tabs.shape, BF16),
            pltpu.VMEM(consts.shape, F32),
            pltpu.VMEM((SLAB, WIDTH), F32),
            pltpu.VMEM((SLAB, WIDTH), F32),
            pltpu.VMEM((WIDTH, 256), BF16),
            pltpu.VMEM(up.shape, BF16),
            pltpu.VMEM(down.shape, BF16),
            pltpu.VMEM((KERNELS, ROW_FREQS, 128), F32),
            pltpu.VMEM((KERNELS // GROUP, 2 * GRID_ROWS, 128 * GROUP), F32),
            pltpu.VMEM((32, 128), F32),
            pltpu.VMEM((2, 32, 128), F32),
            pltpu.VMEM((32, 128), F32),
            pltpu.VMEM((2, 32, 128), F32),
            pltpu.VMEM((KERNELS, ROW_FREQS, 128), F32),
            pltpu.VMEM((KERNELS, ROW_FREQS, 128), F32),
            pltpu.VMEM((WIDTH // 2, 128), F32),
            pltpu.VMEM((2, SLOTS), F32),
            dma((2 * CHUNKS + 10,)),
            dma((3,)),
            dma((2,)),
            dma((2,)),
            pltpu.SemaphoreType.REGULAR((2,)),
        ],
        compiler_params=pltpu.CompilerParams(
            collective_id=0, has_side_effects=True, vmem_limit_bytes=60 * 1024 * 1024
        ),
    )(
        weights,
        counts,
        frag_rows.reshape(1, SLOTS),
        frag_cols.reshape(1, SLOTS),
        step.reshape(1, SLOTS),
        spectra,
        jnp.asarray(tabs),
        jnp.asarray(consts),
        mask,
        target,
        jnp.asarray(fwd),
        jnp.asarray(up),
        jnp.asarray(down),
    )
    return outs[0], outs[1]


def solution(mesh):
    return jax.shard_map(
        shards,
        mesh=mesh,
        in_specs=(
            P("tile", None),
            P("tile", None),
            P("kern", None, None),
            P("kern"),
            P("tile"),
            P("tile"),
            P("tile"),
            P("tile"),
        ),
        out_specs=(P("tile"), P("tile")),
        check_vma=False,
    )
```

```python
import functools
import math

import jax
import jax.numpy as jnp
import ml_dtypes
import numpy as np
from jax import lax
from jax.experimental import pallas as pl
from jax.experimental.pallas import tpu as pltpu
from jax.sharding import PartitionSpec as P

WIDTH = 2048
COL_FREQS = 64
ROW_FREQS = 16
KERNELS = 24
FRAG_LEN = 32
SLAB = 64
SLOTS = 256
EXT = 192
TILES = 64
KERN = 4
LOCAL = KERNELS // KERN
GRID_ROWS = 32
GRID_COLS = 128
STEEP = 10.0
THRESH = 0.1
F32 = jnp.float32
BF16 = jnp.bfloat16
CHUNKS = 1
GROUP = 8
SPAN = 256
AHEAD = 1
AGROUP = 8
AAHEAD = 1
PLANE = 16
MESH = pl.DeviceIdType.MESH


def np_split(x):
    hi = x.astype(np.float32).astype(ml_dtypes.bfloat16)
    lo = (x - hi.astype(np.float64)).astype(np.float32).astype(ml_dtypes.bfloat16)
    return hi, lo


def pad_lanes(x, lanes=256):
    return np.pad(x, ((0, 0), (0, lanes - x.shape[1])))


@functools.lru_cache(maxsize=None)
def make_tables():
    kc = np.arange(COL_FREQS) - COL_FREQS // 2
    kr = np.arange(ROW_FREQS) - ROW_FREQS // 2
    x = np.arange(WIDTH)
    ang = 2 * np.pi * (np.outer(x, kc) % WIDTH) / WIDTH
    f_hi, f_lo = np_split(np.concatenate([np.cos(ang), -np.sin(ang)], 1) / math.sqrt(WIDTH))
    fwd = np.concatenate([f_hi, f_lo], 1)

    n = np.arange(GRID_COLS)
    step = WIDTH // GRID_COLS
    dist = (x[None, :] - step * n[:, None]) % WIDTH
    base = np.ones(WIDTH)
    for kap in range(1, COL_FREQS):
        base += 2 * np.cos(2 * np.pi * ((np.arange(WIDTH) * kap) % WIDTH) / WIDTH)
    g = (base / GRID_COLS)[dist]
    g = g[:, : WIDTH // 2]
    g_hi, g_lo = np_split(g)
    up = np.concatenate([g_hi.T, g_lo.T], 1)
    down = np.concatenate([g_hi, g_lo], 0)

    ang = 2 * np.pi * (np.outer(kc, n) % GRID_COLS) / GRID_COLS
    c, s = np.cos(ang) / math.sqrt(WIDTH), np.sin(ang) / math.sqrt(WIDTH)
    inv = np.block([[c, s], [-s, c]])
    i_hi, i_lo = np_split(inv)
    inv3 = np.concatenate([i_hi, i_hi, i_lo], 0)
    t_hi, t_lo = np_split(inv.T)
    adj = np.concatenate([t_hi, t_lo], 1)

    e = np.arange(SLAB)
    ang = 2 * np.pi * (np.outer(kr, e) % EXT) / EXT
    a_hi, a_lo = np_split(np.concatenate([np.cos(ang), np.sin(ang)], 0) / math.sqrt(EXT))
    lt3 = np.concatenate([a_hi, a_hi, a_lo], 1)

    m = np.arange(GRID_ROWS)
    ang = 2 * np.pi * (np.outer(m, kr) % GRID_ROWS) / GRID_ROWS
    c, s = np.cos(ang) / math.sqrt(EXT), np.sin(ang) / math.sqrt(EXT)
    ag = np.block([[c, -s], [s, c]])
    hi, lo = np_split(ag)
    ag3 = np.concatenate([hi, hi, lo], 1)
    hi, lo = np_split(ag.T)
    agt3 = np.concatenate([np.concatenate([hi, hi], 1), np.concatenate([lo, lo], 1)], 0)

    rstep = EXT // GRID_ROWS
    dist = (e[:, None] - rstep * m[None, :]) % EXT
    base = np.ones(EXT)
    for rho in range(1, ROW_FREQS):
        base += 2 * np.cos(2 * np.pi * ((np.arange(EXT) * rho) % EXT) / EXT)
    r = (base / GRID_ROWS)[dist]
    hi, lo = np_split(r)
    r3 = np.concatenate([hi, hi, lo], 1)
    hi, lo = np_split(np.concatenate([r.T, r.T], 1))
    rt2 = np.concatenate([hi, lo], 1)

    tabs = np.concatenate(
        [inv3, adj, pad_lanes(lt3), pad_lanes(ag3), pad_lanes(agt3), pad_lanes(r3), rt2], 0
    )

    ang = 2 * np.pi * (kr % 3) / 3
    cr = np.tile(np.cos(ang), 2)
    ci = np.tile(np.sin(ang), 2)
    with np.errstate(invalid="ignore"):
        d = np.where(kc == 0, FRAG_LEN, np.sin(np.pi * FRAG_LEN * kc / WIDTH) / np.sin(np.pi * kc / WIDTH))
    d = d / math.sqrt(WIDTH)
    col = np.concatenate([cr, ci, d, -d])
    consts = np.repeat(col[:, None], 128, 1).astype(np.float32)
    blocks = [down[:, i : i + SPAN] for i in range(0, WIDTH // 2, SPAN)]
    first = np.concatenate([tabs, fwd], 0)
    return first, np.concatenate([up] + blocks, 0), consts


def split(x):
    hi = x.astype(BF16)
    return hi, (x - hi.astype(F32)).astype(BF16)


def dot(a, b):
    return lax.dot_general(a, b, (((1,), (0,)), ((), ())), preferred_element_type=F32)


def dot_nt(a, b):
    return lax.dot_general(a, b, (((1,), (1,)), ((), ())), preferred_element_type=F32)


def table_dot(table3, x):
    hi, lo = split(x)
    return dot(table3, jnp.concatenate([hi, lo, hi], 0))


def with_halves_swapped(x):
    return pltpu.roll(x, 64, axis=1)


def column_rows(grids):
    i, d = grids[:, :128], grids[:, 128:]
    hi, lo = split(jnp.concatenate([i, with_halves_swapped(i), d, with_halves_swapped(d)], 0))
    return jnp.concatenate([hi, lo, hi], 1)


def weighted_back(full, target, down):
    w0, w1 = weighting(full[:, :128], full[:, 128:], target)
    hi, lo = split(jnp.concatenate([w0, w1], 1))
    both = dot(down, hi)
    return both[:128] + both[128:] + dot(down[:128], lo)


def weighted_grid(z, rt2):
    swapped = jnp.concatenate([z[64:], z[:64]], 0)
    low = (lax.broadcasted_iota(jnp.int32, z.shape, 1) & 64) == 0
    v = jnp.where(low, z, swapped)
    hi, lo = split(jnp.concatenate([v[:, :128], v[:, 128:]], 0))
    rt_hi, rt_lo = rt2[:, :128], rt2[:, 128:]
    return dot_nt(jnp.concatenate([rt_hi, rt_hi, rt_lo], 1), jnp.concatenate([hi, lo, hi], 1))


def sin_turns(u):
    y = u * (2.0 * math.pi)
    s = y * y
    p = jnp.full_like(s, -1.0 / 39916800.0)
    for coef in (1.0 / 362880.0, -1.0 / 5040.0, 1.0 / 120.0, -1.0 / 6.0):
        p = p * s + coef
    return y + y * (s * p)


def cos_turns(t):
    t = t - jnp.floor(t + 0.5)
    return sin_turns(0.25 - jnp.abs(t))


def times_i(z, sign):
    return pltpu.roll(z, 64, axis=1) * sign


def lane_sign(shape):
    lane = lax.broadcasted_iota(jnp.int32, shape, 1)
    return jnp.where(lane < 64, -1.0, 1.0).astype(F32)


def fragment_tables(rows, cols, dsc):
    kr = lax.broadcasted_iota(jnp.int32, (32, SLOTS), 0)
    is_sin = kr >= 16
    kr = ((kr & 15) - 8).astype(F32)
    t = kr * rows.astype(F32) * (1.0 / EXT)
    row_tab = cos_turns(t - jnp.where(is_sin, 0.25, 0.0)) * (1.0 / math.sqrt(EXT))
    kc = lax.broadcasted_iota(jnp.int32, (128, SLOTS), 0)
    is_sin = kc >= 64
    kc = ((kc & 63) - 32).astype(F32)
    t = kc * (2 * cols + (FRAG_LEN - 1)).astype(F32) * (1.0 / (2 * WIDTH))
    col_tab = cos_turns(t - jnp.where(is_sin, 0.25, 0.0)) * dsc
    return row_tab, col_tab


def own_modes(packed, row_tab, col_hi, col_lo, amp, lt3, sign):
    u0 = table_dot(lt3, packed)
    hi, lo = split(row_tab * amp)
    u1 = dot_nt(
        jnp.concatenate([hi, lo, hi], 1), jnp.concatenate([col_hi, col_hi, col_lo], 1)
    )
    u_re = jnp.concatenate([u0[:16], u1[:16]], 0)
    u_im = jnp.concatenate([u0[16:], u1[16:]], 0)
    return u_re - times_i(u_im, sign)


def combine(own, left, right, cr, ci, sign):
    both, odd = left + right, left - right
    return (
        own + cr * both + ci * times_i(odd, sign),
        times_i(own, sign) + cr * times_i(both, sign) - ci * odd,
    )


def two_forms(h, low):
    turned = pltpu.roll(h, 64, axis=1)
    return jnp.where(low, h, turned), jnp.where(low, turned, h)


def side_by_side(x, rows):
    return jnp.concatenate([x[i : i + rows] for i in range(0, x.shape[0], rows)], 1)


def forward_group(hrr, hii, modes, imodes, inv3):
    blocks = []
    for j in range(2):
        m, im = modes[16 * j : 16 * j + 16], imodes[16 * j : 16 * j + 16]
        blocks += [hrr[k] * m + hii[k] * im for k in range(hrr.shape[0])]
    hi, lo = split(jnp.concatenate(blocks, 0))
    return dot(jnp.concatenate([hi, lo, hi], 1), inv3)


def forward_rows(q, ag3):
    q_re, q_im = side_by_side(q[:, :128], 16), side_by_side(q[:, 128:], 16)
    return table_dot(ag3, jnp.concatenate([q_re, q_im], 0))


def intensity_terms(amps, kernels):
    total0 = total1 = None
    for k in range(kernels):
        a, b = amps[:, 128 * k : 128 * k + 128], amps[:, 128 * (kernels + k) : 128 * (kernels + k) + 128]
        s0, s1 = a * a, a * b
        total0 = s0 if total0 is None else total0 + s0
        total1 = s1 if total1 is None else total1 + s1
    return total0[:32] + total0[32:], total1[:32] + total1[32:]


def weighting(inten, change, target):
    developed = 1.0 / (1.0 + jnp.exp(-STEEP * (inten - THRESH)))
    steep = STEEP * developed * (1.0 - developed)
    return steep * (developed - target), steep * steep * change


def adjoint_rows(e0, w0, w1, agt3):
    kernels = e0.shape[1] // 128
    loads = []
    for w in (w0, w1):
        ww = jnp.concatenate([w, w], 0)
        loads += [ww * e0[:, 128 * k : 128 * k + 128] for k in range(kernels)]
    hi, lo = split(jnp.concatenate(loads, 1))
    u = dot(agt3, jnp.concatenate([hi, lo], 0))
    return u[:32] + u[32:]


def adjoint_columns(u, hrr, hii, adj):
    kernels = hrr.shape[0]
    rows = [
        jnp.concatenate([u[:16, 128 * b : 128 * b + 128], u[16:, 128 * b : 128 * b + 128]], 1)
        for b in range(2 * kernels)
    ]
    hi, lo = split(jnp.concatenate(rows, 0))
    both = dot(hi, adj)
    back = both[:, :128] + both[:, 128:] + dot(lo, adj[:, :128])
    first, second = [], []
    for j in range(2):
        f = s = None
        for k in range(kernels):
            at = 16 * (j * kernels + k)
            a, b = hrr[k] * back[at : at + 16], hii[k] * back[at : at + 16]
            f = a if f is None else f + a
            s = b if s is None else s + b
        first.append(f)
        second.append(s)
    return jnp.concatenate(first, 0), jnp.concatenate(second, 0)


def project(total, it, row_tab, col_hi, col_lo):
    lhs = jnp.concatenate([total[:16], it[:16], total[16:], it[16:]], 0)
    hi, lo = split(lhs)
    q = dot(jnp.concatenate([hi, lo, hi], 1), jnp.concatenate([col_hi, col_hi, col_lo], 0))
    return [jnp.sum(q[32 * j : 32 * j + 32] * row_tab, axis=0, keepdims=True) for j in range(2)]


def kernel(
    weights_hbm,
    counts_s,
    rows_hbm,
    cols_hbm,
    step_hbm,
    spectra_hbm,
    tabs_hbm,
    consts_hbm,
    mask_hbm,
    target_hbm,
    later_hbm,
    out_ref,
    weights_s,
    rows_v,
    cols_v,
    step_v,
    spectra_v,
    tabs_v,
    consts_v,
    mask_v,
    target_v,
    later_v,
    h_v,
    e0_v,
    m_own,
    m_got,
    y_own,
    y_got,
    hrr_v,
    hii_v,
    turned_v,
    res_v,
    load_sem,
    h_recv,
    m_recv,
    far_sem,
):
    tile = lax.axis_index("tile")
    kern = lax.axis_index("kern")
    barrier = pltpu.get_barrier_semaphore()
    is_last = jnp.logical_and(lax.rem(tile, PLANE) == PLANE - 1, tile < TILES - 1)

    @pl.when(jnp.logical_and(is_last, kern == 1))
    def _():
        pl.semaphore_signal(
            barrier,
            inc=1,
            device_id={"tile": lax.max(tile - (PLANE - 2), 0), "kern": 1},
            device_id_type=MESH,
        )

    def depot_tile(t):
        return jnp.logical_and(lax.rem(t, PLANE) == 1, t < TILES - PLANE).astype(jnp.int32)

    def lead_of(t):
        return 3 - 2 * lax.rem(t, 2) - depot_tile(t)

    lead = lead_of(tile)
    is_lead = kern == lead
    others = [{"tile": tile, "kern": lax.rem(lead + d, KERN)} for d in (1, 2, 3)]
    before, after = lax.max(tile - 1, 0), lax.min(tile + 1, TILES - 1)
    sides = (
        (tile > 0, {"tile": before, "kern": lead_of(before)}),
        (tile < TILES - 1, {"tile": after, "kern": lead_of(after)}),
    )
    first = 1 - lax.min(lax.rem(tile, PLANE), 1)
    left_of_modes = {
        "tile": lax.max(tile - 1 - (PLANE - 2) * first, 0),
        "kern": lead_of(before) * (1 - first) + first,
    }
    is_first = jnp.logical_and(first == 1, tile > 0)
    has_depot = depot_tile(tile) == 1

    def far_of(t):
        base = 2 - 2 * (lead_of(t) // 2)
        return [{"tile": t, "kern": base + c} for c in range(2)]

    is_far = kern // 2 != lead // 2
    mate = {"tile": tile, "kern": lead + 1 - 2 * lax.rem(lead, 2)}
    is_depot = jnp.logical_and(has_depot, kern == 1)
    used = []

    def load(src, dst):
        copy = pltpu.make_async_copy(src, dst, load_sem.at[len(used)])
        used.append(copy)
        return copy

    early = [load(weights_hbm, weights_s), load(spectra_hbm, spectra_v)]
    mine = pl.multiple_of(kern * LOCAL, LOCAL)

    def scale_own():
        for copy in early:
            copy.wait()
        for k in range(LOCAL):
            scale = jnp.sqrt(jnp.full((ROW_FREQS, 128), weights_s[k] * (2.0 / KERNELS), F32))
            h_v[mine + k] = spectra_v[k] * scale

    def fragments():
        sign = lane_sign((32, 128))
        cr, ci = consts_v[0:32], consts_v[32:64]
        dsc = consts_v[64:192]
        row_tab, col_tab = fragment_tables(rows_v[...], cols_v[...], jnp.concatenate([dsc, dsc], 1))
        col_hi, col_lo = split(col_tab)
        active = lax.broadcasted_iota(jnp.int32, (1, SLOTS), 1) < counts_s[0]
        return sign, cr, ci, row_tab, col_hi, col_lo, active

    def finish(spectrum, sign, cr, ci, row_tab, col_hi, col_lo, active):
        whole = combine(spectrum, y_got[1], y_got[0], cr, ci, sign)
        outs = project(*whole, row_tab, col_hi, col_lo)
        for j in range(2):
            res_v[j : j + 1, :] = jnp.where(active, outs[j] * (1.0 / math.sqrt(FRAG_LEN)), 0.0)

    @pl.when(jnp.logical_not(is_lead))
    def _():
        lead_device = {"tile": tile, "kern": lead}
        small = [
            load(a, b)
            for a, b in (
                (rows_hbm, rows_v),
                (cols_hbm, cols_v),
                (consts_hbm, consts_v),
            )
        ]

        @pl.when(is_far)
        def _():
            for d, (exists, _) in enumerate(sides):

                @pl.when(jnp.logical_not(exists))
                def _():
                    y_got[1 - d] = jnp.zeros((32, 128), F32)


        @pl.when(is_depot)
        def _():
            pl.semaphore_signal(
                barrier,
                inc=1,
                device_id={"tile": lax.min(tile + PLANE - 1, TILES - 1), "kern": 3},
                device_id_type=MESH,
            )
            pl.semaphore_signal(barrier, inc=1, device_id=lead_device, device_id_type=MESH)

        for copy in early:
            copy.start()
        scale_own()

        @pl.when(is_depot)
        def _():
            pl.semaphore_wait(far_sem.at[1], 1)

        @pl.when(jnp.logical_not(is_depot))
        def _():
            pl.semaphore_wait(barrier, 1)

        place = lax.rem(kern - lead + KERN, KERN) - 1
        copy = pltpu.make_async_remote_copy(
            src_ref=h_v.at[pl.ds(mine, LOCAL)],
            dst_ref=h_v.at[pl.ds(mine, LOCAL)],
            send_sem=load_sem.at[5],
            recv_sem=h_recv.at[place],
            device_id=lead_device,
            device_id_type=MESH,
        )
        copy.start()

        @pl.when(is_depot)
        def _():
            pl.semaphore_wait(barrier, 1)
            onward = pltpu.make_async_remote_copy(
                src_ref=m_got.at[0],
                dst_ref=m_got.at[0],
                send_sem=load_sem.at[6],
                recv_sem=m_recv.at[0],
                device_id={"tile": lax.min(tile + PLANE - 2, TILES - 1), "kern": 1},
                device_id_type=MESH,
            )
            onward.wait_recv()
            onward.start()
            pl.semaphore_wait(far_sem.at[0], 1)
            pl.semaphore_signal(
                far_sem.at[0],
                inc=1,
                device_id={"tile": lax.min(tile + PLANE - 2, TILES - 1), "kern": 1},
                device_id_type=MESH,
            )
            onward.wait_send()

        @pl.when(jnp.logical_not(is_far))
        def _():
            pltpu.make_async_remote_copy(
                src_ref=res_v,
                dst_ref=res_v,
                send_sem=load_sem.at[0],
                recv_sem=h_recv.at[0],
                device_id=lead_device,
                device_id_type=MESH,
            ).wait_recv()

        @pl.when(is_far)
        def _():
            for load_copy in small:
                load_copy.start()
            for load_copy in small:
                load_copy.wait()
            sign, cr, ci, row_tab, col_hi, col_lo, active = fragments()
            for d, (exists, _) in enumerate(sides):

                @pl.when(exists)
                def _():
                    pltpu.make_async_remote_copy(
                        src_ref=y_own,
                        dst_ref=y_got.at[1 - d],
                        send_sem=load_sem.at[0],
                        recv_sem=h_recv.at[2 - 2 * d],
                        device_id=lead_device,
                        device_id_type=MESH,
                    ).wait_recv()

            pltpu.make_async_remote_copy(
                src_ref=y_own,
                dst_ref=y_own,
                send_sem=load_sem.at[0],
                recv_sem=h_recv.at[1],
                device_id=lead_device,
                device_id_type=MESH,
            ).wait_recv()
            finish(y_own[...], sign, cr, ci, row_tab, col_hi, col_lo, active)

        copy.wait_send()

    @pl.when(is_lead)
    def _():
        for d, (exists, _) in enumerate(sides):

            @pl.when(jnp.logical_not(exists))
            def _():
                m_got[1 - d] = jnp.zeros((32, 128), F32)
                y_got[1 - d] = jnp.zeros((32, 128), F32)

        @pl.when(jnp.logical_not(has_depot))
        def _():
            pl.semaphore_signal(barrier, inc=1, device_id=others[0], device_id_type=MESH)

        for device in others[1:]:
            pl.semaphore_signal(barrier, inc=1, device_id=device, device_id_type=MESH)

        for exists, device in (sides[0], (jnp.logical_and(sides[1][0], jnp.logical_not(is_last)), sides[1][1])):

            @pl.when(exists)
            def _():
                pl.semaphore_signal(barrier, inc=1, device_id=device, device_id_type=MESH)

        del used[2:]
        width = WIDTH // CHUNKS
        small = [
            load(a, b)
            for a, b in (
                (rows_hbm, rows_v),
                (cols_hbm, cols_v),
                (step_hbm, step_v),
                (consts_hbm, consts_v),
            )
        ]
        parts = [pl.ds(c * width, width) for c in range(CHUNKS)]
        mask_copies = [load(mask_hbm.at[:, p], mask_v.at[:, p]) for p in parts]
        fwd_copies = [load(tabs_hbm, tabs_v)]
        later = [load(later_hbm, later_v), load(target_hbm, target_v)]
        for copy in small:
            copy.start()
        for a, b in zip(mask_copies, fwd_copies):
            a.start()
            b.start()
        for copy in early + later:
            copy.start()

        for copy in small:
            copy.wait()
        sign, cr, ci, row_tab, col_hi, col_lo, active = fragments()
        amp = jnp.where(active, step_v[...], 0.0) * (1.0 / math.sqrt(FRAG_LEN))

        total = jnp.zeros((2 * SLAB, 256), F32)
        for c in range(CHUNKS):
            mask_copies[c].wait()
            fwd_copies[c].wait()
            hi, lo = split(mask_v[:, c * width : (c + 1) * width])
            total += dot(jnp.concatenate([hi, lo], 0), tabs_v[896 + c * width : 896 + (c + 1) * width, :])
        packed = total[:SLAB, :128] + total[:SLAB, 128:] + total[SLAB:, :128]
        modes_own = own_modes(packed, row_tab, col_hi, col_lo, amp, tabs_v[640:672, :192], sign)
        m_own[...] = modes_own

        def exchange(own, got, recv, devices):
            copies = [
                pltpu.make_async_remote_copy(
                    src_ref=own,
                    dst_ref=got.at[d],
                    send_sem=load_sem.at[2 + d],
                    recv_sem=recv.at[d],
                    device_id=device,
                    device_id_type=MESH,
                )
                for d, device in enumerate(devices)
            ]
            for d, (exists, _) in enumerate(sides):

                @pl.when(exists)
                def _():
                    copies[d].start()

            return copies

        def arrived(copies):
            for d, (exists, _) in enumerate(sides):

                @pl.when(exists)
                def _():
                    copies[1 - d].wait_recv()

        def sent(copies):
            for d, (exists, _) in enumerate(sides):

                @pl.when(exists)
                def _():
                    copies[d].wait_send()

        pl.semaphore_wait(
            barrier, lax.min(tile, 1) + lax.min(TILES - 1 - tile, 1) + depot_tile(tile)
        )

        @pl.when(has_depot)
        def _():
            pl.semaphore_signal(far_sem.at[1], inc=1, device_id=others[0], device_id_type=MESH)

        m_copies = exchange(m_own, m_got, m_recv, (left_of_modes, sides[1][1]))

        scale_own()
        low = lax.broadcasted_iota(jnp.int32, (ROW_FREQS, 128), 1) < 64

        def spectra_from(d):
            at = pl.multiple_of(lax.rem(lead + d, KERN) * LOCAL, LOCAL)
            return pltpu.make_async_remote_copy(
                src_ref=h_v.at[pl.ds(at, LOCAL)],
                dst_ref=h_v.at[pl.ds(at, LOCAL)],
                send_sem=load_sem.at[0],
                recv_sem=h_recv.at[d - 1],
                device_id=others[0],
                device_id_type=MESH,
            )

        def far_is_here(d):
            pl.semaphore_signal(
                far_sem.at[d],
                inc=1,
                device_id=(left_of_modes, sides[1][1])[d],
                device_id_type=MESH,
            )

        @pl.when(is_first)
        def _():
            for d in (1, 2, 3):
                spectra_from(d).wait_recv()
            far_is_here(0)

        def take(place, d):
            at = pl.multiple_of(lax.rem(lead + d, KERN) * LOCAL, LOCAL)
            if d > 0:

                @pl.when(jnp.logical_not(is_first))
                def _():
                    spectra_from(d).wait_recv()

            for k in range(LOCAL):
                a, b = two_forms(h_v[at + k], low)
                hrr_v[place * LOCAL + k] = a
                hii_v[place * LOCAL + k] = b

        take(0, 0)
        take(1, 3)

        def forms(g):
            ks = pl.ds(g * GROUP, GROUP)
            return hrr_v[ks], hii_v[ks]

        for copy in later:
            copy.wait()
        for c in range(8):
            ends = [target_v[:, h + 128 * c : h + 128 * c + 128] for h in (0, WIDTH // 2)]
            turned_v[128 * c : 128 * c + 128, :] = jnp.transpose(jnp.concatenate(ends, 0))
        take(2, 2)
        arrived(m_copies)
        modes, imodes = combine(modes_own, m_got[1], m_got[0], cr, ci, sign)

        inten = change = jnp.zeros((GRID_ROWS, 128), F32)
        n = KERNELS // GROUP
        ready = []
        for g in range(n + AHEAD):
            if g == max(3 * n // 4, 1):
                take(3, 1)

                @pl.when(jnp.logical_and(sides[0][0], jnp.logical_not(is_first)))
                def _():
                    far_is_here(0)

                @pl.when(sides[1][0])
                def _():
                    far_is_here(1)

            if g < n:
                hrr, hii = forms(g)
                ready.append(forward_group(hrr, hii, modes, imodes, tabs_v[0:384, :]))
            if g >= AHEAD:
                amps = forward_rows(ready[g - AHEAD], tabs_v[672:736, :96])
                e0_v[g - AHEAD] = amps[:, : 128 * GROUP]
                s0, s1 = intensity_terms(amps, GROUP)
                inten, change = inten + s0, change + s1

        grids = table_dot(tabs_v[800:864, :96], jnp.concatenate([0.5 * inten, change], 1))
        rows3 = column_rows(grids)

        n = WIDTH // 2 // SPAN
        parts = [slice(c * SPAN, (c + 1) * SPAN) for c in range(n)]
        total = jnp.zeros((128, 256), F32)

        def up(c):
            u = later_v[parts[c], :]
            return jnp.concatenate([u[:, :128], u[:, :128], u[:, 128:]], 1)

        def down(c):
            return later_v[WIDTH // 2 + SPAN * c : WIDTH // 2 + SPAN * c + 256, :]

        full = dot_nt(up(0), rows3)
        for c in range(n):
            ahead = dot_nt(up(c + 1), rows3) if c + 1 < n else None
            total += weighted_back(full, turned_v[parts[c], :], down(c))
            full = ahead
        wgrid = weighted_grid(total, tabs_v[864:896, :])
        w0, w1 = wgrid[:, :128], wgrid[:, 128:]

        first = second = jnp.zeros((32, 128), F32)
        ready = []
        n = KERNELS // AGROUP
        for g in range(n + AAHEAD):
            if g < n:
                e0 = e0_v[g * AGROUP // GROUP, :, pl.ds(g * AGROUP % GROUP * 128, AGROUP * 128)]
                ready.append(adjoint_rows(e0, w0, w1, tabs_v[736:800, :128]))
            if g >= AAHEAD:
                ks = pl.ds((g - AAHEAD) * AGROUP, AGROUP)
                a, b = adjoint_columns(ready[g - AAHEAD], hrr_v[ks], hii_v[ks], tabs_v[384:640, :])
                first, second = first + a, second + b
        spectrum = first - times_i(second, sign)
        y_own[...] = spectrum
        sent(m_copies)

        def send_own(i, device, d=None):
            return pltpu.make_async_remote_copy(
                src_ref=y_own,
                dst_ref=y_own if d is None else y_got.at[d],
                send_sem=load_sem.at[2 + i],
                recv_sem=h_recv.at[1] if d is None else h_recv.at[2 * d],
                device_id=device,
                device_id_type=MESH,
            )

        y_copies = [send_own(d, sides[d][1], d) for d in range(2)]
        own_copies = [send_own(2 + c, device) for c, device in enumerate(far_of(tile))]
        far_copies = [
            [send_own(4 + 2 * d + c, device, d) for c, device in enumerate(far_of(t))]
            for d, t in enumerate((before, after))
        ]
        for d in (1, 0):

            @pl.when(sides[d][0])
            def _():
                pl.semaphore_wait(far_sem.at[1 - d], 1)
                for copy in reversed(far_copies[d]):
                    copy.start()
                y_copies[d].start()

            if d == 1:
                for copy in own_copies:
                    copy.start()

        arrived(y_copies)
        finish(spectrum, sign, cr, ci, row_tab, col_hi, col_lo, active)
        res_copy = pltpu.make_async_remote_copy(
            src_ref=res_v,
            dst_ref=res_v,
            send_sem=load_sem.at[0],
            recv_sem=h_recv.at[0],
            device_id=mate,
            device_id_type=MESH,
        )
        res_copy.start()
        sent(y_copies)
        for copy in own_copies:
            copy.wait_send()
        for d in range(2):

            @pl.when(sides[d][0])
            def _():
                for copy in far_copies[d]:
                    copy.wait_send()

        res_copy.wait_send()

    out_ref[...] = res_v[...]


def shards(mask, target, spectra, weights, counts, frag_rows, frag_cols, step):
    tabs, later_tabs, consts = make_tables()
    vmem = pl.BlockSpec(memory_space=pltpu.VMEM)
    hbm = pl.BlockSpec(memory_space=pltpu.HBM)
    dma = pltpu.SemaphoreType.DMA
    outs = pl.pallas_call(
        kernel,
        out_shape=pltpu.VMEM((2, SLOTS), F32),
        in_specs=[hbm, pl.BlockSpec(memory_space=pltpu.SMEM)] + [hbm] * 9,
        out_specs=vmem,
        scratch_shapes=[
            pltpu.SMEM((LOCAL,), F32),
            pltpu.VMEM((1, SLOTS), jnp.int32),
            pltpu.VMEM((1, SLOTS), jnp.int32),
            pltpu.VMEM((1, SLOTS), F32),
            pltpu.VMEM((LOCAL, ROW_FREQS, 128), F32),
            pltpu.VMEM(tabs.shape, BF16),
            pltpu.VMEM(consts.shape, F32),
            pltpu.VMEM((SLAB, WIDTH), F32),
            pltpu.VMEM((SLAB, WIDTH), F32),
            pltpu.VMEM(later_tabs.shape, BF16),
            pltpu.VMEM((KERNELS, ROW_FREQS, 128), F32),
            pltpu.VMEM((KERNELS // GROUP, 2 * GRID_ROWS, 128 * GROUP), F32),
            pltpu.VMEM((32, 128), F32),
            pltpu.VMEM((2, 32, 128), F32),
            pltpu.VMEM((32, 128), F32),
            pltpu.VMEM((2, 32, 128), F32),
            pltpu.VMEM((KERNELS, ROW_FREQS, 128), F32),
            pltpu.VMEM((KERNELS, ROW_FREQS, 128), F32),
            pltpu.VMEM((WIDTH // 2, 128), F32),
            pltpu.VMEM((2, SLOTS), F32),
            dma((10,)),
            dma((3,)),
            dma((2,)),
            pltpu.SemaphoreType.REGULAR((2,)),
        ],
        compiler_params=pltpu.CompilerParams(
            collective_id=0, has_side_effects=True, vmem_limit_bytes=60 * 1024 * 1024
        ),
    )(
        weights,
        counts,
        frag_rows.reshape(1, SLOTS),
        frag_cols.reshape(1, SLOTS),
        step.reshape(1, SLOTS),
        spectra,
        jnp.asarray(tabs),
        jnp.asarray(consts),
        mask,
        target,
        jnp.asarray(later_tabs),
    )
    return outs[0], outs[1]


def solution(mesh):
    return jax.shard_map(
        shards,
        mesh=mesh,
        in_specs=(
            P("tile", None),
            P("tile", None),
            P("kern", None, None),
            P("kern"),
            P("tile"),
            P("tile"),
            P("tile"),
            P("tile"),
        ),
        out_specs=(P("tile"), P("tile")),
        check_vma=False,
    )
```
